32 devices in a mesh: rows: 16 (over z, y, core), chan: 2 (over x).
Axes of the slice: x: 2, y: 2, z: 4, core: 2. Of those that a mesh axis runs over, the one named last changes fastest.
Arguments:
- frame_one: bfloat16 [4096, 256], P('rows', 'chan'), may hold values from -6 to 6
- frame_two: bfloat16 [128, 480, 256], P('rows', None, 'chan'), may hold values from -6 to 6
Outputs:
- pyramid: bfloat16 [16, 5040, 4096], P(None, 'chan', 'rows')
The draws below stay inside these ranges and needn't reach their ends.
All inputs are finite; a program needn't handle non-finite values.
Results may differ from the reference program's by a relative error of at most 0.0016.
Values may be sent and summed in bfloat16 or wider, within the bound.
No kernel may reach another device: no remote copies, remote signals or barrier semaphores. Data moves between devices by JAX's collectives and lax.ppermute only.
A program may use at most 128 MiB of HBM per device.

```python
import jax
import jax.numpy as jnp
from jax import lax

C = 256
W = 480
SR = 8
Q = 4096
NS = 16
H2 = 128


def block_levels(stream_key, shape, split, least, top_value):
    level, own = 1.0, jax.random.fold_in(stream_key, 6)
    for axis_at, blocks in split:
        steps = jnp.exp(jax.random.uniform(jax.random.fold_in(own, axis_at), (blocks,), jnp.float32, least / len(split), top_value / len(split)))
        level = level * jnp.repeat(steps, shape[axis_at] // blocks).reshape([-1 if axis == axis_at else 1 for axis in range(len(shape))])
    return level


def noise(rng, dims, deviation, limit, shards=(), dtype=jnp.bfloat16):
    entries = jax.random.normal(rng, dims, jnp.float32) * deviation
    if len(shards) > 0:
        entries = block_levels(rng, dims, shards, -0.22, 0.18) * entries
    return jnp.clip(entries, min=-limit, max=limit).astype(dtype)


def setup_inputs(seed: int = 0) -> dict:
    key_of = jax.random.split(jax.random.key(seed), 3)
    frame_one = noise(key_of[0], (Q, C), 1.0, 6.0, ((0, 16), (1, 2)))
    frame_two = noise(key_of[1], (H2, W, C), 1.0, 6.0, ((0, 16), (2, 2)))
    return dict(frame_one=frame_one, frame_two=frame_two)


def pool_strip(strip):
    full = strip.astype(jnp.float32)
    rows_n, cols_n, chans = full.shape
    level_one = full.reshape(rows_n // 2, 2, cols_n // 2, 2, chans).mean(axis=(1, 3))
    level_two = level_one.reshape(rows_n // 4, 2, cols_n // 4, 2, chans).mean(axis=(1, 3))
    joined = jnp.concatenate([full.reshape(-1, chans), level_one.reshape(-1, chans), level_two.reshape(-1, chans)], axis=0)
    return joined.astype(jnp.bfloat16)

def reference(frame_one, frame_two):
    strips = frame_two.reshape(NS, SR, W, C)
    factor = 1.0 / jnp.sqrt(jnp.float32(C))

    def one_strip(strip):
        pooled = pool_strip(strip)
        values = lax.dot_general(pooled, frame_one, (((1,), (1,)), ((), ())), preferred_element_type=jnp.float32)
        return (values * factor).astype(jnp.bfloat16)
    return lax.map(one_strip, strips)
```

```python
import jax
import jax.numpy as jnp
from jax import lax
from jax.sharding import PartitionSpec as P


def pool_strip(strip):
    full = strip.astype(jnp.float32)
    rows_n, cols_n, chans = full.shape
    level_one = full.reshape(rows_n // 2, 2, cols_n // 2, 2, chans).mean(axis=(1, 3))
    level_two = level_one.reshape(rows_n // 4, 2, cols_n // 4, 2, chans).mean(axis=(1, 3))
    joined = jnp.concatenate(
        [full.reshape(-1, chans), level_one.reshape(-1, chans), level_two.reshape(-1, chans)],
        axis=0,
    )
    return joined.astype(jnp.bfloat16)


def local(frame_one, frame_two):
    groups = lax.axis_size("chan")
    queries = lax.all_gather(frame_one, "chan", axis=0, tiled=False)
    channels = queries.shape[0] * queries.shape[2]
    factor = 1.0 / jnp.sqrt(jnp.float32(channels))
    pooled = pool_strip(frame_two)
    share = pooled.shape[0] // groups
    traded = lax.all_to_all(pooled.reshape(groups, share, pooled.shape[1]), "chan", split_axis=0, concat_axis=0, tiled=True)
    gathered = lax.all_gather(traded, "rows", axis=0, tiled=False)
    values = jnp.einsum("skpc,kqc->spq", gathered, queries, preferred_element_type=jnp.float32)
    return (values * factor).astype(jnp.bfloat16)


def solution(mesh):
    in_specs = (P("rows", "chan"), P("rows", None, "chan"))
    out_specs = P(None, "chan", "rows")
    return jax.shard_map(local, mesh=mesh, in_specs=in_specs, out_specs=out_specs, check_vma=False)
```

```python
import functools

import jax
import jax.numpy as jnp
from jax import lax
from jax.experimental import pallas as pl
from jax.experimental.pallas import tpu as pltpu
from jax.sharding import PartitionSpec as P

LANES = 128
VMEM_BYTES = 48 * 1024 * 1024


def pool_strip(strip):
    full = strip.astype(jnp.float32)
    rows_n, cols_n, chans = full.shape
    level_one = full.reshape(rows_n // 2, 2, cols_n // 2, 2, chans).mean(axis=(1, 3))
    level_two = level_one.reshape(rows_n // 4, 2, cols_n // 4, 2, chans).mean(axis=(1, 3))
    joined = jnp.concatenate(
        [full.reshape(-1, chans), level_one.reshape(-1, chans), level_two.reshape(-1, chans)],
        axis=0,
    )
    return joined.astype(jnp.bfloat16)


def gather_local(frame_one, frame_two):
    groups = lax.axis_size("chan")
    queries = lax.all_gather(frame_one, "chan", axis=0, tiled=False)
    channels = queries.shape[0] * queries.shape[2]
    factor = 1.0 / jnp.sqrt(jnp.float32(channels))
    pooled = pool_strip(frame_two)
    share = pooled.shape[0] // groups
    traded = lax.all_to_all(
        pooled.reshape(groups, share, pooled.shape[1]), "chan", split_axis=0, concat_axis=0, tiled=True
    )
    gathered = lax.all_gather(traded, "rows", axis=0, tiled=False)
    values = jnp.einsum("skpc,kqc->spq", gathered, queries, preferred_element_type=jnp.float32)
    return (values * factor).astype(jnp.bfloat16)


def pooled_levels(half, sums, sums_two):
    rows_n, cols_n, chans = half.shape
    means = []
    for row in range(rows_n // 2):
        sums[row] = half[2 * row].astype(jnp.float32) + half[2 * row + 1].astype(jnp.float32)
        left = sums[row, pl.ds(0, cols_n // 2, stride=2), :]
        right = sums[row, pl.ds(1, cols_n // 2, stride=2), :]
        means.append((left + right) * 0.25)
    means_two = []
    for row in range(rows_n // 4):
        sums_two[row] = means[2 * row] + means[2 * row + 1]
        left = sums_two[row, pl.ds(0, cols_n // 4, stride=2), :]
        right = sums_two[row, pl.ds(1, cols_n // 4, stride=2), :]
        means_two.append((left + right) * 0.25)
    return jnp.concatenate(means + means_two, axis=0)


def extra_kernel(meta, own, other, extra, sums, sums_two):
    count = extra.shape[1]
    cols_n = own.shape[1]

    @pl.when(meta[0] == 0)
    def _():
        for index, half in enumerate((own, other)):
            extra[index] = pooled_levels(half, sums, sums_two).astype(extra.dtype)

    @pl.when(meta[0] != 0)
    def _():
        for index, half in enumerate((own, other)):
            pieces, left = [], count
            row = 0
            while left > 0:
                pieces.append(half[row].astype(jnp.float32)[: min(left, cols_n)])
                left -= cols_n
                row += 1
            extra[index] = jnp.concatenate(pieces, axis=0).astype(extra.dtype)


def corr_kernel(factor, aliased, meta, own, other, came, queries, *rest):
    out, sums, sums_two, values = rest[1:] if aliased else rest
    rows_n, cols_n, chans = own.shape
    raw, count = rows_n * cols_n, came.shape[1]
    ones = (rows_n // 2) * (cols_n // 2)

    def times(left):
        return jnp.dot(left, queries[...], preferred_element_type=jnp.float32) * factor

    for row in range(rows_n):
        values[row * cols_n : (row + 1) * cols_n] = times(jnp.concatenate([own[row], other[row]], axis=1))
    values[raw : raw + count] = times(jnp.concatenate([came[1], came[0]], axis=1))

    def put(segments):
        step, at = 240, 0
        todo = list(segments)
        while todo:
            pieces, room = [], step
            while todo and room > 0:
                first, last = todo.pop(0)
                take = min(room, last - first)
                pieces.append(values[first : first + take])
                room -= take
                if first + take < last:
                    todo.insert(0, (first + take, last))
            size = step - room
            piece = pieces[0] if len(pieces) == 1 else jnp.concatenate(pieces, axis=0)
            out[0, at : at + size] = piece.astype(out.dtype)
            at += size

    @pl.when(meta[0] == 0)
    def _():
        put([(0, raw + count)])

    @pl.when(meta[0] != 0)
    def _():
        levels = [pooled_levels(half, sums, sums_two).astype(own.dtype) for half in (own, other)]
        values[raw + count : raw + 2 * count] = times(jnp.concatenate(levels, axis=1))
        lower = raw + count
        put(
            [
                (count, raw),
                (raw, raw + ones),
                (lower, lower + ones),
                (raw + ones, raw + count),
                (lower + ones, lower + count),
            ]
        )


def ring_local(frame_one, frame_two):
    rows_axis = lax.axis_size("rows")
    rows_n, cols_n, chans = frame_two.shape
    queries_n = frame_one.shape[0]
    half_rows = rows_n // 2
    raw = half_rows * cols_n
    count = (half_rows // 2) * (cols_n // 2) + (half_rows // 4) * (cols_n // 4)
    factor = float(1.0 / (2 * chans) ** 0.5)
    me, side = lax.axis_index("rows"), lax.axis_index("chan")

    chips = rows_axis // 2
    columns = chips // 2
    order = [2 * z for z in range(columns)] + [2 * z + 1 for z in reversed(range(columns))]
    right = [(2 * order[p] + c, 2 * order[(p + 1) % chips] + c) for p in range(chips) for c in (0, 1)]
    left = [(b, a) for a, b in right]
    swap = [(r, r ^ 1) for r in range(rows_axis)]
    across = [(0, 1), (1, 0)]

    core, column, line = me % 2, me // 4, (me // 2) % 2
    place = jnp.where(line == 0, column, chips - 1 - column)

    def strip_at(distance, other_core):
        p = (place - distance) % chips
        chip = jnp.where(p < columns, 2 * p, 2 * (chips - 1 - p) + 1)
        return 2 * chip + (1 - core if other_core else core)

    scratch = [
        pltpu.VMEM((half_rows // 2, cols_n, chans), jnp.float32),
        pltpu.VMEM((half_rows // 4, cols_n // 2, chans), jnp.float32),
    ]

    def make_extra(own, other):
        return pl.pallas_call(
            extra_kernel,
            out_shape=jax.ShapeDtypeStruct((2, count, chans), frame_two.dtype),
            grid_spec=pltpu.PrefetchScalarGridSpec(
                num_scalar_prefetch=1,
                grid=(1,),
                in_specs=[pl.BlockSpec((half_rows, cols_n, chans), lambda i, m: (0, 0, 0))] * 2,
                out_specs=pl.BlockSpec((2, count, chans), lambda i, m: (0, 0, 0)),
                scratch_shapes=scratch,
            ),
            compiler_params=pltpu.CompilerParams(vmem_limit_bytes=VMEM_BYTES),
            cost_estimate=pl.CostEstimate(flops=8 * raw * chans, bytes_accessed=6 * raw * chans, transcendentals=0),
            name="extra",
        )(side[None], own, other)

    def correlate(out, strip, own, other, came):
        aliased = out is not None
        whole = [pl.BlockSpec((half_rows, cols_n, chans), lambda i, m: (0, 0, 0))] * 2
        whole += [pl.BlockSpec((2, count, chans), lambda i, m: (0, 0, 0))]
        whole += [pl.BlockSpec((2 * chans, queries_n), lambda i, m: (0, 0))]
        operands = [jnp.stack([side, strip]).astype(jnp.int32), own, other, came, queries]
        if aliased:
            whole += [pl.BlockSpec(memory_space=pl.ANY)]
            operands += [out]
        return pl.pallas_call(
            functools.partial(corr_kernel, factor, aliased),
            out_shape=jax.ShapeDtypeStruct((rows_axis, raw + count, queries_n), frame_two.dtype),
            grid_spec=pltpu.PrefetchScalarGridSpec(
                num_scalar_prefetch=1,
                grid=(1,),
                in_specs=whole,
                out_specs=pl.BlockSpec((1, raw + count, queries_n), lambda i, m: (m[1], 0, 0)),
                scratch_shapes=scratch + [pltpu.VMEM((raw + 2 * count, queries_n), jnp.float32)],
            ),
            input_output_aliases={5: 0} if aliased else {},
            compiler_params=pltpu.CompilerParams(vmem_limit_bytes=VMEM_BYTES),
            cost_estimate=pl.CostEstimate(
                flops=4 * (raw + count) * chans * queries_n,
                bytes_accessed=2 * (raw + count) * (2 * chans + queries_n),
                transcendentals=0,
            ),
            name="correlate",
        )(*operands)

    own = lax.dynamic_slice_in_dim(frame_two, side * half_rows, half_rows, axis=0)
    theirs = lax.dynamic_slice_in_dim(frame_two, (1 - side) * half_rows, half_rows, axis=0)
    other = lax.ppermute(theirs, "chan", across)
    queries_other = lax.ppermute(frame_one, "chan", across)
    queries = jnp.concatenate([frame_one.T, queries_other.T], axis=0)

    half_way = chips // 2
    came_right, came_left = {0: [own, other]}, {0: [own, other]}
    for d in range(1, half_way + 1):
        far = d == half_way
        came_right[d] = [
            lax.ppermute(came_right[d - 1][0], "rows", right),
            None if far else lax.ppermute(came_right[d - 1][1], "rows", right),
        ]
        came_left[d] = [
            None if far else lax.ppermute(came_left[d - 1][0], "rows", left),
            lax.ppermute(came_left[d - 1][1], "rows", left),
        ]
    strips = [(0, came_right[0])]
    for d in range(1, half_way):
        strips += [(d, came_right[d]), (chips - d, came_left[d])]
    strips += [(half_way, [came_right[half_way][0], came_left[half_way][1]])]

    out = None
    for distance, (mine, partner) in strips:
        came = lax.ppermute(make_extra(mine, partner), "chan", across)
        swapped = [lax.ppermute(piece, "rows", swap) for piece in (mine, partner, came)]
        out = correlate(out, strip_at(distance, False), mine, partner, came)
        out = correlate(out, strip_at(distance, True), *swapped)
    return out


def solution(mesh):
    rows_axis, groups = mesh.shape["rows"], mesh.shape["chan"]

    def local(frame_one, frame_two):
        rows_n, cols_n, chans = frame_two.shape
        ring = groups == 2 and rows_axis % 8 == 0 and rows_n % 8 == 0 and cols_n % 32 == 0 and chans % LANES == 0
        return (ring_local if ring else gather_local)(frame_one, frame_two)

    in_specs = (P("rows", "chan"), P("rows", None, "chan"))
    out_specs = P(None, "chan", "rows")
    return jax.shard_map(local, mesh=mesh, in_specs=in_specs, out_specs=out_specs, check_vma=False)
```

```python
import functools

import jax
import jax.numpy as jnp
from jax import lax
from jax.experimental import pallas as pl
from jax.experimental.pallas import tpu as pltpu
from jax.sharding import PartitionSpec as P

LANES = 128
VMEM_BYTES = 28 * 1024 * 1024


def pool_strip(strip):
    full = strip.astype(jnp.float32)
    rows_n, cols_n, chans = full.shape
    level_one = full.reshape(rows_n // 2, 2, cols_n // 2, 2, chans).mean(axis=(1, 3))
    level_two = level_one.reshape(rows_n // 4, 2, cols_n // 4, 2, chans).mean(axis=(1, 3))
    joined = jnp.concatenate(
        [full.reshape(-1, chans), level_one.reshape(-1, chans), level_two.reshape(-1, chans)],
        axis=0,
    )
    return joined.astype(jnp.bfloat16)


def gather_local(frame_one, frame_two):
    groups = lax.axis_size("chan")
    queries = lax.all_gather(frame_one, "chan", axis=0, tiled=False)
    channels = queries.shape[0] * queries.shape[2]
    factor = 1.0 / jnp.sqrt(jnp.float32(channels))
    pooled = pool_strip(frame_two)
    share = pooled.shape[0] // groups
    traded = lax.all_to_all(
        pooled.reshape(groups, share, pooled.shape[1]), "chan", split_axis=0, concat_axis=0, tiled=True
    )
    gathered = lax.all_gather(traded, "rows", axis=0, tiled=False)
    values = jnp.einsum("skpc,kqc->spq", gathered, queries, preferred_element_type=jnp.float32)
    return (values * factor).astype(jnp.bfloat16)


def pooled_levels(half, sums, sums_two):
    rows_n, cols_n, _ = half.shape
    means = []
    for row in range(rows_n // 2):
        sums[row] = half[2 * row].astype(jnp.float32) + half[2 * row + 1].astype(jnp.float32)
        left = sums[row, pl.ds(0, cols_n // 2, stride=2), :]
        right = sums[row, pl.ds(1, cols_n // 2, stride=2), :]
        means.append((left + right) * 0.25)
    means_two = []
    for row in range(rows_n // 4):
        sums_two[row] = means[2 * row] + means[2 * row + 1]
        left = sums_two[row, pl.ds(0, cols_n // 4, stride=2), :]
        right = sums_two[row, pl.ds(1, cols_n // 4, stride=2), :]
        means_two.append((left + right) * 0.25)
    return jnp.concatenate(means + means_two, axis=0)


def extra_kernel(meta, half, *refs):
    extra, _, sums, sums_two = refs[-4:]
    strips, _, cols_n, _ = half.shape
    count = extra.shape[1]

    @pl.when(meta[0] == 0)
    def _():
        for index in range(strips):
            extra[index] = pooled_levels(half.at[index], sums, sums_two).astype(extra.dtype)

    @pl.when(meta[0] != 0)
    def _():
        for index in range(strips):
            parts, left, row = [], count, 0
            while left > 0:
                parts.append(half[index, row].astype(jnp.float32)[: min(left, cols_n)])
                left, row = left - cols_n, row + 1
            extra[index] = jnp.concatenate(parts, axis=0).astype(extra.dtype)


def corr_kernel(factor, wide, slots, landing, meta, own, other, came_own, came_other, queries, *refs):
    refs = list(refs)
    landed = refs.pop(0) if landing else None
    out = refs[1]
    refs = refs[2:]
    pair = refs.pop(0) if wide else None
    done, values, sums, sums_two, sems, land_sems = refs
    strips, rows_n, cols_n, _ = own.shape
    count, width = came_own.shape[1], done.shape[2]
    raw = rows_n * cols_n
    ones = (rows_n // 2) * (cols_n // 2)

    copies = []
    for index, slot in enumerate(landing):
        copies.append(pltpu.make_async_copy(landed.at[index], out.at[meta[slot]], land_sems.at[index]))
        copies[-1].start()

    def times(left):
        return jnp.dot(left, queries[...], preferred_element_type=jnp.float32) * factor

    def store(index, at, part):
        done[index, at : at + part.shape[0]] = part[:, :width].astype(done.dtype)
        if wide:
            pair[index, at : at + part.shape[0]] = part[:, width:].astype(done.dtype)

    def put(index, segments):
        step, at = cols_n // 2, 0
        todo = list(segments)
        while todo:
            parts, room = [], step
            while todo and room > 0:
                first, last = todo.pop(0)
                take = min(room, last - first)
                parts.append(values[first : first + take])
                room -= take
                if first + take < last:
                    todo.insert(0, (first + take, last))
            part = parts[0] if len(parts) == 1 else jnp.concatenate(parts, axis=0)
            store(index, at, part)
            at += step - room

    for index in range(strips):

        def raw_row(row):
            return jnp.concatenate([own[index, row], other[index, row]], axis=1)

        def came_rows():
            return jnp.concatenate([came_own[index], came_other[index]], axis=1)

        @pl.when(meta[0] == 0)
        def _():
            for row in range(rows_n):
                store(index, row * cols_n, times(raw_row(row)))
            store(index, raw, times(came_rows()))

        @pl.when(meta[0] != 0)
        def _():
            for row in range(count // cols_n, rows_n):
                values[row * cols_n : (row + 1) * cols_n] = times(raw_row(row))
            values[raw : raw + count] = times(came_rows())
            levels = [
                pooled_levels(half.at[index], sums, sums_two).astype(done.dtype) for half in (own, other)
            ]
            lower = raw + count
            values[lower : lower + count] = times(jnp.concatenate(levels, axis=1))
            put(
                index,
                [
                    (count, raw),
                    (raw, raw + ones),
                    (lower, lower + ones),
                    (raw + ones, raw + count),
                    (lower + ones, lower + count),
                ],
            )

        copies.append(pltpu.make_async_copy(done.at[index], out.at[meta[slots[index]]], sems.at[index]))
        copies[-1].start()
    for copy in copies:
        copy.wait()


def ring_local(frame_one, frame_two):
    rows_axis = lax.axis_size("rows")
    rows_n, cols_n, chans = frame_two.shape
    queries_n = frame_one.shape[0]
    half_rows = rows_n // 2
    raw = half_rows * cols_n
    count = (half_rows // 2) * (cols_n // 2) + (half_rows // 4) * (cols_n // 4)
    factor = float(1.0 / (2 * chans) ** 0.5)
    me, side = lax.axis_index("rows"), lax.axis_index("chan")

    chips = rows_axis // 2
    columns, half_way = chips // 2, chips // 2
    order = [2 * z for z in range(columns)] + [2 * z + 1 for z in reversed(range(columns))]
    ring = [(2 * order[p], 2 * order[(p + 1) % chips]) for p in range(chips)]
    ring += [(2 * order[p] + 1, 2 * order[p - 1] + 1) for p in range(chips)]
    swap = [(r, r ^ 1) for r in range(rows_axis)]
    across = [(0, 1), (1, 0)]

    core, column, line = me % 2, me // 4, (me // 2) % 2
    place = jnp.where(line == 0, column, chips - 1 - column)
    steps = jnp.arange(half_way + 1, dtype=jnp.int32)

    def strips_of(c):
        p = (place + jnp.where(c == 0, -steps, steps)) % chips
        chip = jnp.where(p < columns, 2 * p, 2 * (chips - 1 - p) + 1)
        return [2 * chip + c, 2 * chip + 1 - c]

    meta = jnp.concatenate([side[None], *strips_of(core), *strips_of(1 - core)]).astype(jnp.int32)

    def slots_of(d, other_core):
        first = 1 + (2 * other_core) * (half_way + 1) + d
        return (first,) if d in (0, half_way) else (first, first + half_way + 1)

    in_vmem = pl.BlockSpec(memory_space=pltpu.VMEM)
    anywhere = pl.BlockSpec(memory_space=pl.ANY)
    scalars = pl.BlockSpec(memory_space=pltpu.SMEM)
    out_type = jax.ShapeDtypeStruct((rows_axis, raw + count, queries_n), frame_two.dtype)
    pooling = [
        pltpu.VMEM((half_rows // 2, cols_n, chans), jnp.float32),
        pltpu.VMEM((half_rows // 4, cols_n // 2, chans), jnp.float32),
    ]
    params = pltpu.CompilerParams(vmem_limit_bytes=VMEM_BYTES)
    cheap = pl.CostEstimate(flops=1000, bytes_accessed=1000, transcendentals=0)

    def make_extra(out, half):
        aliased = out is not None
        return pl.pallas_call(
            extra_kernel,
            out_shape=(jax.ShapeDtypeStruct((half.shape[0], count, chans), frame_two.dtype), out_type),
            in_specs=[scalars, in_vmem] + [anywhere] * aliased,
            out_specs=(in_vmem, anywhere),
            scratch_shapes=pooling,
            input_output_aliases={2: 1} if aliased else {},
            compiler_params=params,
            cost_estimate=cheap,
            name="extra",
        )(meta, half, *([out] if aliased else []))

    def correlate(out, slots, own, other, came_own, came_other, wide, landing=(), landed=None):
        strips = own.shape[0]
        operands = [own, other, came_own, came_other, queries_wide if wide else queries]
        pair_type = jax.ShapeDtypeStruct((strips, raw + count, queries_n), frame_two.dtype)
        return pl.pallas_call(
            functools.partial(corr_kernel, factor, wide, slots, landing),
            out_shape=(out_type, pair_type) if wide else out_type,
            in_specs=[scalars] + [in_vmem] * 5 + [anywhere] * (1 + bool(landing)),
            out_specs=(anywhere, in_vmem) if wide else anywhere,
            scratch_shapes=[
                pltpu.VMEM((strips, raw + count, queries_n), frame_two.dtype),
                pltpu.VMEM((raw + 2 * count, queries_n * (1 + wide)), jnp.float32),
                *pooling,
                pltpu.SemaphoreType.DMA((strips,)),
                pltpu.SemaphoreType.DMA((max(1, len(landing)),)),
            ],
            input_output_aliases={6 + bool(landing): 0},
            compiler_params=params,
            cost_estimate=cheap,
            name="correlate",
        )(meta, *operands, *([landed] if landing else []), out)

    mine = lax.dynamic_slice_in_dim(frame_two, side * half_rows, half_rows, axis=0)[None]
    theirs = lax.dynamic_slice_in_dim(frame_two, (1 - side) * half_rows, half_rows, axis=0)[None]
    partner = lax.ppermute(theirs, "chan", across)
    queries_other = lax.ppermute(frame_one, "chan", across)
    queries = jnp.concatenate([frame_one.T, queries_other.T], axis=0)
    queries_wide = jnp.concatenate([queries, lax.ppermute(queries, "rows", swap)], axis=1)

    came = {0: (mine, partner)}
    moving = [jnp.concatenate([half, lax.ppermute(half, "rows", swap)], axis=0) for half in came[0]]
    for d in range(1, half_way + 1):
        if d == half_way:
            moving = [half[:1] for half in moving]
        moving = [lax.ppermute(half, "rows", ring) for half in moving]
        came[d] = tuple(moving)
    far_swapped = [lax.ppermute(half, "rows", swap) for half in came[half_way]]

    across_came = {}

    def do_extra(out, d, part):
        extra, out = make_extra(out, came[d][part])
        across_came[d, 1 - part] = lax.ppermute(extra, "chan", across)
        return out

    def do_correlate(out, d, landing=(), landed=None):
        out, pair = correlate(
            out, slots_of(d, 0), *came[d], across_came[d, 0], across_came[d, 1], True, landing, landed
        )
        return out, lax.ppermute(pair, "rows", swap)

    out = do_extra(None, 0, 0)
    out = do_extra(out, 0, 1)
    out = do_extra(out, 1, 0)
    out, pair = do_correlate(out, 0)
    out = do_extra(out, 1, 1)
    for d in range(2, half_way):
        out = do_extra(out, d, 0)
        out, pair = do_correlate(out, d - 1, slots_of(d - 2, 1), pair)
        out = do_extra(out, d, 1)
    out = do_extra(out, half_way, 0)
    out = do_extra(out, half_way, 1)
    out, pair = do_correlate(out, half_way - 1, slots_of(half_way - 2, 1), pair)
    far = [across_came[half_way, 0], across_came[half_way, 1]]
    out = correlate(out, slots_of(half_way, 0), *came[half_way], *far, False)
    far = [lax.ppermute(part, "rows", swap) for part in far]
    return correlate(out, slots_of(half_way, 1), *far_swapped, *far, False, slots_of(half_way - 1, 1), pair)


def solution(mesh):
    rows_axis, groups = mesh.shape["rows"], mesh.shape["chan"]

    def local(frame_one, frame_two):
        rows_n, cols_n, chans = frame_two.shape
        ring = groups == 2 and rows_axis % 8 == 0 and rows_axis >= 16 and rows_n % 8 == 0 and cols_n % 32 == 0 and chans % LANES == 0
        return (ring_local if ring else gather_local)(frame_one, frame_two)

    in_specs = (P("rows", "chan"), P("rows", None, "chan"))
    out_specs = P(None, "chan", "rows")
    return jax.shard_map(local, mesh=mesh, in_specs=in_specs, out_specs=out_specs, check_vma=False)
```

```python
import functools

import jax
import jax.numpy as jnp
from jax import lax
from jax.experimental import pallas as pl
from jax.experimental.pallas import tpu as pltpu
from jax.sharding import PartitionSpec as P

LANES = 128
PARAMS = {'LAG': 2, 'F0': 26, 'PINA': 1, 'PINB': 1, 'EARLY': 1, 'EARLY0': 0, 'PS0': 1, 'PS1': 1, 'PC': 0, 'X00': 10, 'X01': 10, 'C0': 10, 'X10': 10, 'X11': 10, 'C1': 10, 'X20': 10, 'X21': 10, 'C2': 10, 'X30': 10, 'X31': 10, 'C3': 10, 'X40': 10, 'X41': 10, 'C4': 10}


def G(name):
    return PARAMS.get(name, 0)


VMEM_BYTES = 28 * 1024 * 1024


def pool_strip(strip):
    full = strip.astype(jnp.float32)
    rows_n, cols_n, chans = full.shape
    level_one = full.reshape(rows_n // 2, 2, cols_n // 2, 2, chans).mean(axis=(1, 3))
    level_two = level_one.reshape(rows_n // 4, 2, cols_n // 4, 2, chans).mean(axis=(1, 3))
    joined = jnp.concatenate(
        [full.reshape(-1, chans), level_one.reshape(-1, chans), level_two.reshape(-1, chans)],
        axis=0,
    )
    return joined.astype(jnp.bfloat16)


def gather_local(frame_one, frame_two):
    groups = lax.axis_size("chan")
    queries = lax.all_gather(frame_one, "chan", axis=0, tiled=False)
    channels = queries.shape[0] * queries.shape[2]
    factor = 1.0 / jnp.sqrt(jnp.float32(channels))
    pooled = pool_strip(frame_two)
    share = pooled.shape[0] // groups
    traded = lax.all_to_all(
        pooled.reshape(groups, share, pooled.shape[1]), "chan", split_axis=0, concat_axis=0, tiled=True
    )
    gathered = lax.all_gather(traded, "rows", axis=0, tiled=False)
    values = jnp.einsum("skpc,kqc->spq", gathered, queries, preferred_element_type=jnp.float32)
    return (values * factor).astype(jnp.bfloat16)


def pooled_levels(half, sums, sums_two):
    rows_n, cols_n, _ = half.shape
    means = []
    for row in range(rows_n // 2):
        sums[row] = half[2 * row].astype(jnp.float32) + half[2 * row + 1].astype(jnp.float32)
        left = sums[row, pl.ds(0, cols_n // 2, stride=2), :]
        right = sums[row, pl.ds(1, cols_n // 2, stride=2), :]
        means.append((left + right) * 0.25)
    means_two = []
    for row in range(rows_n // 4):
        sums_two[row] = means[2 * row] + means[2 * row + 1]
        left = sums_two[row, pl.ds(0, cols_n // 4, stride=2), :]
        right = sums_two[row, pl.ds(1, cols_n // 4, stride=2), :]
        means_two.append((left + right) * 0.25)
    return jnp.concatenate(means + means_two, axis=0)


def extra_kernel(handed, meta, half, *refs):
    extra, sums, sums_two = refs[-3 - handed], *refs[-2:]
    strips, _, cols_n, _ = half.shape
    count = extra.shape[1]

    @pl.when(meta[0] == 0)
    def _():
        for index in range(strips):
            extra[index] = pooled_levels(half.at[index], sums, sums_two).astype(extra.dtype)

    @pl.when(meta[0] != 0)
    def _():
        for index in range(strips):
            parts, left, row = [], count, 0
            while left > 0:
                parts.append(half[index, row].astype(jnp.float32)[: min(left, cols_n)])
                left, row = left - cols_n, row + 1
            extra[index] = jnp.concatenate(parts, axis=0).astype(extra.dtype)


def corr_kernel(factor, wide, slots, landing, pins, meta, own, other, came_own, came_other, queries, *refs):
    refs = list(refs)
    landed = refs.pop(0) if landing else None
    out = refs[1 + pins]
    refs = refs[2 + pins :]
    pair = refs.pop(0) if wide else None
    done, values, sums, sums_two, sems, land_sems = refs
    strips, rows_n, cols_n, _ = own.shape
    count, width = came_own.shape[1], done.shape[2]
    raw = rows_n * cols_n
    ones = (rows_n // 2) * (cols_n // 2)

    copies = []
    for index, slot in enumerate(landing):
        copies.append(pltpu.make_async_copy(landed.at[index], out.at[meta[slot]], land_sems.at[index]))
        copies[-1].start()

    def times(left):
        return jnp.dot(left, queries[...], preferred_element_type=jnp.float32) * factor

    def store(index, at, part):
        done[index, at : at + part.shape[0]] = part[:, :width].astype(done.dtype)
        if wide:
            pair[index, at : at + part.shape[0]] = part[:, width:].astype(done.dtype)

    def put(index, segments):
        step, at = cols_n // 2, 0
        todo = list(segments)
        while todo:
            parts, room = [], step
            while todo and room > 0:
                first, last = todo.pop(0)
                take = min(room, last - first)
                parts.append(values[first : first + take])
                room -= take
                if first + take < last:
                    todo.insert(0, (first + take, last))
            part = parts[0] if len(parts) == 1 else jnp.concatenate(parts, axis=0)
            store(index, at, part)
            at += step - room

    for index in range(strips):

        def raw_row(row):
            return jnp.concatenate([own[index, row], other[index, row]], axis=1)

        def came_rows():
            return jnp.concatenate([came_own[index], came_other[index]], axis=1)

        @pl.when(meta[0] == 0)
        def _():
            for row in range(rows_n):
                store(index, row * cols_n, times(raw_row(row)))
            store(index, raw, times(came_rows()))

        @pl.when(meta[0] != 0)
        def _():
            for row in range(count // cols_n, rows_n):
                values[row * cols_n : (row + 1) * cols_n] = times(raw_row(row))
            values[raw : raw + count] = times(came_rows())
            levels = [
                pooled_levels(half.at[index], sums, sums_two).astype(done.dtype) for half in (own, other)
            ]
            lower = raw + count
            values[lower : lower + count] = times(jnp.concatenate(levels, axis=1))
            put(
                index,
                [
                    (count, raw),
                    (raw, raw + ones),
                    (lower, lower + ones),
                    (raw + ones, raw + count),
                    (lower + ones, lower + count),
                ],
            )

        copies.append(pltpu.make_async_copy(done.at[index], out.at[meta[slots[index]]], sems.at[index]))
        copies[-1].start()
    for copy in copies:
        copy.wait()


def ring_local(frame_one, frame_two):
    rows_axis = lax.axis_size("rows")
    rows_n, cols_n, chans = frame_two.shape
    queries_n = frame_one.shape[0]
    half_rows = rows_n // 2
    raw = half_rows * cols_n
    count = (half_rows // 2) * (cols_n // 2) + (half_rows // 4) * (cols_n // 4)
    factor = float(1.0 / (2 * chans) ** 0.5)
    me, side = lax.axis_index("rows"), lax.axis_index("chan")

    chips = rows_axis // 2
    columns, half_way = chips // 2, chips // 2
    order = [2 * z for z in range(columns)] + [2 * z + 1 for z in reversed(range(columns))]
    ring = [(2 * order[p], 2 * order[(p + 1) % chips]) for p in range(chips)]
    ring += [(2 * order[p] + 1, 2 * order[p - 1] + 1) for p in range(chips)]
    swap = [(r, r ^ 1) for r in range(rows_axis)]
    across = [(0, 1), (1, 0)]

    core, column, line = me % 2, me // 4, (me // 2) % 2
    place = jnp.where(line == 0, column, chips - 1 - column)
    steps = jnp.arange(half_way + 1, dtype=jnp.int32)

    def strips_of(c):
        p = (place + jnp.where(c == 0, -steps, steps)) % chips
        chip = jnp.where(p < columns, 2 * p, 2 * (chips - 1 - p) + 1)
        return [2 * chip + c, 2 * chip + 1 - c]

    meta = jnp.concatenate([side[None], *strips_of(core), *strips_of(1 - core)]).astype(jnp.int32)

    def slots_of(d, other_core):
        first = 1 + (2 * other_core) * (half_way + 1) + d
        return (first,) if d in (0, half_way) else (first, first + half_way + 1)

    in_vmem = pl.BlockSpec(memory_space=pltpu.VMEM)
    anywhere = pl.BlockSpec(memory_space=pl.ANY)
    scalars = pl.BlockSpec(memory_space=pltpu.SMEM)
    out_type = jax.ShapeDtypeStruct((rows_axis, raw + count, queries_n), frame_two.dtype)
    pooling = [
        pltpu.VMEM((half_rows // 2, cols_n, chans), jnp.float32),
        pltpu.VMEM((half_rows // 4, cols_n // 2, chans), jnp.float32),
    ]
    params = pltpu.CompilerParams(vmem_limit_bytes=VMEM_BYTES)
    def modelled(us):
        return pl.CostEstimate(flops=int(us * 10**9) + 1000, bytes_accessed=1000, transcendentals=0)


    def make_extra(out, half, cost, pins, *pair):
        handed = (() if out is None else (out,)) + pair
        results = (jax.ShapeDtypeStruct((half.shape[0], count, chans), frame_two.dtype), out_type)
        results += tuple(jax.ShapeDtypeStruct(product.shape, product.dtype) for product in pair)
        return pl.pallas_call(
            functools.partial(extra_kernel, len(results) - 1),
            out_shape=results,
            in_specs=[scalars, in_vmem] + [anywhere] * len(handed + pins),
            out_specs=(in_vmem,) + (anywhere,) * (len(results) - 1),
            scratch_shapes=pooling,
            input_output_aliases={2 + index: 1 + index for index in range(len(handed))},
            compiler_params=params,
            cost_estimate=modelled(cost),
            name="extra",
        )(meta, half, *handed, *pins)

    def correlate(out, slots, own, other, came_own, came_other, wide, landing=(), landed=None, cost=0, pins=()):
        strips = own.shape[0]
        operands = [own, other, came_own, came_other, queries_wide if wide else queries]
        pair_type = jax.ShapeDtypeStruct((strips, raw + count, queries_n), frame_two.dtype)
        return pl.pallas_call(
            functools.partial(corr_kernel, factor, wide, slots, landing, len(pins)),
            out_shape=(out_type, pair_type) if wide else out_type,
            in_specs=[scalars] + [in_vmem] * 5 + [anywhere] * (1 + bool(landing) + len(pins)),
            out_specs=(anywhere, in_vmem) if wide else anywhere,
            scratch_shapes=[
                pltpu.VMEM((strips, raw + count, queries_n), frame_two.dtype),
                pltpu.VMEM((raw + 2 * count, queries_n * (1 + wide)), jnp.float32),
                *pooling,
                pltpu.SemaphoreType.DMA((strips,)),
                pltpu.SemaphoreType.DMA((max(1, len(landing)),)),
            ],
            input_output_aliases={6 + bool(landing): 0},
            compiler_params=params,
            cost_estimate=modelled(cost),
            name="correlate",
        )(meta, *operands, *([landed] if landing else []), out, *pins)

    mine = lax.dynamic_slice_in_dim(frame_two, side * half_rows, half_rows, axis=0)[None]
    theirs = lax.dynamic_slice_in_dim(frame_two, (1 - side) * half_rows, half_rows, axis=0)[None]
    if G("XQ"):
        sent = jnp.concatenate([theirs.reshape(raw, chans), frame_one], axis=0)
        got = lax.ppermute(sent, "chan", across)
        partner, queries_other = got[:raw].reshape(theirs.shape), got[raw:]
    else:
        partner = lax.ppermute(theirs, "chan", across)
        queries_other = lax.ppermute(frame_one, "chan", across)
    queries = jnp.concatenate([frame_one.T, queries_other.T], axis=0)
    queries_wide = jnp.concatenate([queries, lax.ppermute(queries, "rows", swap)], axis=1)

    def permute_rows(pairs, piece):
        return lax.ppermute(piece, "rows", pairs)

    came = {0: (mine, partner)}
    both = [[half, permute_rows(swap, half)] for half in came[0]]
    if G("A1SPLIT"):
        moving = [
            jnp.concatenate([permute_rows(ring, half) for half in both[0]], axis=0),
            permute_rows(ring, jnp.concatenate(both[1], axis=0)),
        ]
    else:
        moving = [permute_rows(ring, jnp.concatenate(both[i], axis=0)) for i in (0, 1)]
    came[1] = tuple(moving)
    for d in range(2, half_way + 1):
        if d == half_way:
            moving = [half[:1] for half in moving]
        moving = [permute_rows(ring, half) for half in moving]
        came[d] = tuple(moving)
    far_swapped = [permute_rows(swap, half) for half in came[half_way]]

    across_came = {}

    def do_extra(out, d, part, pin, *pair):
        pins = () if pin is None else (across_came[pin],) if isinstance(pin, tuple) else (pin,)
        extra, *handed = make_extra(out, came[d][part], G(f"X{d}{part}"), pins, *pair)
        across_came[d, 1 - part] = lax.ppermute(extra, "chan", across)
        return handed if pair else handed[0]

    def do_correlate(out, d, landing=(), landed=None, pins=()):
        return correlate(out, slots_of(d, 0), *came[d], across_came[d, 0], across_came[d, 1], True, landing, landed, cost=G(f"C{d}"), pins=pins)

    lag = G("LAG")
    waiting = []

    def landing(now):
        if waiting and waiting[0][0] <= now:
            return waiting.pop(0)[1:]
        return (), None

    def product(out, d, pins=()):
        out, pair = do_correlate(out, d, *landing(d), pins)
        waiting.append((d + lag, slots_of(d, 1), permute_rows(swap, pair)))
        return out

    out = do_extra(None, 0, 0, partner if G("PINX") else None)
    out = do_extra(out, 0, 1, None)
    out = do_extra(out, 1, 0, (0, 1) if G("PIN0") else None)
    if G("EARLY0"): out = product(out, 0)
    out = do_extra(out, 1, 1, (1, 1) if G("PINB") else None)
    if not G("EARLY0"): out = product(out, 0)
    for d in range(2, half_way):
        out = do_extra(out, d, 0, (d - 1, 0) if G("PINA") else None)
        if G("EARLY"): out = product(out, d - 1)
        out = do_extra(out, d, 1, (d, 1) if G("PINB") else None)
        if not G("EARLY"): out = product(out, d - 1)
    out = do_extra(out, half_way, 0, None)
    out = do_extra(out, half_way, 1, far_swapped[0] if G("PS0") == 1 else None)
    out = product(out, half_way - 1, (far_swapped[0],) if G("PS0") == 2 else ())
    far = [across_came[half_way, 0], across_came[half_way, 1]]
    swapped = [permute_rows(swap, part) for part in far]
    pins = ((far_swapped[1],) if G("PS1") else ()) + ((swapped[1],) if G("PC") else ())
    out = correlate(out, slots_of(half_way, 0), *came[half_way], *far, False, *landing(half_way), cost=G("F0"), pins=pins)
    return correlate(out, slots_of(half_way, 1), *far_swapped, *swapped, False, *landing(half_way + 1), cost=G("F1"))


def solution(mesh):
    rows_axis, groups = mesh.shape["rows"], mesh.shape["chan"]

    def local(frame_one, frame_two):
        rows_n, cols_n, chans = frame_two.shape
        ring = groups == 2 and rows_axis % 8 == 0 and rows_axis >= 16 and rows_n % 8 == 0 and cols_n % 32 == 0 and chans % LANES == 0
        return (ring_local if ring else gather_local)(frame_one, frame_two)

    in_specs = (P("rows", "chan"), P("rows", None, "chan"))
    out_specs = P(None, "chan", "rows")
    return jax.shard_map(local, mesh=mesh, in_specs=in_specs, out_specs=out_specs, check_vma=False)
```

```python
import functools

import jax
import jax.numpy as jnp
from jax import lax
from jax.experimental import pallas as pl
from jax.experimental.pallas import tpu as pltpu
from jax.sharding import PartitionSpec as P

LANES = 128
PARAMS = {'LAG': 2, 'F0': 20, 'F1': 0, 'PS0': 1, 'JA': 1, 'JB': 1, 'C0POS': 2, 'BSPL': 0, 'C3POS': 1, 'GATE': 30, 'X00': 10, 'X01': 10, 'C0': 10, 'X10': 10, 'X11': 10, 'C1': 10, 'X20': 10, 'X21': 10, 'C2': 10, 'X30': 10, 'X31': 10, 'C3': 10, 'X40': 10, 'X41': 10, 'C4': 10}


def G(name):
    return PARAMS.get(name, 0)


VMEM_BYTES = 28 * 1024 * 1024


def pool_strip(strip):
    full = strip.astype(jnp.float32)
    rows_n, cols_n, chans = full.shape
    level_one = full.reshape(rows_n // 2, 2, cols_n // 2, 2, chans).mean(axis=(1, 3))
    level_two = level_one.reshape(rows_n // 4, 2, cols_n // 4, 2, chans).mean(axis=(1, 3))
    joined = jnp.concatenate(
        [full.reshape(-1, chans), level_one.reshape(-1, chans), level_two.reshape(-1, chans)],
        axis=0,
    )
    return joined.astype(jnp.bfloat16)


def gather_local(frame_one, frame_two):
    groups = lax.axis_size("chan")
    queries = lax.all_gather(frame_one, "chan", axis=0, tiled=False)
    channels = queries.shape[0] * queries.shape[2]
    factor = 1.0 / jnp.sqrt(jnp.float32(channels))
    pooled = pool_strip(frame_two)
    share = pooled.shape[0] // groups
    traded = lax.all_to_all(
        pooled.reshape(groups, share, pooled.shape[1]), "chan", split_axis=0, concat_axis=0, tiled=True
    )
    gathered = lax.all_gather(traded, "rows", axis=0, tiled=False)
    values = jnp.einsum("skpc,kqc->spq", gathered, queries, preferred_element_type=jnp.float32)
    return (values * factor).astype(jnp.bfloat16)


def pooled_levels(half, sums, sums_two):
    rows_n, cols_n, _ = half.shape
    means = []
    for row in range(rows_n // 2):
        sums[row] = half[2 * row].astype(jnp.float32) + half[2 * row + 1].astype(jnp.float32)
        left = sums[row, pl.ds(0, cols_n // 2, stride=2), :]
        right = sums[row, pl.ds(1, cols_n // 2, stride=2), :]
        means.append((left + right) * 0.25)
    means_two = []
    for row in range(rows_n // 4):
        sums_two[row] = means[2 * row] + means[2 * row + 1]
        left = sums_two[row, pl.ds(0, cols_n // 4, stride=2), :]
        right = sums_two[row, pl.ds(1, cols_n // 4, stride=2), :]
        means_two.append((left + right) * 0.25)
    return jnp.concatenate(means + means_two, axis=0)


def strips_in(refs):
    return [ref.at[index] for ref in refs for index in range(ref.shape[0])]


def extra_kernel(pieces, results, flip, meta, *refs):
    halves = strips_in(refs[:pieces])
    extra, sums, sums_two = refs[-2 - results], *refs[-2:]
    count, cols_n = extra.shape[1], halves[0].shape[1]
    upper = meta[0] == (1 if flip else 0)

    @pl.when(upper)
    def _():
        for index, half in enumerate(halves):
            extra[index] = pooled_levels(half, sums, sums_two).astype(extra.dtype)

    @pl.when(jnp.logical_not(upper))
    def _():
        for index, half in enumerate(halves):
            parts, left, row = [], count, 0
            while left > 0:
                parts.append(half[row].astype(jnp.float32)[: min(left, cols_n)])
                left, row = left - cols_n, row + 1
            extra[index] = jnp.concatenate(parts, axis=0).astype(extra.dtype)


def chunks(segments, step):
    todo, runs = list(segments), []
    while todo:
        run, room = [], step
        while todo and room > 0:
            ref, first, last = todo.pop(0)
            take = min(room, last - first)
            run.append((ref, first, first + take))
            room -= take
            if first + take < last:
                todo.insert(0, (ref, first + take, last))
        runs.append(run)
    return runs


def joined(run):
    parts = [ref[first:last].astype(jnp.float32) for ref, first, last in run]
    return parts[0] if len(parts) == 1 else jnp.concatenate(parts, axis=0)


def corr_kernel(factor, pieces, wide, slots, landing, pins, meta, *refs):
    own, other = strips_in(refs[: pieces[0]]), strips_in(refs[pieces[0] : sum(pieces[:2])])
    refs = refs[sum(pieces[:2]) :]
    came_own, came_other = strips_in(refs[: pieces[2]]), strips_in(refs[pieces[2] : pieces[2] + pieces[3]])
    queries, *refs = refs[pieces[2] + pieces[3] :]
    landed = refs.pop(0) if landing else None
    out, *refs = refs[1 + pins :]
    pair = refs.pop(0) if wide else None
    done, values, sums, sums_two, sems, land_sems = refs
    rows_n, cols_n, _ = own[0].shape
    count, width = came_own[0].shape[0], done.shape[2]
    raw = rows_n * cols_n
    ones = (rows_n // 2) * (cols_n // 2)

    copies = []
    for index, slot in enumerate(landing):
        copies.append(pltpu.make_async_copy(landed.at[index], out.at[meta[slot]], land_sems.at[index]))
        copies[-1].start()

    def times(left):
        return jnp.dot(left, queries[...], preferred_element_type=jnp.float32) * factor

    def store(index, at, part):
        done[index, at : at + part.shape[0]] = part[:, :width].astype(done.dtype)
        if wide:
            pair[index, at : at + part.shape[0]] = part[:, width:].astype(done.dtype)

    for index in range(len(own)):

        def raw_row(row):
            return jnp.concatenate([own[index][row], other[index][row]], axis=1)

        def came_rows():
            return jnp.concatenate([came_own[index][...], came_other[index][...]], axis=1)

        @pl.when(meta[0] == 0)
        def _():
            for row in range(rows_n):
                store(index, row * cols_n, times(raw_row(row)))
            store(index, raw, times(came_rows()))

        @pl.when(meta[0] != 0)
        def _():
            for row in range(count // cols_n, rows_n):
                values[row * cols_n : (row + 1) * cols_n] = times(raw_row(row))
            values[raw : raw + count] = times(came_rows())
            levels = [pooled_levels(half[index], sums, sums_two).astype(done.dtype) for half in (own, other)]
            lower = raw + count
            values[lower : lower + count] = times(jnp.concatenate(levels, axis=1))
            segments = [
                (values, count, raw),
                (values, raw, raw + ones),
                (values, lower, lower + ones),
                (values, raw + ones, raw + count),
                (values, lower + ones, lower + count),
            ]
            step = cols_n // 2
            for at, run in enumerate(chunks(segments, step)):
                store(index, at * step, joined(run))

        copies.append(pltpu.make_async_copy(done.at[index], out.at[meta[slots[index]]], sems.at[index]))
        copies[-1].start()
    for copy in copies:
        copy.wait()


def gate_kernel(*refs):
    pass


def far_raw_kernel(factor, landing, meta, own, other, own_swapped, other_swapped, queries, landed, _, done, out, values, sums, sums_two, land_sems):
    rows_n, cols_n, _ = own.shape[1:]
    count = done.shape[1] - rows_n * cols_n
    raw = rows_n * cols_n
    ones = (rows_n // 2) * (cols_n // 2)

    copies = []
    for index, slot in enumerate(landing):
        copies.append(pltpu.make_async_copy(landed.at[index], out.at[meta[slot]], land_sems.at[index]))
        copies[-1].start()

    def times(left):
        return jnp.dot(left, queries[...], preferred_element_type=jnp.float32) * factor

    for index, halves in enumerate(((own, other), (own_swapped, other_swapped))):

        def raw_row(row):
            return jnp.concatenate([half[0, row] for half in halves], axis=1)

        @pl.when(meta[0] == 0)
        def _():
            for row in range(rows_n):
                done[index, row * cols_n : (row + 1) * cols_n] = times(raw_row(row)).astype(done.dtype)
            done[index, raw : raw + count] = jnp.zeros((count, done.shape[2]), done.dtype)

        @pl.when(meta[0] != 0)
        def _():
            for row in range(count // cols_n, rows_n):
                values[row * cols_n : (row + 1) * cols_n] = times(raw_row(row))
            levels = [pooled_levels(half.at[0], sums, sums_two).astype(done.dtype) for half in halves]
            values[raw : raw + count] = times(jnp.concatenate(levels, axis=1))
            segments = [
                (values, count, raw),
                (values, raw, raw + ones),
                (values, raw, raw + ones),
                (values, raw + ones, raw + count),
                (values, raw + ones, raw + count),
            ]
            step = cols_n // 2
            for at, run in enumerate(chunks(segments, step)):
                part = joined(run)
                done[index, at * step : at * step + part.shape[0]] = part.astype(done.dtype)

    for copy in copies:
        copy.wait()


def far_came_kernel(factor, slots, landing, meta, came_own, came_other, came_own_swapped, came_other_swapped, queries, landed, done_in, _, done, out, values, sems, land_sems):
    count = came_own.shape[1]
    raw = done.shape[1] - count
    ones = count * 4 // 5
    copies = []
    for index, slot in enumerate(landing):
        copies.append(pltpu.make_async_copy(landed.at[index], out.at[meta[slot]], land_sems.at[index]))
        copies[-1].start()

    for index, halves in enumerate(((came_own, came_other), (came_own_swapped, came_other_swapped))):
        left = jnp.concatenate([half[0] for half in halves], axis=1)
        part = jnp.dot(left, queries[...], preferred_element_type=jnp.float32) * factor

        @pl.when(meta[0] == 0)
        def _():
            done[index, raw : raw + count] = part.astype(done.dtype)

        @pl.when(meta[0] != 0)
        def _():
            values[:count] = part
            at = raw - count
            for first, last, into in ((0, ones, at), (ones, count, at + 2 * ones)):
                start = into // 16 * 16
                end = -(-(into + last - first) // 16) * 16
                parts = [values[first:last]]
                if start < into:
                    parts.insert(0, done[index, start : start + 16].astype(jnp.float32)[: into - start])
                over = end - (into + last - first)
                if over:
                    parts.append(done[index, end - 16 : end].astype(jnp.float32)[16 - over :])
                done[index, start:end] = jnp.concatenate(parts, axis=0).astype(done.dtype)

        copies.append(pltpu.make_async_copy(done.at[index], out.at[meta[slots[index]]], sems.at[index]))
        copies[-1].start()
    for copy in copies:
        copy.wait()


def ring_local(frame_one, frame_two):
    rows_axis = lax.axis_size("rows")
    rows_n, cols_n, chans = frame_two.shape
    queries_n = frame_one.shape[0]
    half_rows = rows_n // 2
    raw = half_rows * cols_n
    count = (half_rows // 2) * (cols_n // 2) + (half_rows // 4) * (cols_n // 4)
    factor = float(1.0 / (2 * chans) ** 0.5)
    me, side = lax.axis_index("rows"), lax.axis_index("chan")

    chips = rows_axis // 2
    columns, half_way = chips // 2, chips // 2
    order = [2 * z for z in range(columns)] + [2 * z + 1 for z in reversed(range(columns))]
    ring = [(2 * order[p], 2 * order[(p + 1) % chips]) for p in range(chips)]
    ring += [(2 * order[p] + 1, 2 * order[p - 1] + 1) for p in range(chips)]
    swap = [(r, r ^ 1) for r in range(rows_axis)]
    across = [(0, 1), (1, 0)]

    core, column, line = me % 2, me // 4, (me // 2) % 2
    place = jnp.where(line == 0, column, chips - 1 - column)
    steps = jnp.arange(half_way + 1, dtype=jnp.int32)

    def strips_of(c):
        p = (place + jnp.where(c == 0, -steps, steps)) % chips
        chip = jnp.where(p < columns, 2 * p, 2 * (chips - 1 - p) + 1)
        return [2 * chip + c, 2 * chip + 1 - c]

    meta = jnp.concatenate([side[None], *strips_of(core), *strips_of(1 - core)]).astype(jnp.int32)

    def slots_of(d, other_core):
        first = 1 + (2 * other_core) * (half_way + 1) + d
        return (first,) if d in (0, half_way) else (first, first + half_way + 1)

    in_vmem = pl.BlockSpec(memory_space=pltpu.VMEM)
    anywhere = pl.BlockSpec(memory_space=pl.ANY)
    scalars = pl.BlockSpec(memory_space=pltpu.SMEM)
    out_type = jax.ShapeDtypeStruct((rows_axis, raw + count, queries_n), frame_two.dtype)
    pooling = [
        pltpu.VMEM((half_rows // 2, cols_n, chans), jnp.float32),
        pltpu.VMEM((half_rows // 4, cols_n // 2, chans), jnp.float32),
    ]
    params = pltpu.CompilerParams(vmem_limit_bytes=VMEM_BYTES)
    def modelled(us):
        return pl.CostEstimate(flops=int(us * 10**9) + 1000, bytes_accessed=1000, transcendentals=0)


    def make_extra(out, halves, cost=0, pins=(), flip=False):
        strips = sum(half.shape[0] for half in halves)
        handed = () if out is None else (out,)
        return pl.pallas_call(
            functools.partial(extra_kernel, len(halves), 2, flip),
            out_shape=(jax.ShapeDtypeStruct((strips, count, chans), frame_two.dtype), out_type),
            in_specs=[scalars] + [in_vmem] * len(halves) + [anywhere] * len(handed + pins),
            out_specs=(in_vmem, anywhere),
            scratch_shapes=pooling,
            input_output_aliases={1 + len(halves): 1} if handed else {},
            compiler_params=params,
            cost_estimate=modelled(cost),
            name="extra",
        )(meta, *halves, *handed, *pins)

    def correlate(out, slots, own, other, came_own, came_other, landing=(), landed=None, cost=0, pins=()):
        parts = (own, other, came_own, came_other)
        strips = sum(piece.shape[0] for piece in own)
        operands = [*own, *other, *came_own, *came_other, queries_wide]
        pair_type = jax.ShapeDtypeStruct((strips, raw + count, queries_n), frame_two.dtype)
        return pl.pallas_call(
            functools.partial(corr_kernel, factor, tuple(len(part) for part in parts), True, slots, landing, len(pins)),
            out_shape=(out_type, pair_type),
            in_specs=[scalars] + [in_vmem] * len(operands) + [anywhere] * (1 + bool(landing) + len(pins)),
            out_specs=(anywhere, in_vmem),
            scratch_shapes=[
                pltpu.VMEM((strips, raw + count, queries_n), frame_two.dtype),
                pltpu.VMEM((raw + 2 * count, 2 * queries_n), jnp.float32),
                *pooling,
                pltpu.SemaphoreType.DMA((strips,)),
                pltpu.SemaphoreType.DMA((max(1, len(landing)),)),
            ],
            input_output_aliases={1 + len(operands) + bool(landing): 0},
            compiler_params=params,
            cost_estimate=modelled(cost),
            name="correlate",
        )(meta, *operands, *([landed] if landing else []), out, *pins)

    def correlate_far_raw(out, halves, landing, landed, cost=0):
        done_type = jax.ShapeDtypeStruct((2, raw + count, queries_n), frame_two.dtype)
        return pl.pallas_call(
            functools.partial(far_raw_kernel, factor, landing),
            out_shape=(done_type, out_type),
            in_specs=[scalars] + [in_vmem] * 5 + [anywhere] * 2,
            out_specs=(in_vmem, anywhere),
            scratch_shapes=[
                pltpu.VMEM((raw + count, queries_n), jnp.float32),
                *pooling,
                pltpu.SemaphoreType.DMA((len(landing),)),
            ],
            input_output_aliases={7: 1},
            compiler_params=params,
            cost_estimate=modelled(cost),
            name="far_raw",
        )(meta, *halves, queries, landed, out)

    def correlate_far_came(out, done, slots, extras, landing, landed, cost=0):
        return pl.pallas_call(
            functools.partial(far_came_kernel, factor, slots, landing),
            out_shape=(jax.ShapeDtypeStruct(done.shape, done.dtype), out_type),
            in_specs=[scalars] + [in_vmem] * 5 + [anywhere, in_vmem, anywhere],
            out_specs=(in_vmem, anywhere),
            scratch_shapes=[
                pltpu.VMEM((count, queries_n), jnp.float32),
                pltpu.SemaphoreType.DMA((2,)),
                pltpu.SemaphoreType.DMA((len(landing),)),
            ],
            input_output_aliases={7: 0, 8: 1},
            compiler_params=params,
            cost_estimate=modelled(cost),
            name="far_came",
        )(meta, *extras, queries, landed, done, out)[1]

    def gate(out, pins, cost):
        handed = (out, *pins)
        return pl.pallas_call(
            gate_kernel,
            out_shape=tuple(jax.ShapeDtypeStruct(array.shape, array.dtype) for array in handed),
            in_specs=[anywhere] * len(handed),
            out_specs=(anywhere,) * len(handed),
            input_output_aliases={index: index for index in range(len(handed))},
            compiler_params=params,
            cost_estimate=modelled(cost),
            name="gate",
        )(*handed)

    mine = lax.dynamic_slice_in_dim(frame_two, side * half_rows, half_rows, axis=0)[None]
    theirs = lax.dynamic_slice_in_dim(frame_two, (1 - side) * half_rows, half_rows, axis=0)[None]
    if G("XQ"):
        sent = jnp.concatenate([theirs.reshape(raw, chans), frame_one], axis=0)
        got = lax.ppermute(sent, "chan", across)
        partner, queries_other = got[:raw].reshape(theirs.shape), got[raw:]
    else:
        partner = lax.ppermute(theirs, "chan", across)
        queries_other = lax.ppermute(frame_one, "chan", across)
    queries = jnp.concatenate([frame_one.T, queries_other.T], axis=0)
    queries_wide = jnp.concatenate([queries, lax.ppermute(queries, "rows", swap)], axis=1)

    def permute_rows(pairs, pieces):
        return [lax.ppermute(piece, "rows", pairs) for piece in pieces]

    def whole(pieces):
        return pieces if len(pieces) == 1 else [jnp.concatenate(pieces, axis=0)]

    came = {0: ([mine], [partner])}
    moving = [[half, *permute_rows(swap, [half])] for half in (mine, partner)]
    join = [G("JA"), G("JB")]
    for d in range(1, half_way + 1):
        if d == half_way:
            moving = [[pieces[0][:1]] for pieces in moving]
        if d == half_way - 1 and G("BSPL"):
            moving[1] = [moving[1][0][:1], moving[1][0][1:]]
        moving = [
            permute_rows(ring, whole(pieces) if d == join[part] else pieces) for part, pieces in enumerate(moving)
        ]
        came[d] = tuple(moving)
    far_swapped = [permute_rows(swap, half)[0] for half in came[half_way]]

    across_came = {}

    def do_extra(out, d, part, pin=None):
        pins = () if pin is None else tuple(across_came[pin]) if isinstance(pin, tuple) else (pin,)
        across_came[d, 1 - part] = []
        groups = [[piece] for piece in came[d][part]] if part and d == half_way - 1 else [came[d][part]]
        for pieces in groups:
            extra, out = make_extra(out, pieces, G(f"X{d}{part}"), pins)
            across_came[d, 1 - part].append(lax.ppermute(extra, "chan", across))
            pins = ()
        return out

    lag = G("LAG")
    waiting = []

    def landing(now):
        if waiting and waiting[0][0] <= now:
            return waiting.pop(0)[1:]
        return (), None

    def product(out, d, pins=()):
        out, pair = correlate(out, slots_of(d, 0), *came[d], across_came[d, 0], across_came[d, 1], *landing(d), G(f"C{d}"), pins)
        waiting.append((d + lag, slots_of(d, 1), permute_rows(swap, [pair])[0]))
        return out

    out = do_extra(None, 0, 0, partner if G("PINX") else None)
    lacking, out = make_extra(out, [theirs], G("X01"), tuple(across_came[0, 1]) if G("PIN01") else (), flip=True)
    across_came[0, 0] = [lacking]
    if G("C0POS") == 0: out = product(out, 0)
    out = do_extra(out, 1, 0, (0, 1) if G("PIN0") else None)
    if G("C0POS") == 1: out = product(out, 0)
    out = do_extra(out, 1, 1, (1, 1))
    if G("C0POS") == 2: out = product(out, 0)
    for d in range(2, half_way):
        out = do_extra(out, d, 0, (d - 1, 0))
        out = product(out, d - 1)
        out = do_extra(out, d, 1, (d, 1))
    out = do_extra(out, half_way, 0)
    if G("C3POS") == 0: out = product(out, half_way - 1)
    out = do_extra(out, half_way, 1, far_swapped[0] if G("PS0") else None)
    if G("C3POS") == 1: out = product(out, half_way - 1)
    done, out = correlate_far_raw(out, [came[half_way][0][0], came[half_way][1][0], *far_swapped], *landing(half_way), G("F0"))
    far = [across_came[half_way, 0][0], across_came[half_way, 1][0]]
    if G("GATE"): out, *far = gate(out, far, G("GATE"))
    far += permute_rows(swap, far)
    slots = slots_of(half_way, 0) + slots_of(half_way, 1)
    return correlate_far_came(out, done, slots, far, *landing(half_way + 1), G("F1"))


def solution(mesh):
    rows_axis, groups = mesh.shape["rows"], mesh.shape["chan"]

    def local(frame_one, frame_two):
        rows_n, cols_n, chans = frame_two.shape
        ring = groups == 2 and rows_axis % 8 == 0 and rows_axis >= 16 and rows_n % 8 == 0 and cols_n % 32 == 0 and chans % LANES == 0
        return (ring_local if ring else gather_local)(frame_one, frame_two)

    in_specs = (P("rows", "chan"), P("rows", None, "chan"))
    out_specs = P(None, "chan", "rows")
    return jax.shard_map(local, mesh=mesh, in_specs=in_specs, out_specs=out_specs, check_vma=False)
```

```python
import functools

import jax
import jax.numpy as jnp
from jax import lax
from jax.experimental import pallas as pl
from jax.experimental.pallas import tpu as pltpu
from jax.sharding import PartitionSpec as P

LANES = 128
PARAMS = {'LAG': 2, 'F0': 10, 'F1': 0, 'PS0': 2, 'JA': 1, 'JB': 1, 'C0POS': 2, 'R3POS': 0, 'GATE': 30, 'F3': 10, 'F2': 10, 'PE4': 1, 'X00': 10, 'X01': 10, 'C0': 10, 'X10': 10, 'X11': 10, 'C1': 10, 'X20': 10, 'X21': 10, 'C2': 10, 'X30': 10, 'X31': 10, 'C3': 10, 'X40': 10, 'X41': 10, 'C4': 10}


def G(name):
    return PARAMS.get(name, 0)


VMEM_BYTES = 28 * 1024 * 1024


def pool_strip(strip):
    full = strip.astype(jnp.float32)
    rows_n, cols_n, chans = full.shape
    level_one = full.reshape(rows_n // 2, 2, cols_n // 2, 2, chans).mean(axis=(1, 3))
    level_two = level_one.reshape(rows_n // 4, 2, cols_n // 4, 2, chans).mean(axis=(1, 3))
    joined = jnp.concatenate(
        [full.reshape(-1, chans), level_one.reshape(-1, chans), level_two.reshape(-1, chans)],
        axis=0,
    )
    return joined.astype(jnp.bfloat16)


def gather_local(frame_one, frame_two):
    groups = lax.axis_size("chan")
    queries = lax.all_gather(frame_one, "chan", axis=0, tiled=False)
    channels = queries.shape[0] * queries.shape[2]
    factor = 1.0 / jnp.sqrt(jnp.float32(channels))
    pooled = pool_strip(frame_two)
    share = pooled.shape[0] // groups
    traded = lax.all_to_all(
        pooled.reshape(groups, share, pooled.shape[1]), "chan", split_axis=0, concat_axis=0, tiled=True
    )
    gathered = lax.all_gather(traded, "rows", axis=0, tiled=False)
    values = jnp.einsum("skpc,kqc->spq", gathered, queries, preferred_element_type=jnp.float32)
    return (values * factor).astype(jnp.bfloat16)


def pooled_levels(half, sums, sums_two):
    rows_n, cols_n, _ = half.shape
    means = []
    for row in range(rows_n // 2):
        sums[row] = half[2 * row].astype(jnp.float32) + half[2 * row + 1].astype(jnp.float32)
        left = sums[row, pl.ds(0, cols_n // 2, stride=2), :]
        right = sums[row, pl.ds(1, cols_n // 2, stride=2), :]
        means.append((left + right) * 0.25)
    means_two = []
    for row in range(rows_n // 4):
        sums_two[row] = means[2 * row] + means[2 * row + 1]
        left = sums_two[row, pl.ds(0, cols_n // 4, stride=2), :]
        right = sums_two[row, pl.ds(1, cols_n // 4, stride=2), :]
        means_two.append((left + right) * 0.25)
    return jnp.concatenate(means + means_two, axis=0)


def strips_in(refs):
    return [ref.at[index] for ref in refs for index in range(ref.shape[0])]


def extra_kernel(pieces, results, flip, meta, *refs):
    halves = strips_in(refs[:pieces])
    extra, sums, sums_two = refs[-2 - results], *refs[-2:]
    count, cols_n = extra.shape[1], halves[0].shape[1]
    upper = meta[0] == (1 if flip else 0)

    @pl.when(upper)
    def _():
        for index, half in enumerate(halves):
            extra[index] = pooled_levels(half, sums, sums_two).astype(extra.dtype)

    @pl.when(jnp.logical_not(upper))
    def _():
        for index, half in enumerate(halves):
            parts, left, row = [], count, 0
            while left > 0:
                parts.append(half[row].astype(jnp.float32)[: min(left, cols_n)])
                left, row = left - cols_n, row + 1
            extra[index] = jnp.concatenate(parts, axis=0).astype(extra.dtype)


def chunks(segments, step):
    todo, runs = list(segments), []
    while todo:
        run, room = [], step
        while todo and room > 0:
            ref, first, last = todo.pop(0)
            take = min(room, last - first)
            run.append((ref, first, first + take))
            room -= take
            if first + take < last:
                todo.insert(0, (ref, first + take, last))
        runs.append(run)
    return runs


def joined(run):
    parts = [ref[first:last].astype(jnp.float32) for ref, first, last in run]
    return parts[0] if len(parts) == 1 else jnp.concatenate(parts, axis=0)


def corr_kernel(factor, pieces, wide, slots, landing, pins, meta, *refs):
    own, other = strips_in(refs[: pieces[0]]), strips_in(refs[pieces[0] : sum(pieces[:2])])
    refs = refs[sum(pieces[:2]) :]
    came_own, came_other = strips_in(refs[: pieces[2]]), strips_in(refs[pieces[2] : pieces[2] + pieces[3]])
    queries, *refs = refs[pieces[2] + pieces[3] :]
    landed = refs.pop(0) if landing else None
    out, *refs = refs[1 + pins :]
    pair = refs.pop(0) if wide else None
    done, values, sums, sums_two, sems, land_sems = refs
    rows_n, cols_n, _ = own[0].shape
    count, width = came_own[0].shape[0], done.shape[2]
    raw = rows_n * cols_n
    ones = (rows_n // 2) * (cols_n // 2)

    copies = []
    for index, slot in enumerate(landing):
        copies.append(pltpu.make_async_copy(landed.at[index], out.at[meta[slot]], land_sems.at[index]))
        copies[-1].start()

    def times(left):
        return jnp.dot(left, queries[...], preferred_element_type=jnp.float32) * factor

    def store(index, at, part):
        done[index, at : at + part.shape[0]] = part[:, :width].astype(done.dtype)
        if wide:
            pair[index, at : at + part.shape[0]] = part[:, width:].astype(done.dtype)

    for index in range(len(own)):

        def raw_row(row):
            return jnp.concatenate([own[index][row], other[index][row]], axis=1)

        def came_rows():
            return jnp.concatenate([came_own[index][...], came_other[index][...]], axis=1)

        @pl.when(meta[0] == 0)
        def _():
            for row in range(rows_n):
                store(index, row * cols_n, times(raw_row(row)))
            store(index, raw, times(came_rows()))

        @pl.when(meta[0] != 0)
        def _():
            for row in range(count // cols_n, rows_n):
                values[row * cols_n : (row + 1) * cols_n] = times(raw_row(row))
            values[raw : raw + count] = times(came_rows())
            levels = [pooled_levels(half[index], sums, sums_two).astype(done.dtype) for half in (own, other)]
            lower = raw + count
            values[lower : lower + count] = times(jnp.concatenate(levels, axis=1))
            segments = [
                (values, count, raw),
                (values, raw, raw + ones),
                (values, lower, lower + ones),
                (values, raw + ones, raw + count),
                (values, lower + ones, lower + count),
            ]
            step = cols_n // 2
            for at, run in enumerate(chunks(segments, step)):
                store(index, at * step, joined(run))

        copies.append(pltpu.make_async_copy(done.at[index], out.at[meta[slots[index]]], sems.at[index]))
        copies[-1].start()
    for copy in copies:
        copy.wait()


def gate_kernel(*refs):
    pass


def raw_kernel(factor, arrays, wide, landing, meta, *refs):
    own, other = strips_in(refs[:arrays]), strips_in(refs[arrays : 2 * arrays])
    queries, *refs = refs[2 * arrays :]
    landed = refs.pop(0) if landing else None
    _, out, done, *refs = refs
    pair = refs.pop(0) if wide else None
    values, sums, sums_two, land_sems = refs
    rows_n, cols_n, _ = own[0].shape
    count, width = done.shape[1] - rows_n * cols_n, done.shape[2]
    raw = rows_n * cols_n
    ones = (rows_n // 2) * (cols_n // 2)

    copies = []
    for index, slot in enumerate(landing):
        copies.append(pltpu.make_async_copy(landed.at[index], out.at[meta[slot]], land_sems.at[index]))
        copies[-1].start()

    def times(left):
        return jnp.dot(left, queries[...], preferred_element_type=jnp.float32) * factor

    def store(index, at, part):
        done[index, at : at + part.shape[0]] = part[:, :width].astype(done.dtype)
        if wide:
            pair[index, at : at + part.shape[0]] = part[:, width:].astype(done.dtype)

    for index, halves in enumerate(zip(own, other)):

        def raw_row(row):
            return jnp.concatenate([half[row] for half in halves], axis=1)

        @pl.when(meta[0] == 0)
        def _():
            for row in range(rows_n):
                store(index, row * cols_n, times(raw_row(row)))
            store(index, raw, jnp.zeros((count, values.shape[1]), jnp.float32))

        @pl.when(meta[0] != 0)
        def _():
            for row in range(count // cols_n, rows_n):
                values[row * cols_n : (row + 1) * cols_n] = times(raw_row(row))
            levels = [pooled_levels(half, sums, sums_two).astype(done.dtype) for half in halves]
            values[raw : raw + count] = times(jnp.concatenate(levels, axis=1))
            segments = [
                (values, count, raw),
                (values, raw, raw + ones),
                (values, raw, raw + ones),
                (values, raw + ones, raw + count),
                (values, raw + ones, raw + count),
            ]
            step = cols_n // 2
            for at, run in enumerate(chunks(segments, step)):
                store(index, at * step, joined(run))

    for copy in copies:
        copy.wait()


def came_kernel(factor, arrays, wide, late, pins, slots, meta, *refs):
    own, other = strips_in(refs[:arrays]), strips_in(refs[arrays : 2 * arrays])
    queries, *refs = refs[2 * arrays :]
    late_rows = refs.pop(0) if late else None
    refs = refs[2 + late + pins :]
    out, done, *refs = refs
    late_done = refs.pop(0) if late else None
    pair = refs.pop(0) if wide else None
    values, sems = refs
    count, width = own[0].shape[0], done.shape[2]
    raw = done.shape[1] - count
    ones = count * 4 // 5
    copies = []

    def leave(strip):
        copies.append(pltpu.make_async_copy(strip, out.at[meta[slots[len(copies)]]], sems.at[len(copies)]))
        copies[-1].start()

    def merge(strip, part):
        @pl.when(meta[0] == 0)
        def _():
            strip[raw : raw + count] = part.astype(done.dtype)

        @pl.when(meta[0] != 0)
        def _():
            values[...] = part
            at = raw - count
            for first, last, into in ((0, ones, at), (ones, count, at + 2 * ones)):
                start = into // 16 * 16
                end = -(-(into + last - first) // 16) * 16
                parts = [values[first:last]]
                if start < into:
                    parts.insert(0, strip[start : start + 16].astype(jnp.float32)[: into - start])
                over = end - (into + last - first)
                if over:
                    parts.append(strip[end - 16 : end].astype(jnp.float32)[16 - over :])
                strip[start:end] = jnp.concatenate(parts, axis=0).astype(done.dtype)

    if late:
        for index in range(late_done.shape[0]):
            merge(late_done.at[index], late_rows[index].astype(jnp.float32))
            leave(late_done.at[index])
    for index, halves in enumerate(zip(own, other)):
        left = jnp.concatenate([half[...] for half in halves], axis=1)
        part = jnp.dot(left, queries[...], preferred_element_type=jnp.float32) * factor
        if wide:
            pair[index] = part[:, width:].astype(done.dtype)
        merge(done.at[index], part[:, :width])
        leave(done.at[index])
    for copy in copies:
        copy.wait()


def ring_local(frame_one, frame_two):
    rows_axis = lax.axis_size("rows")
    rows_n, cols_n, chans = frame_two.shape
    queries_n = frame_one.shape[0]
    half_rows = rows_n // 2
    raw = half_rows * cols_n
    count = (half_rows // 2) * (cols_n // 2) + (half_rows // 4) * (cols_n // 4)
    factor = float(1.0 / (2 * chans) ** 0.5)
    me, side = lax.axis_index("rows"), lax.axis_index("chan")

    chips = rows_axis // 2
    columns, half_way = chips // 2, chips // 2
    order = [2 * z for z in range(columns)] + [2 * z + 1 for z in reversed(range(columns))]
    ring = [(2 * order[p], 2 * order[(p + 1) % chips]) for p in range(chips)]
    ring += [(2 * order[p] + 1, 2 * order[p - 1] + 1) for p in range(chips)]
    swap = [(r, r ^ 1) for r in range(rows_axis)]
    across = [(0, 1), (1, 0)]

    core, column, line = me % 2, me // 4, (me // 2) % 2
    place = jnp.where(line == 0, column, chips - 1 - column)
    steps = jnp.arange(half_way + 1, dtype=jnp.int32)

    def strips_of(c):
        p = (place + jnp.where(c == 0, -steps, steps)) % chips
        chip = jnp.where(p < columns, 2 * p, 2 * (chips - 1 - p) + 1)
        return [2 * chip + c, 2 * chip + 1 - c]

    meta = jnp.concatenate([side[None], *strips_of(core), *strips_of(1 - core)]).astype(jnp.int32)

    def slots_of(d, other_core):
        first = 1 + (2 * other_core) * (half_way + 1) + d
        return (first,) if d in (0, half_way) else (first, first + half_way + 1)

    in_vmem = pl.BlockSpec(memory_space=pltpu.VMEM)
    anywhere = pl.BlockSpec(memory_space=pl.ANY)
    scalars = pl.BlockSpec(memory_space=pltpu.SMEM)
    out_type = jax.ShapeDtypeStruct((rows_axis, raw + count, queries_n), frame_two.dtype)
    pooling = [
        pltpu.VMEM((half_rows // 2, cols_n, chans), jnp.float32),
        pltpu.VMEM((half_rows // 4, cols_n // 2, chans), jnp.float32),
    ]
    params = pltpu.CompilerParams(vmem_limit_bytes=VMEM_BYTES)
    def modelled(us):
        return pl.CostEstimate(flops=int(us * 10**9) + 1000, bytes_accessed=1000, transcendentals=0)


    def make_extra(out, halves, cost=0, pins=(), flip=False, carry=False):
        strips = sum(half.shape[0] for half in halves)
        handed = () if out is None else (out,)
        carried = tuple(halves) if carry else ()
        aliases = {1 + len(halves): 1} if handed else {}
        aliases.update({1 + index: 2 + index for index in range(len(carried))})
        return pl.pallas_call(
            functools.partial(extra_kernel, len(halves), 2 + len(carried), flip),
            out_shape=(jax.ShapeDtypeStruct((strips, count, chans), frame_two.dtype), out_type)
            + tuple(jax.ShapeDtypeStruct(half.shape, half.dtype) for half in carried),
            in_specs=[scalars] + [in_vmem] * len(halves) + [anywhere] * len(handed + pins),
            out_specs=(in_vmem, anywhere) + (in_vmem,) * len(carried),
            scratch_shapes=pooling,
            input_output_aliases=aliases,
            compiler_params=params,
            cost_estimate=modelled(cost),
            name="extra",
        )(meta, *halves, *handed, *pins)

    def correlate(out, slots, own, other, came_own, came_other, landing=(), landed=None, cost=0, pins=()):
        parts = (own, other, came_own, came_other)
        strips = sum(piece.shape[0] for piece in own)
        operands = [*own, *other, *came_own, *came_other, queries_wide]
        pair_type = jax.ShapeDtypeStruct((strips, raw + count, queries_n), frame_two.dtype)
        return pl.pallas_call(
            functools.partial(corr_kernel, factor, tuple(len(part) for part in parts), True, slots, landing, len(pins)),
            out_shape=(out_type, pair_type),
            in_specs=[scalars] + [in_vmem] * len(operands) + [anywhere] * (1 + bool(landing) + len(pins)),
            out_specs=(anywhere, in_vmem),
            scratch_shapes=[
                pltpu.VMEM((strips, raw + count, queries_n), frame_two.dtype),
                pltpu.VMEM((raw + 2 * count, 2 * queries_n), jnp.float32),
                *pooling,
                pltpu.SemaphoreType.DMA((strips,)),
                pltpu.SemaphoreType.DMA((max(1, len(landing)),)),
            ],
            input_output_aliases={1 + len(operands) + bool(landing): 0},
            compiler_params=params,
            cost_estimate=modelled(cost),
            name="correlate",
        )(meta, *operands, *([landed] if landing else []), out, *pins)

    def product_type(strips, pixels):
        return jax.ShapeDtypeStruct((strips, pixels, queries_n), frame_two.dtype)

    def raw_rows(out, own, other, wide, landing=(), landed=None, cost=0):
        operands = [*own, *other, queries_wide if wide else queries]
        strips = sum(half.shape[0] for half in own)
        return pl.pallas_call(
            functools.partial(raw_kernel, factor, len(own), wide, landing),
            out_shape=(out_type,) + (product_type(strips, raw + count),) * (1 + wide),
            in_specs=[scalars] + [in_vmem] * len(operands) + [anywhere] * (1 + bool(landing)),
            out_specs=(anywhere,) + (in_vmem,) * (1 + wide),
            scratch_shapes=[
                pltpu.VMEM((raw + count, queries_n * (1 + wide)), jnp.float32),
                *pooling,
                pltpu.SemaphoreType.DMA((max(1, len(landing)),)),
            ],
            input_output_aliases={1 + len(operands) + bool(landing): 0},
            compiler_params=params,
            cost_estimate=modelled(cost),
            name="raw_rows",
        )(meta, *operands, *([landed] if landing else []), out)

    def came_rows(out, done, slots, own, other, wide, late=(), cost=0, pins=()):
        operands = [*own, *other, queries_wide if wide else queries, *late[:1]]
        first = 1 + len(operands)
        inout = [out, done, *late[1:]]
        extra_types = (product_type(done.shape[0], count),) if wide else ()
        return pl.pallas_call(
            functools.partial(came_kernel, factor, len(own), wide, len(late) // 2, len(pins), slots),
            out_shape=tuple(jax.ShapeDtypeStruct(array.shape, array.dtype) for array in inout) + extra_types,
            in_specs=[scalars] + [in_vmem] * len(operands) + [anywhere] + [in_vmem] * (len(inout) - 1) + [anywhere] * len(pins),
            out_specs=(anywhere,) + (in_vmem,) * (len(inout) - 1 + wide),
            scratch_shapes=[
                pltpu.VMEM((count, queries_n), jnp.float32),
                pltpu.SemaphoreType.DMA((len(slots),)),
            ],
            input_output_aliases={first + index: index for index in range(len(inout))},
            compiler_params=params,
            cost_estimate=modelled(cost),
            name="came_rows",
        )(meta, *operands, *inout, *pins)

    def gate(out, pins, cost):
        handed = (out, *pins)
        return pl.pallas_call(
            gate_kernel,
            out_shape=tuple(jax.ShapeDtypeStruct(array.shape, array.dtype) for array in handed),
            in_specs=[anywhere] * len(handed),
            out_specs=(anywhere,) * len(handed),
            input_output_aliases={index: index for index in range(len(handed))},
            compiler_params=params,
            cost_estimate=modelled(cost),
            name="gate",
        )(*handed)

    mine = lax.dynamic_slice_in_dim(frame_two, side * half_rows, half_rows, axis=0)[None]
    theirs = lax.dynamic_slice_in_dim(frame_two, (1 - side) * half_rows, half_rows, axis=0)[None]
    if G("XQ"):
        sent = jnp.concatenate([theirs.reshape(raw, chans), frame_one], axis=0)
        got = lax.ppermute(sent, "chan", across)
        partner, queries_other = got[:raw].reshape(theirs.shape), got[raw:]
    else:
        partner = lax.ppermute(theirs, "chan", across)
        queries_other = lax.ppermute(frame_one, "chan", across)
    queries = jnp.concatenate([frame_one.T, queries_other.T], axis=0)
    queries_wide = jnp.concatenate([queries, lax.ppermute(queries, "rows", swap)], axis=1)

    def permute_rows(pairs, pieces):
        return [lax.ppermute(piece, "rows", pairs) for piece in pieces]

    def whole(pieces):
        return pieces if len(pieces) == 1 else [jnp.concatenate(pieces, axis=0)]

    came = {0: ([mine], [partner])}
    moving = [[half, *permute_rows(swap, [half])] for half in (mine, partner)]
    join = [G("JA"), G("JB")]
    for d in range(1, half_way + 1):
        if d == half_way:
            moving = [[pieces[0][:1]] for pieces in moving]
        if d == half_way - 1 and G("BSPL"):
            moving[1] = [moving[1][0][:1], moving[1][0][1:]]
        moving = [
            permute_rows(ring, whole(pieces) if d == join[part] else pieces) for part, pieces in enumerate(moving)
        ]
        came[d] = tuple(moving)
    across_came = {}

    def do_extra(out, d, part, pin=None):
        pins = () if pin is None else tuple(across_came[pin]) if isinstance(pin, tuple) else (pin,)
        across_came[d, 1 - part] = []
        groups = [[piece] for piece in came[d][part]] if part and d == half_way - 1 else [came[d][part]]
        for pieces in groups:
            extra, out = make_extra(out, pieces, G(f"X{d}{part}"), pins)
            across_came[d, 1 - part].append(lax.ppermute(extra, "chan", across))
            pins = ()
        return out

    lag = G("LAG")
    waiting = []

    def landing(now):
        if waiting and waiting[0][0] <= now:
            return waiting.pop(0)[1:]
        return (), None

    def product(out, d, pins=()):
        out, pair = correlate(out, slots_of(d, 0), *came[d], across_came[d, 0], across_came[d, 1], *landing(d), G(f"C{d}"), pins)
        waiting.append((d + lag, slots_of(d, 1), permute_rows(swap, [pair])[0]))
        return out

    out = do_extra(None, 0, 0, partner if G("PINX") else None)
    lacking, out = make_extra(out, [theirs], G("X01"), tuple(across_came[0, 1]) if G("PIN01") else (), flip=True)
    across_came[0, 0] = [lacking]
    if G("C0POS") == 0: out = product(out, 0)
    out = do_extra(out, 1, 0, (0, 1) if G("PIN0") else None)
    if G("C0POS") == 1: out = product(out, 0)
    out = do_extra(out, 1, 1, (1, 1))
    if G("C0POS") == 2: out = product(out, 0)
    for d in range(2, half_way):
        out = do_extra(out, d, 0, (d - 1, 0))
        out = product(out, d - 1)
        out = do_extra(out, d, 1, (d, 1))
    near, far = half_way - 1, half_way

    def swap_one(piece):
        return permute_rows(swap, [piece])[0]

    R3 = G("R3POS")
    def near_raw(out):
        return raw_rows(out, *came[near], True, *landing(near), G("F3"))

    swapped = []

    def far_extra(out, part, pins):
        extra, out, piece = make_extra(out, came[far][part], G(f"X4{part}"), pins, carry=True)
        came[far][part][0] = piece
        across_came[far, 1 - part] = [lax.ppermute(extra, "chan", across)]
        swapped.append(swap_one(piece))
        return out

    if R3 == 0: out, near_done, near_pair = near_raw(out)
    out = far_extra(out, 0, ())
    if R3 == 1: out, near_done, near_pair = near_raw(out)
    out = far_extra(out, 1, (swapped[0],) if G("PS0") == 1 else ())
    near_late = swap_one(near_pair)
    pins = (tuple(across_came[far, 1]) if G("PE4") else ()) + ((swapped[0],) if G("PS0") == 2 else ())

    def far_rows(out):
        return raw_rows(out, [came[far][0][0], swapped[0]], [came[far][1][0], swapped[1]], False, *landing(far), G("F0"))

    def near_came(out):
        return came_rows(out, near_done, slots_of(near, 0), across_came[near, 0], across_came[near, 1], True, cost=G("F2"), pins=pins)

    if G("FAR1"): out, far_done = far_rows(out)
    out, _, near_rows = near_came(out)
    near_rows = swap_one(near_rows)
    if not G("FAR1"): out, far_done = far_rows(out)
    out, own, other = gate(out, [across_came[far, 0][0], across_came[far, 1][0]], G("GATE"))
    slots = slots_of(near, 1) + slots_of(far, 0) + slots_of(far, 1)
    return came_rows(out, far_done, slots, [own, swap_one(own)], [other, swap_one(other)], False, (near_rows, near_late), G("F1"))[0]


def solution(mesh):
    rows_axis, groups = mesh.shape["rows"], mesh.shape["chan"]

    def local(frame_one, frame_two):
        rows_n, cols_n, chans = frame_two.shape
        ring = groups == 2 and rows_axis % 8 == 0 and rows_axis >= 16 and rows_n % 8 == 0 and cols_n % 32 == 0 and chans % LANES == 0
        return (ring_local if ring else gather_local)(frame_one, frame_two)

    in_specs = (P("rows", "chan"), P("rows", None, "chan"))
    out_specs = P(None, "chan", "rows")
    return jax.shard_map(local, mesh=mesh, in_specs=in_specs, out_specs=out_specs, check_vma=False)
```

```python
import functools

import jax
import jax.numpy as jnp
from jax import lax
from jax.experimental import pallas as pl
from jax.experimental.pallas import tpu as pltpu
from jax.sharding import PartitionSpec as P

LANES = 128
PARAMS = {'LAG': 2, 'F0': 10, 'F1': 0, 'PS0': 2, 'JA': 1, 'JB': 1, 'C0POS': 2, 'R3POS': 0, 'GATE': 30, 'F3': 10, 'F2': 10, 'PE4': 0, 'X00': 10, 'X01': 10, 'C0': 10, 'X10': 10, 'X11': 10, 'C1': 10, 'X20': 10, 'X21': 10, 'C2': 10, 'X30': 10, 'X31': 10, 'C3': 10, 'X40': 10, 'X41': 10, 'C4': 10, 'NL': 1}


def G(name):
    return PARAMS.get(name, 0)


VMEM_BYTES = 28 * 1024 * 1024


def pool_strip(strip):
    full = strip.astype(jnp.float32)
    rows_n, cols_n, chans = full.shape
    level_one = full.reshape(rows_n // 2, 2, cols_n // 2, 2, chans).mean(axis=(1, 3))
    level_two = level_one.reshape(rows_n // 4, 2, cols_n // 4, 2, chans).mean(axis=(1, 3))
    joined = jnp.concatenate(
        [full.reshape(-1, chans), level_one.reshape(-1, chans), level_two.reshape(-1, chans)],
        axis=0,
    )
    return joined.astype(jnp.bfloat16)


def gather_local(frame_one, frame_two):
    groups = lax.axis_size("chan")
    queries = lax.all_gather(frame_one, "chan", axis=0, tiled=False)
    channels = queries.shape[0] * queries.shape[2]
    factor = 1.0 / jnp.sqrt(jnp.float32(channels))
    pooled = pool_strip(frame_two)
    share = pooled.shape[0] // groups
    traded = lax.all_to_all(
        pooled.reshape(groups, share, pooled.shape[1]), "chan", split_axis=0, concat_axis=0, tiled=True
    )
    gathered = lax.all_gather(traded, "rows", axis=0, tiled=False)
    values = jnp.einsum("skpc,kqc->spq", gathered, queries, preferred_element_type=jnp.float32)
    return (values * factor).astype(jnp.bfloat16)


def pooled_levels(half, sums, sums_two):
    rows_n, cols_n, _ = half.shape
    means = []
    for row in range(rows_n // 2):
        sums[row] = half[2 * row].astype(jnp.float32) + half[2 * row + 1].astype(jnp.float32)
        left = sums[row, pl.ds(0, cols_n // 2, stride=2), :]
        right = sums[row, pl.ds(1, cols_n // 2, stride=2), :]
        means.append((left + right) * 0.25)
    means_two = []
    for row in range(rows_n // 4):
        sums_two[row] = means[2 * row] + means[2 * row + 1]
        left = sums_two[row, pl.ds(0, cols_n // 4, stride=2), :]
        right = sums_two[row, pl.ds(1, cols_n // 4, stride=2), :]
        means_two.append((left + right) * 0.25)
    return jnp.concatenate(means + means_two, axis=0)


def strips_in(refs):
    return [ref.at[index] for ref in refs for index in range(ref.shape[0])]


def extra_kernel(pieces, results, flip, meta, *refs):
    halves = strips_in(refs[:pieces])
    extra, sums, sums_two = refs[-2 - results], *refs[-2:]
    count, cols_n = extra.shape[1], halves[0].shape[1]
    upper = meta[0] == (1 if flip else 0)

    @pl.when(upper)
    def _():
        for index, half in enumerate(halves):
            extra[index] = pooled_levels(half, sums, sums_two).astype(extra.dtype)

    @pl.when(jnp.logical_not(upper))
    def _():
        for index, half in enumerate(halves):
            parts, left, row = [], count, 0
            while left > 0:
                parts.append(half[row].astype(jnp.float32)[: min(left, cols_n)])
                left, row = left - cols_n, row + 1
            extra[index] = jnp.concatenate(parts, axis=0).astype(extra.dtype)


def chunks(segments, step):
    todo, runs = list(segments), []
    while todo:
        run, room = [], step
        while todo and room > 0:
            ref, first, last = todo.pop(0)
            take = min(room, last - first)
            run.append((ref, first, first + take))
            room -= take
            if first + take < last:
                todo.insert(0, (ref, first + take, last))
        runs.append(run)
    return runs


def joined(run):
    parts = [ref[first:last].astype(jnp.float32) for ref, first, last in run]
    return parts[0] if len(parts) == 1 else jnp.concatenate(parts, axis=0)


def corr_kernel(factor, pieces, wide, slots, landing, pins, meta, *refs):
    own, other = strips_in(refs[: pieces[0]]), strips_in(refs[pieces[0] : sum(pieces[:2])])
    refs = refs[sum(pieces[:2]) :]
    came_own, came_other = strips_in(refs[: pieces[2]]), strips_in(refs[pieces[2] : pieces[2] + pieces[3]])
    queries, *refs = refs[pieces[2] + pieces[3] :]
    landed = refs.pop(0) if landing else None
    out, *refs = refs[1 + pins :]
    pair = refs.pop(0) if wide else None
    done, values, sums, sums_two, sems, land_sems = refs
    rows_n, cols_n, _ = own[0].shape
    count, width = came_own[0].shape[0], done.shape[2]
    raw = rows_n * cols_n
    ones = (rows_n // 2) * (cols_n // 2)

    copies = []
    for index, slot in enumerate(landing):
        copies.append(pltpu.make_async_copy(landed.at[index], out.at[meta[slot]], land_sems.at[index]))
        copies[-1].start()

    def times(left):
        return jnp.dot(left, queries[...], preferred_element_type=jnp.float32) * factor

    def store(index, at, part):
        done[index, at : at + part.shape[0]] = part[:, :width].astype(done.dtype)
        if wide:
            pair[index, at : at + part.shape[0]] = part[:, width:].astype(done.dtype)

    for index in range(len(own)):

        def raw_row(row):
            return jnp.concatenate([own[index][row], other[index][row]], axis=1)

        def came_rows():
            return jnp.concatenate([came_own[index][...], came_other[index][...]], axis=1)

        @pl.when(meta[0] == 0)
        def _():
            for row in range(rows_n):
                store(index, row * cols_n, times(raw_row(row)))
            store(index, raw, times(came_rows()))

        @pl.when(meta[0] != 0)
        def _():
            for row in range(count // cols_n, rows_n):
                values[row * cols_n : (row + 1) * cols_n] = times(raw_row(row))
            values[raw : raw + count] = times(came_rows())
            levels = [pooled_levels(half[index], sums, sums_two).astype(done.dtype) for half in (own, other)]
            lower = raw + count
            values[lower : lower + count] = times(jnp.concatenate(levels, axis=1))
            segments = [
                (values, count, raw),
                (values, raw, raw + ones),
                (values, lower, lower + ones),
                (values, raw + ones, raw + count),
                (values, lower + ones, lower + count),
            ]
            step = cols_n // 2
            for at, run in enumerate(chunks(segments, step)):
                store(index, at * step, joined(run))

        copies.append(pltpu.make_async_copy(done.at[index], out.at[meta[slots[index]]], sems.at[index]))
        copies[-1].start()
    for copy in copies:
        copy.wait()


def gate_kernel(*refs):
    pass


def first_open_row(total, raw):
    return (2 * raw - total) // 16 * 16


def raw_kernel(factor, arrays, wide, landing, leaving, slots, meta, *refs):
    own, other = strips_in(refs[:arrays]), strips_in(refs[arrays : 2 * arrays])
    queries, *refs = refs[2 * arrays :]
    landed = refs.pop(0) if landing else None
    leavers, refs = refs[: len(leaving)], refs[len(leaving) :]
    _, out, done, *refs = refs
    pair = refs.pop(0) if wide else None
    values, sums, sums_two, land_sems, sems = refs
    rows_n, cols_n, _ = own[0].shape
    count, width = done.shape[1] - rows_n * cols_n, done.shape[2]
    raw = rows_n * cols_n
    ones = (rows_n // 2) * (cols_n // 2)

    copies = []
    for index, slot in enumerate(landing):
        copies.append(pltpu.make_async_copy(landed.at[index], out.at[meta[slot]], land_sems.at[index]))
        copies[-1].start()
    total, cut = done.shape[1], first_open_row(done.shape[1], rows_n * cols_n)
    slots = list(slots)

    def leave(strip, whole):
        rows = pl.ds(0, total if whole else cut)
        number = len(copies) - len(landing)
        copies.append(pltpu.make_async_copy(strip.at[rows], out.at[meta[slots.pop(0)], rows], sems.at[number]))
        copies[-1].start()

    for strips, whole in zip(leavers, leaving):
        for index in range(strips.shape[0]):
            leave(strips.at[index], whole)

    def times(left):
        return jnp.dot(left, queries[...], preferred_element_type=jnp.float32) * factor

    def store(index, at, part):
        done[index, at : at + part.shape[0]] = part[:, :width].astype(done.dtype)
        if wide:
            pair[index, at : at + part.shape[0]] = part[:, width:].astype(done.dtype)

    for index, halves in enumerate(zip(own, other)):

        def raw_row(row):
            return jnp.concatenate([half[row] for half in halves], axis=1)

        @pl.when(meta[0] == 0)
        def _():
            for row in range(rows_n):
                store(index, row * cols_n, times(raw_row(row)))
            store(index, raw, jnp.zeros((count, values.shape[1]), jnp.float32))

        @pl.when(meta[0] != 0)
        def _():
            for row in range(count // cols_n, rows_n):
                values[row * cols_n : (row + 1) * cols_n] = times(raw_row(row))
            levels = [pooled_levels(half, sums, sums_two).astype(done.dtype) for half in halves]
            values[raw : raw + count] = times(jnp.concatenate(levels, axis=1))
            segments = [
                (values, count, raw),
                (values, raw, raw + ones),
                (values, raw, raw + ones),
                (values, raw + ones, raw + count),
                (values, raw + ones, raw + count),
            ]
            step = cols_n // 2
            for at, run in enumerate(chunks(segments, step)):
                store(index, at * step, joined(run))

        if slots:
            leave(done.at[index], False)
    for copy in copies:
        copy.wait()


def came_kernel(factor, arrays, wide, late, pins, slots, late_whole, meta, *refs):
    own, other = strips_in(refs[:arrays]), strips_in(refs[arrays : 2 * arrays])
    queries, *refs = refs[2 * arrays :]
    late_rows = refs.pop(0) if late else None
    refs = refs[2 + late + pins :]
    out, done, *refs = refs
    late_done = refs.pop(0) if late else None
    pair = refs.pop(0) if wide else None
    values, sems = refs
    count, width = own[0].shape[0], done.shape[2]
    raw = done.shape[1] - count
    ones = count * 4 // 5
    copies = []

    def leave(strip, whole=False):
        if slots:
            cut = 0 if whole else first_open_row(raw + count, raw)
            rows = pl.ds(cut, raw + count - cut)
            slot = meta[slots[len(copies)]]
            copies.append(pltpu.make_async_copy(strip.at[rows], out.at[slot, rows], sems.at[len(copies)]))
            copies[-1].start()

    def merge(strip, part):
        @pl.when(meta[0] == 0)
        def _():
            strip[raw : raw + count] = part.astype(done.dtype)

        @pl.when(meta[0] != 0)
        def _():
            values[...] = part
            at = raw - count
            for first, last, into in ((0, ones, at), (ones, count, at + 2 * ones)):
                start = into // 16 * 16
                end = -(-(into + last - first) // 16) * 16
                parts = [values[first:last]]
                if start < into:
                    parts.insert(0, strip[start : start + 16].astype(jnp.float32)[: into - start])
                over = end - (into + last - first)
                if over:
                    parts.append(strip[end - 16 : end].astype(jnp.float32)[16 - over :])
                strip[start:end] = jnp.concatenate(parts, axis=0).astype(done.dtype)

    if late:
        for index in range(late_done.shape[0]):
            merge(late_done.at[index], late_rows[index].astype(jnp.float32))
            leave(late_done.at[index], late_whole)
    for index, halves in enumerate(zip(own, other)):
        left = jnp.concatenate([half[...] for half in halves], axis=1)
        part = jnp.dot(left, queries[...], preferred_element_type=jnp.float32) * factor
        if wide:
            pair[index] = part[:, width:].astype(done.dtype)
        merge(done.at[index], part[:, :width])
        leave(done.at[index])
    for copy in copies:
        copy.wait()


def ring_local(frame_one, frame_two):
    rows_axis = lax.axis_size("rows")
    rows_n, cols_n, chans = frame_two.shape
    queries_n = frame_one.shape[0]
    half_rows = rows_n // 2
    raw = half_rows * cols_n
    count = (half_rows // 2) * (cols_n // 2) + (half_rows // 4) * (cols_n // 4)
    factor = float(1.0 / (2 * chans) ** 0.5)
    me, side = lax.axis_index("rows"), lax.axis_index("chan")

    chips = rows_axis // 2
    columns, half_way = chips // 2, chips // 2
    order = [2 * z for z in range(columns)] + [2 * z + 1 for z in reversed(range(columns))]
    ring = [(2 * order[p], 2 * order[(p + 1) % chips]) for p in range(chips)]
    ring += [(2 * order[p] + 1, 2 * order[p - 1] + 1) for p in range(chips)]
    swap = [(r, r ^ 1) for r in range(rows_axis)]
    across = [(0, 1), (1, 0)]

    core, column, line = me % 2, me // 4, (me // 2) % 2
    place = jnp.where(line == 0, column, chips - 1 - column)
    steps = jnp.arange(half_way + 1, dtype=jnp.int32)

    def strips_of(c):
        p = (place + jnp.where(c == 0, -steps, steps)) % chips
        chip = jnp.where(p < columns, 2 * p, 2 * (chips - 1 - p) + 1)
        return [2 * chip + c, 2 * chip + 1 - c]

    meta = jnp.concatenate([side[None], *strips_of(core), *strips_of(1 - core)]).astype(jnp.int32)

    def slots_of(d, other_core):
        first = 1 + (2 * other_core) * (half_way + 1) + d
        return (first,) if d in (0, half_way) else (first, first + half_way + 1)

    in_vmem = pl.BlockSpec(memory_space=pltpu.VMEM)
    anywhere = pl.BlockSpec(memory_space=pl.ANY)
    scalars = pl.BlockSpec(memory_space=pltpu.SMEM)
    out_type = jax.ShapeDtypeStruct((rows_axis, raw + count, queries_n), frame_two.dtype)
    pooling = [
        pltpu.VMEM((half_rows // 2, cols_n, chans), jnp.float32),
        pltpu.VMEM((half_rows // 4, cols_n // 2, chans), jnp.float32),
    ]
    params = pltpu.CompilerParams(vmem_limit_bytes=VMEM_BYTES)
    def modelled(us):
        return pl.CostEstimate(flops=int(us * 10**9) + 1000, bytes_accessed=1000, transcendentals=0)


    def make_extra(out, halves, cost=0, pins=(), flip=False, carry=False, passed=None):
        strips = sum(half.shape[0] for half in halves)
        handed = () if out is None else (out,)
        carried = tuple(halves) if carry else ()
        aliases = {1 + len(halves): 1} if handed else {}
        aliases.update({1 + index: 2 + index for index in range(len(carried))})
        if passed is not None:
            pins, carried = (passed, *pins), (passed,)
            aliases[1 + len(halves) + len(handed)] = 2
        return pl.pallas_call(
            functools.partial(extra_kernel, len(halves), 2 + len(carried), flip),
            out_shape=(jax.ShapeDtypeStruct((strips, count, chans), frame_two.dtype), out_type)
            + tuple(jax.ShapeDtypeStruct(half.shape, half.dtype) for half in carried),
            in_specs=[scalars] + [in_vmem] * len(halves) + [anywhere] * len(handed + pins),
            out_specs=(in_vmem, anywhere) + (in_vmem if carry else anywhere,) * len(carried),
            scratch_shapes=pooling,
            input_output_aliases=aliases,
            compiler_params=params,
            cost_estimate=modelled(cost),
            name="extra",
        )(meta, *halves, *handed, *pins)

    def correlate(out, slots, own, other, came_own, came_other, landing=(), landed=None, cost=0, pins=()):
        parts = (own, other, came_own, came_other)
        strips = sum(piece.shape[0] for piece in own)
        operands = [*own, *other, *came_own, *came_other, queries_wide]
        pair_type = jax.ShapeDtypeStruct((strips, raw + count, queries_n), frame_two.dtype)
        return pl.pallas_call(
            functools.partial(corr_kernel, factor, tuple(len(part) for part in parts), True, slots, landing, len(pins)),
            out_shape=(out_type, pair_type),
            in_specs=[scalars] + [in_vmem] * len(operands) + [anywhere] * (1 + bool(landing) + len(pins)),
            out_specs=(anywhere, in_vmem),
            scratch_shapes=[
                pltpu.VMEM((strips, raw + count, queries_n), frame_two.dtype),
                pltpu.VMEM((raw + 2 * count, 2 * queries_n), jnp.float32),
                *pooling,
                pltpu.SemaphoreType.DMA((strips,)),
                pltpu.SemaphoreType.DMA((max(1, len(landing)),)),
            ],
            input_output_aliases={1 + len(operands) + bool(landing): 0},
            compiler_params=params,
            cost_estimate=modelled(cost),
            name="correlate",
        )(meta, *operands, *([landed] if landing else []), out, *pins)

    def product_type(strips, pixels):
        return jax.ShapeDtypeStruct((strips, pixels, queries_n), frame_two.dtype)

    def raw_rows(out, own, other, wide, landing=(), landed=None, cost=0, leavers=(), leaving=(), slots=(), pins=()):
        operands = [*own, *other, queries_wide if wide else queries]
        strips = sum(half.shape[0] for half in own)
        passive = ([landed] if landing else []) + list(leavers)
        pins = tuple(pins)
        return pl.pallas_call(
            functools.partial(raw_kernel, factor, len(own), wide, landing, leaving, slots),
            out_shape=(out_type,) + (product_type(strips, raw + count),) * (1 + wide),
            in_specs=[scalars] + [in_vmem] * len(operands) + [anywhere] * (1 + len(passive)),
            out_specs=(anywhere,) + (in_vmem,) * (1 + wide),
            scratch_shapes=[
                pltpu.VMEM((raw + count, queries_n * (1 + wide)), jnp.float32),
                *pooling,
                pltpu.SemaphoreType.DMA((max(1, len(landing)),)),
                pltpu.SemaphoreType.DMA((max(1, len(slots)),)),
            ],
            input_output_aliases={1 + len(operands) + len(passive): 0},
            compiler_params=params,
            cost_estimate=modelled(cost),
            name="raw_rows",
        )(meta, *operands, *passive, out)

    def came_rows(out, done, slots, own, other, wide, late=(), cost=0, pins=()):
        operands = [*own, *other, queries_wide if wide else queries, *late[:1]]
        first = 1 + len(operands)
        inout = [out, done, *late[1:]]
        extra_types = (product_type(done.shape[0], count),) if wide else ()
        return pl.pallas_call(
            functools.partial(came_kernel, factor, len(own), wide, len(late) // 2, len(pins), slots, not G("NL")),
            out_shape=tuple(jax.ShapeDtypeStruct(array.shape, array.dtype) for array in inout) + extra_types,
            in_specs=[scalars] + [in_vmem] * len(operands) + [anywhere] + [in_vmem] * (len(inout) - 1) + [anywhere] * len(pins),
            out_specs=(anywhere,) + (in_vmem,) * (len(inout) - 1 + wide),
            scratch_shapes=[
                pltpu.VMEM((count, queries_n), jnp.float32),
                pltpu.SemaphoreType.DMA((max(1, len(slots)),)),
            ],
            input_output_aliases={first + index: index for index in range(len(inout))},
            compiler_params=params,
            cost_estimate=modelled(cost),
            name="came_rows",
        )(meta, *operands, *inout, *pins)

    def gate(out, pins, cost):
        handed = (out, *pins)
        return pl.pallas_call(
            gate_kernel,
            out_shape=tuple(jax.ShapeDtypeStruct(array.shape, array.dtype) for array in handed),
            in_specs=[anywhere] * len(handed),
            out_specs=(anywhere,) * len(handed),
            input_output_aliases={index: index for index in range(len(handed))},
            compiler_params=params,
            cost_estimate=modelled(cost),
            name="gate",
        )(*handed)

    mine = lax.dynamic_slice_in_dim(frame_two, side * half_rows, half_rows, axis=0)[None]
    theirs = lax.dynamic_slice_in_dim(frame_two, (1 - side) * half_rows, half_rows, axis=0)[None]
    if G("XQ"):
        sent = jnp.concatenate([theirs.reshape(raw, chans), frame_one], axis=0)
        got = lax.ppermute(sent, "chan", across)
        partner, queries_other = got[:raw].reshape(theirs.shape), got[raw:]
    else:
        partner = lax.ppermute(theirs, "chan", across)
        queries_other = lax.ppermute(frame_one, "chan", across)
    def all_queries(mine, theirs):
        own_core = jnp.concatenate([mine.T, theirs.T], axis=0)
        return own_core, jnp.concatenate([own_core, lax.ppermute(own_core, "rows", swap)], axis=1)

    if not G("QC"): queries, queries_wide = all_queries(frame_one, queries_other)

    def permute_rows(pairs, pieces):
        return [lax.ppermute(piece, "rows", pairs) for piece in pieces]

    def whole(pieces):
        return pieces if len(pieces) == 1 else [jnp.concatenate(pieces, axis=0)]

    came = {0: ([mine], [partner])}
    moving = [[half, *permute_rows(swap, [half])] for half in (mine, partner)]
    join = [G("JA"), G("JB")]
    for d in range(1, half_way + 1):
        if d == half_way:
            moving = [[pieces[0][:1]] for pieces in moving]
        if d == half_way - 1 and G("BSPL"):
            moving[1] = [moving[1][0][:1], moving[1][0][1:]]
        moving = [whole(pieces) if d == join[part] else pieces for part, pieces in enumerate(moving)]
        if d == 1:
            ring_first = moving[1][-1]
        moving = [permute_rows(ring, pieces) for pieces in moving]
        came[d] = tuple(moving)
    across_came = {}

    def do_extra(out, d, part, pin=None):
        pins = () if pin is None else tuple(across_came[pin]) if isinstance(pin, tuple) else (pin,)
        across_came[d, 1 - part] = []
        groups = [[piece] for piece in came[d][part]] if part and d == half_way - 1 else [came[d][part]]
        for pieces in groups:
            extra, out = make_extra(out, pieces, G(f"X{d}{part}"), pins)
            across_came[d, 1 - part].append(lax.ppermute(extra, "chan", across))
            pins = ()
        return out

    lag = G("LAG")
    waiting = []

    def landing(now):
        if waiting and waiting[0][0] <= now:
            return waiting.pop(0)[1:]
        return (), None

    def product(out, d, pins=()):
        out, pair = correlate(out, slots_of(d, 0), *came[d], across_came[d, 0], across_came[d, 1], *landing(d), G(f"C{d}"), pins)
        waiting.append((d + lag, slots_of(d, 1), permute_rows(swap, [pair])[0]))
        return out

    if G("QC"):
        extra, out, sent = make_extra(None, came[0][0], G("X00"), ({1: partner, 2: ring_first}[G("PINX")],) if G("PINX") else (), passed=frame_one)
        across_came[0, 1] = [lax.ppermute(extra, "chan", across)]
        queries, queries_wide = all_queries(frame_one, lax.ppermute(sent, "chan", across))
    else:
        out = do_extra(None, 0, 0, partner if G("PINX") else None)
    lacking, out = make_extra(out, [theirs], G("X01"), tuple(across_came[0, 1]) if G("PIN01") else (), flip=True)
    across_came[0, 0] = [lacking]
    if G("C0POS") == 0: out = product(out, 0)
    out = do_extra(out, 1, 0, (0, 1) if G("PIN0") else None)
    if G("C0POS") == 1: out = product(out, 0)
    out = do_extra(out, 1, 1, (1, 1))
    if G("C0POS") == 2: out = product(out, 0)
    for d in range(2, half_way):
        out = do_extra(out, d, 0, (d - 1, 0))
        out = product(out, d - 1)
        out = do_extra(out, d, 1, (d, 1))
    near, far = half_way - 1, half_way

    def swap_one(piece):
        return permute_rows(swap, [piece])[0]

    R3 = G("R3POS")
    def near_raw(out):
        return raw_rows(out, *came[near], True, *landing(near), G("F3"))

    swapped = []

    def far_extra(out, part, pins):
        extra, out, piece = make_extra(out, came[far][part], G(f"X4{part}"), pins, carry=True)
        came[far][part][0] = piece
        across_came[far, 1 - part] = [lax.ppermute(extra, "chan", across)]
        swapped.append(swap_one(piece))
        return out

    if R3 == 0: out, near_done, near_pair = near_raw(out)
    out = far_extra(out, 0, ())
    if R3 == 1: out, near_done, near_pair = near_raw(out)
    out = far_extra(out, 1, (swapped[0],) if G("PS0") == 1 else ())
    near_late = swap_one(near_pair)
    pins = (tuple(across_came[far, 1]) if G("PE4") == 1 else ()) + ((swapped[0],) if G("PS0") == 2 else ())

    slots = slots_of(near, 1) + slots_of(far, 0) + slots_of(far, 1)

    out, near_done, near_rows = came_rows(out, near_done, (), across_came[near, 0], across_came[near, 1], True, cost=G("F2"), pins=pins)
    near_rows = swap_one(near_rows)
    out, far_done = raw_rows(
        out,
        [came[far][0][0], swapped[0]],
        [came[far][1][0], swapped[1]],
        False,
        *landing(far),
        G("F0"),
        (near_done, near_late) if G("NL") else (near_done,),
        (True, False)[: 1 + G("NL")],
        slots_of(near, 0) + (slots if G("NL") else slots[len(slots_of(near, 1)) :]),
    )
    out, own, other = gate(out, [across_came[far, 0][0], across_came[far, 1][0]], G("GATE"))
    return came_rows(out, far_done, slots, [own, swap_one(own)], [other, swap_one(other)], False, (near_rows, near_late), G("F1"))[0]


def solution(mesh):
    rows_axis, groups = mesh.shape["rows"], mesh.shape["chan"]

    def local(frame_one, frame_two):
        rows_n, cols_n, chans = frame_two.shape
        ring = groups == 2 and rows_axis % 8 == 0 and rows_axis >= 16 and rows_n % 8 == 0 and cols_n % 32 == 0 and chans % LANES == 0
        return (ring_local if ring else gather_local)(frame_one, frame_two)

    in_specs = (P("rows", "chan"), P("rows", None, "chan"))
    out_specs = P(None, "chan", "rows")
    return jax.shard_map(local, mesh=mesh, in_specs=in_specs, out_specs=out_specs, check_vma=False)
```

```python
import functools

import jax
import jax.numpy as jnp
from jax import lax
from jax.experimental import pallas as pl
from jax.experimental.pallas import tpu as pltpu
from jax.sharding import PartitionSpec as P

LANES = 128
PARAMS = {'LAG': 2, 'F0': 10, 'F1': 0, 'PS0': 2, 'JA': 1, 'JB': 1, 'C0POS': 2, 'R3POS': 0, 'GATE': 30, 'F3': 10, 'F2': 10, 'PE4': 1, 'X00': 10, 'X01': 10, 'C0': 10, 'X10': 10, 'X11': 10, 'C1': 10, 'X20': 10, 'X21': 10, 'C2': 10, 'X30': 10, 'X31': 10, 'C3': 10, 'X40': 10, 'X41': 10, 'C4': 10, 'NL': 0}


def G(name):
    return PARAMS.get(name, 0)


VMEM_BYTES = 28 * 1024 * 1024


def pool_strip(strip):
    full = strip.astype(jnp.float32)
    rows_n, cols_n, chans = full.shape
    level_one = full.reshape(rows_n // 2, 2, cols_n // 2, 2, chans).mean(axis=(1, 3))
    level_two = level_one.reshape(rows_n // 4, 2, cols_n // 4, 2, chans).mean(axis=(1, 3))
    joined = jnp.concatenate(
        [full.reshape(-1, chans), level_one.reshape(-1, chans), level_two.reshape(-1, chans)],
        axis=0,
    )
    return joined.astype(jnp.bfloat16)


def gather_local(frame_one, frame_two):
    groups = lax.axis_size("chan")
    queries = lax.all_gather(frame_one, "chan", axis=0, tiled=False)
    channels = queries.shape[0] * queries.shape[2]
    factor = 1.0 / jnp.sqrt(jnp.float32(channels))
    pooled = pool_strip(frame_two)
    share = pooled.shape[0] // groups
    traded = lax.all_to_all(
        pooled.reshape(groups, share, pooled.shape[1]), "chan", split_axis=0, concat_axis=0, tiled=True
    )
    gathered = lax.all_gather(traded, "rows", axis=0, tiled=False)
    values = jnp.einsum("skpc,kqc->spq", gathered, queries, preferred_element_type=jnp.float32)
    return (values * factor).astype(jnp.bfloat16)


def pooled_levels(half, sums, sums_two):
    rows_n, cols_n, _ = half.shape
    means = []
    for row in range(rows_n // 2):
        sums[row] = half[2 * row].astype(jnp.float32) + half[2 * row + 1].astype(jnp.float32)
        left = sums[row, pl.ds(0, cols_n // 2, stride=2), :]
        right = sums[row, pl.ds(1, cols_n // 2, stride=2), :]
        means.append((left + right) * 0.25)
    means_two = []
    for row in range(rows_n // 4):
        sums_two[row] = means[2 * row] + means[2 * row + 1]
        left = sums_two[row, pl.ds(0, cols_n // 4, stride=2), :]
        right = sums_two[row, pl.ds(1, cols_n // 4, stride=2), :]
        means_two.append((left + right) * 0.25)
    return jnp.concatenate(means + means_two, axis=0)


def strips_in(refs):
    return [ref.at[index] for ref in refs for index in range(ref.shape[0])]


def extra_kernel(pieces, results, flip, meta, *refs):
    halves = strips_in(refs[:pieces])
    extra, sums, sums_two = refs[-2 - results], *refs[-2:]
    count, cols_n = extra.shape[1], halves[0].shape[1]
    upper = meta[0] == (1 if flip else 0)

    @pl.when(upper)
    def _():
        for index, half in enumerate(halves):
            extra[index] = pooled_levels(half, sums, sums_two).astype(extra.dtype)

    @pl.when(jnp.logical_not(upper))
    def _():
        for index, half in enumerate(halves):
            parts, left, row = [], count, 0
            while left > 0:
                parts.append(half[row].astype(jnp.float32)[: min(left, cols_n)])
                left, row = left - cols_n, row + 1
            extra[index] = jnp.concatenate(parts, axis=0).astype(extra.dtype)


def chunks(segments, step):
    todo, runs = list(segments), []
    while todo:
        run, room = [], step
        while todo and room > 0:
            ref, first, last = todo.pop(0)
            take = min(room, last - first)
            run.append((ref, first, first + take))
            room -= take
            if first + take < last:
                todo.insert(0, (ref, first + take, last))
        runs.append(run)
    return runs


def joined(run):
    parts = [ref[first:last].astype(jnp.float32) for ref, first, last in run]
    return parts[0] if len(parts) == 1 else jnp.concatenate(parts, axis=0)


def corr_kernel(factor, pieces, wide, slots, landing, pins, meta, *refs):
    own, other = strips_in(refs[: pieces[0]]), strips_in(refs[pieces[0] : sum(pieces[:2])])
    refs = refs[sum(pieces[:2]) :]
    came_own, came_other = strips_in(refs[: pieces[2]]), strips_in(refs[pieces[2] : pieces[2] + pieces[3]])
    queries, *refs = refs[pieces[2] + pieces[3] :]
    landed = refs.pop(0) if landing else None
    out, *refs = refs[1 + pins :]
    pair = refs.pop(0) if wide else None
    done, values, sums, sums_two, sems, land_sems = refs
    rows_n, cols_n, _ = own[0].shape
    count, width = came_own[0].shape[0], done.shape[2]
    raw = rows_n * cols_n
    ones = (rows_n // 2) * (cols_n // 2)

    copies = []
    for index, slot in enumerate(landing):
        copies.append(pltpu.make_async_copy(landed.at[index], out.at[meta[slot]], land_sems.at[index]))
        copies[-1].start()

    def times(left):
        return jnp.dot(left, queries[...], preferred_element_type=jnp.float32) * factor

    def store(index, at, part):
        done[index, at : at + part.shape[0]] = part[:, :width].astype(done.dtype)
        if wide:
            pair[index, at : at + part.shape[0]] = part[:, width:].astype(done.dtype)

    for index in range(len(own)):

        def raw_row(row):
            return jnp.concatenate([own[index][row], other[index][row]], axis=1)

        def came_rows():
            return jnp.concatenate([came_own[index][...], came_other[index][...]], axis=1)

        @pl.when(meta[0] == 0)
        def _():
            for row in range(rows_n):
                store(index, row * cols_n, times(raw_row(row)))
            store(index, raw, times(came_rows()))

        @pl.when(meta[0] != 0)
        def _():
            for row in range(count // cols_n, rows_n):
                values[row * cols_n : (row + 1) * cols_n] = times(raw_row(row))
            values[raw : raw + count] = times(came_rows())
            levels = [pooled_levels(half[index], sums, sums_two).astype(done.dtype) for half in (own, other)]
            lower = raw + count
            values[lower : lower + count] = times(jnp.concatenate(levels, axis=1))
            segments = [
                (values, count, raw),
                (values, raw, raw + ones),
                (values, lower, lower + ones),
                (values, raw + ones, raw + count),
                (values, lower + ones, lower + count),
            ]
            step = cols_n // 2
            for at, run in enumerate(chunks(segments, step)):
                store(index, at * step, joined(run))

        copies.append(pltpu.make_async_copy(done.at[index], out.at[meta[slots[index]]], sems.at[index]))
        copies[-1].start()
    for copy in copies:
        copy.wait()


def gate_kernel(*refs):
    pass


def first_open_row(total, raw):
    return (2 * raw - total) // 16 * 16


def raw_kernel(factor, arrays, wide, landing, leaving, slots, meta, *refs):
    own, other = strips_in(refs[:arrays]), strips_in(refs[arrays : 2 * arrays])
    queries, *refs = refs[2 * arrays :]
    landed = refs.pop(0) if landing else None
    leavers, refs = refs[: len(leaving)], refs[len(leaving) :]
    _, out, done, *refs = refs
    pair = refs.pop(0) if wide else None
    values, sums, sums_two, land_sems, sems = refs
    rows_n, cols_n, _ = own[0].shape
    count, width = done.shape[1] - rows_n * cols_n, done.shape[2]
    raw = rows_n * cols_n
    ones = (rows_n // 2) * (cols_n // 2)

    copies = []
    for index, slot in enumerate(landing):
        copies.append(pltpu.make_async_copy(landed.at[index], out.at[meta[slot]], land_sems.at[index]))
        copies[-1].start()
    total, cut = done.shape[1], first_open_row(done.shape[1], rows_n * cols_n)
    slots = list(slots)

    def leave(strip, whole):
        rows = pl.ds(0, total if whole else cut)
        number = len(copies) - len(landing)
        copies.append(pltpu.make_async_copy(strip.at[rows], out.at[meta[slots.pop(0)], rows], sems.at[number]))
        copies[-1].start()

    for strips, whole in zip(leavers, leaving):
        for index in range(strips.shape[0]):
            leave(strips.at[index], whole)

    def times(left):
        return jnp.dot(left, queries[...], preferred_element_type=jnp.float32) * factor

    def store(index, at, part):
        done[index, at : at + part.shape[0]] = part[:, :width].astype(done.dtype)
        if wide:
            pair[index, at : at + part.shape[0]] = part[:, width:].astype(done.dtype)

    for index, halves in enumerate(zip(own, other)):

        def raw_row(row):
            return jnp.concatenate([half[row] for half in halves], axis=1)

        @pl.when(meta[0] == 0)
        def _():
            for row in range(rows_n):
                store(index, row * cols_n, times(raw_row(row)))
            store(index, raw, jnp.zeros((count, values.shape[1]), jnp.float32))

        @pl.when(meta[0] != 0)
        def _():
            for row in range(count // cols_n, rows_n):
                values[row * cols_n : (row + 1) * cols_n] = times(raw_row(row))
            levels = [pooled_levels(half, sums, sums_two).astype(done.dtype) for half in halves]
            values[raw : raw + count] = times(jnp.concatenate(levels, axis=1))
            segments = [
                (values, count, raw),
                (values, raw, raw + ones),
                (values, raw, raw + ones),
                (values, raw + ones, raw + count),
                (values, raw + ones, raw + count),
            ]
            step = cols_n // 2
            for at, run in enumerate(chunks(segments, step)):
                store(index, at * step, joined(run))

        if slots:
            leave(done.at[index], False)
    for copy in copies:
        copy.wait()


def came_kernel(factor, arrays, wide, late, pins, slots, late_whole, meta, *refs):
    own, other = strips_in(refs[:arrays]), strips_in(refs[arrays : 2 * arrays])
    queries, *refs = refs[2 * arrays :]
    late_rows = refs.pop(0) if late else None
    refs = refs[2 + late + pins :]
    out, done, *refs = refs
    late_done = refs.pop(0) if late else None
    pair = refs.pop(0) if wide else None
    values, sems = refs
    count, width = own[0].shape[0], done.shape[2]
    raw = done.shape[1] - count
    ones = count * 4 // 5
    copies = []

    def leave(strip, whole=False):
        if slots:
            cut = 0 if whole else first_open_row(raw + count, raw)
            rows = pl.ds(cut, raw + count - cut)
            slot = meta[slots[len(copies)]]
            copies.append(pltpu.make_async_copy(strip.at[rows], out.at[slot, rows], sems.at[len(copies)]))
            copies[-1].start()

    def merge(strip, part):
        @pl.when(meta[0] == 0)
        def _():
            strip[raw : raw + count] = part.astype(done.dtype)

        @pl.when(meta[0] != 0)
        def _():
            values[...] = part
            at = raw - count
            for first, last, into in ((0, ones, at), (ones, count, at + 2 * ones)):
                start = into // 16 * 16
                end = -(-(into + last - first) // 16) * 16
                parts = [values[first:last]]
                if start < into:
                    parts.insert(0, strip[start : start + 16].astype(jnp.float32)[: into - start])
                over = end - (into + last - first)
                if over:
                    parts.append(strip[end - 16 : end].astype(jnp.float32)[16 - over :])
                strip[start:end] = jnp.concatenate(parts, axis=0).astype(done.dtype)

    if late:
        for index in range(late_done.shape[0]):
            merge(late_done.at[index], late_rows[index].astype(jnp.float32))
            leave(late_done.at[index], late_whole)
    for index, halves in enumerate(zip(own, other)):
        left = jnp.concatenate([half[...] for half in halves], axis=1)
        part = jnp.dot(left, queries[...], preferred_element_type=jnp.float32) * factor
        if wide:
            pair[index] = part[:, width:].astype(done.dtype)
        merge(done.at[index], part[:, :width])
        leave(done.at[index])
    for copy in copies:
        copy.wait()


def ring_local(frame_one, frame_two):
    rows_axis = lax.axis_size("rows")
    rows_n, cols_n, chans = frame_two.shape
    queries_n = frame_one.shape[0]
    half_rows = rows_n // 2
    raw = half_rows * cols_n
    count = (half_rows // 2) * (cols_n // 2) + (half_rows // 4) * (cols_n // 4)
    factor = float(1.0 / (2 * chans) ** 0.5)
    me, side = lax.axis_index("rows"), lax.axis_index("chan")

    chips = rows_axis // 2
    columns, half_way = chips // 2, chips // 2
    order = [2 * z for z in range(columns)] + [2 * z + 1 for z in reversed(range(columns))]
    ring = [(2 * order[p], 2 * order[(p + 1) % chips]) for p in range(chips)]
    ring += [(2 * order[p] + 1, 2 * order[p - 1] + 1) for p in range(chips)]
    swap = [(r, r ^ 1) for r in range(rows_axis)]
    across = [(0, 1), (1, 0)]

    core, column, line = me % 2, me // 4, (me // 2) % 2
    place = jnp.where(line == 0, column, chips - 1 - column)
    steps = jnp.arange(half_way + 1, dtype=jnp.int32)

    def strips_of(c):
        p = (place + jnp.where(c == 0, -steps, steps)) % chips
        chip = jnp.where(p < columns, 2 * p, 2 * (chips - 1 - p) + 1)
        return [2 * chip + c, 2 * chip + 1 - c]

    meta = jnp.concatenate([side[None], *strips_of(core), *strips_of(1 - core)]).astype(jnp.int32)

    def slots_of(d, other_core):
        first = 1 + (2 * other_core) * (half_way + 1) + d
        return (first,) if d in (0, half_way) else (first, first + half_way + 1)

    in_vmem = pl.BlockSpec(memory_space=pltpu.VMEM)
    anywhere = pl.BlockSpec(memory_space=pl.ANY)
    scalars = pl.BlockSpec(memory_space=pltpu.SMEM)
    out_type = jax.ShapeDtypeStruct((rows_axis, raw + count, queries_n), frame_two.dtype)
    pooling = [
        pltpu.VMEM((half_rows // 2, cols_n, chans), jnp.float32),
        pltpu.VMEM((half_rows // 4, cols_n // 2, chans), jnp.float32),
    ]
    params = pltpu.CompilerParams(vmem_limit_bytes=VMEM_BYTES)
    def modelled(us):
        return pl.CostEstimate(flops=int(us * 10**9) + 1000, bytes_accessed=1000, transcendentals=0)


    def make_extra(out, halves, cost=0, pins=(), flip=False, carry=False, passed=None):
        strips = sum(half.shape[0] for half in halves)
        handed = () if out is None else (out,)
        carried = tuple(halves) if carry else ()
        aliases = {1 + len(halves): 1} if handed else {}
        aliases.update({1 + index: 2 + index for index in range(len(carried))})
        if passed is not None:
            pins, carried = (passed, *pins), (passed,)
            aliases[1 + len(halves) + len(handed)] = 2
        return pl.pallas_call(
            functools.partial(extra_kernel, len(halves), 2 + len(carried), flip),
            out_shape=(jax.ShapeDtypeStruct((strips, count, chans), frame_two.dtype), out_type)
            + tuple(jax.ShapeDtypeStruct(half.shape, half.dtype) for half in carried),
            in_specs=[scalars] + [in_vmem] * len(halves) + [anywhere] * len(handed + pins),
            out_specs=(in_vmem, anywhere) + (in_vmem if carry else anywhere,) * len(carried),
            scratch_shapes=pooling,
            input_output_aliases=aliases,
            compiler_params=params,
            cost_estimate=modelled(cost),
            name="extra",
        )(meta, *halves, *handed, *pins)

    def correlate(out, slots, own, other, came_own, came_other, landing=(), landed=None, cost=0, pins=()):
        parts = (own, other, came_own, came_other)
        strips = sum(piece.shape[0] for piece in own)
        operands = [*own, *other, *came_own, *came_other, queries_wide]
        pair_type = jax.ShapeDtypeStruct((strips, raw + count, queries_n), frame_two.dtype)
        return pl.pallas_call(
            functools.partial(corr_kernel, factor, tuple(len(part) for part in parts), True, slots, landing, len(pins)),
            out_shape=(out_type, pair_type),
            in_specs=[scalars] + [in_vmem] * len(operands) + [anywhere] * (1 + bool(landing) + len(pins)),
            out_specs=(anywhere, in_vmem),
            scratch_shapes=[
                pltpu.VMEM((strips, raw + count, queries_n), frame_two.dtype),
                pltpu.VMEM((raw + 2 * count, 2 * queries_n), jnp.float32),
                *pooling,
                pltpu.SemaphoreType.DMA((strips,)),
                pltpu.SemaphoreType.DMA((max(1, len(landing)),)),
            ],
            input_output_aliases={1 + len(operands) + bool(landing): 0},
            compiler_params=params,
            cost_estimate=modelled(cost),
            name="correlate",
        )(meta, *operands, *([landed] if landing else []), out, *pins)

    def product_type(strips, pixels):
        return jax.ShapeDtypeStruct((strips, pixels, queries_n), frame_two.dtype)

    def raw_rows(out, own, other, wide, landing=(), landed=None, cost=0, leavers=(), leaving=(), slots=(), pins=()):
        operands = [*own, *other, queries_wide if wide else queries]
        strips = sum(half.shape[0] for half in own)
        passive = ([landed] if landing else []) + list(leavers)
        pins = tuple(pins)
        return pl.pallas_call(
            functools.partial(raw_kernel, factor, len(own), wide, landing, leaving, slots),
            out_shape=(out_type,) + (product_type(strips, raw + count),) * (1 + wide),
            in_specs=[scalars] + [in_vmem] * len(operands) + [anywhere] * (1 + len(passive)),
            out_specs=(anywhere,) + (in_vmem,) * (1 + wide),
            scratch_shapes=[
                pltpu.VMEM((raw + count, queries_n * (1 + wide)), jnp.float32),
                *pooling,
                pltpu.SemaphoreType.DMA((max(1, len(landing)),)),
                pltpu.SemaphoreType.DMA((max(1, len(slots)),)),
            ],
            input_output_aliases={1 + len(operands) + len(passive): 0},
            compiler_params=params,
            cost_estimate=modelled(cost),
            name="raw_rows",
        )(meta, *operands, *passive, out)

    def came_rows(out, done, slots, own, other, wide, late=(), cost=0, pins=()):
        operands = [*own, *other, queries_wide if wide else queries, *late[:1]]
        first = 1 + len(operands)
        inout = [out, done, *late[1:]]
        extra_types = (product_type(done.shape[0], count),) if wide else ()
        return pl.pallas_call(
            functools.partial(came_kernel, factor, len(own), wide, len(late) // 2, len(pins), slots, not G("NL")),
            out_shape=tuple(jax.ShapeDtypeStruct(array.shape, array.dtype) for array in inout) + extra_types,
            in_specs=[scalars] + [in_vmem] * len(operands) + [anywhere] + [in_vmem] * (len(inout) - 1) + [anywhere] * len(pins),
            out_specs=(anywhere,) + (in_vmem,) * (len(inout) - 1 + wide),
            scratch_shapes=[
                pltpu.VMEM((count, queries_n), jnp.float32),
                pltpu.SemaphoreType.DMA((max(1, len(slots)),)),
            ],
            input_output_aliases={first + index: index for index in range(len(inout))},
            compiler_params=params,
            cost_estimate=modelled(cost),
            name="came_rows",
        )(meta, *operands, *inout, *pins)

    def gate(out, pins, cost):
        handed = (out, *pins)
        return pl.pallas_call(
            gate_kernel,
            out_shape=tuple(jax.ShapeDtypeStruct(array.shape, array.dtype) for array in handed),
            in_specs=[anywhere] * len(handed),
            out_specs=(anywhere,) * len(handed),
            input_output_aliases={index: index for index in range(len(handed))},
            compiler_params=params,
            cost_estimate=modelled(cost),
            name="gate",
        )(*handed)

    mine = lax.dynamic_slice_in_dim(frame_two, side * half_rows, half_rows, axis=0)[None]
    theirs = lax.dynamic_slice_in_dim(frame_two, (1 - side) * half_rows, half_rows, axis=0)[None]
    if G("XQ"):
        sent = jnp.concatenate([theirs.reshape(raw, chans), frame_one], axis=0)
        got = lax.ppermute(sent, "chan", across)
        partner, queries_other = got[:raw].reshape(theirs.shape), got[raw:]
    else:
        partner = lax.ppermute(theirs, "chan", across)
        queries_other = lax.ppermute(frame_one, "chan", across)
    def all_queries(mine, theirs):
        own_core = jnp.concatenate([mine.T, theirs.T], axis=0)
        return own_core, jnp.concatenate([own_core, lax.ppermute(own_core, "rows", swap)], axis=1)

    if not G("QC"): queries, queries_wide = all_queries(frame_one, queries_other)

    def permute_rows(pairs, pieces):
        return [lax.ppermute(piece, "rows", pairs) for piece in pieces]

    def whole(pieces):
        return pieces if len(pieces) == 1 else [jnp.concatenate(pieces, axis=0)]

    came = {0: ([mine], [partner])}
    moving = [[half, *permute_rows(swap, [half])] for half in (mine, partner)]
    join = [G("JA"), G("JB")]
    for d in range(1, half_way + 1):
        if d == half_way:
            moving = [[pieces[0][:1]] for pieces in moving]
        if d == half_way - 1 and G("BSPL"):
            moving[1] = [moving[1][0][:1], moving[1][0][1:]]
        moving = [whole(pieces) if d == join[part] else pieces for part, pieces in enumerate(moving)]
        if d == 1:
            ring_first = moving[1][-1]
        moving = [permute_rows(ring, pieces) for pieces in moving]
        came[d] = tuple(moving)
    across_came = {}

    def do_extra(out, d, part, pin=None):
        pins = () if pin is None else tuple(across_came[pin]) if isinstance(pin, tuple) else (pin,)
        across_came[d, 1 - part] = []
        groups = [[piece] for piece in came[d][part]] if part and d == half_way - 1 else [came[d][part]]
        for pieces in groups:
            extra, out = make_extra(out, pieces, G(f"X{d}{part}"), pins)
            across_came[d, 1 - part].append(lax.ppermute(extra, "chan", across))
            pins = ()
        return out

    lag = G("LAG")
    waiting = []

    def landing(now):
        if waiting and waiting[0][0] <= now:
            return waiting.pop(0)[1:]
        return (), None

    def product(out, d, pins=()):
        out, pair = correlate(out, slots_of(d, 0), *came[d], across_came[d, 0], across_came[d, 1], *landing(d), G(f"C{d}"), pins)
        waiting.append((d + lag, slots_of(d, 1), permute_rows(swap, [pair])[0]))
        return out

    if G("QC"):
        extra, out, sent = make_extra(None, came[0][0], G("X00"), ({1: partner, 2: ring_first}[G("PINX")],) if G("PINX") else (), passed=frame_one)
        across_came[0, 1] = [lax.ppermute(extra, "chan", across)]
        queries, queries_wide = all_queries(frame_one, lax.ppermute(sent, "chan", across))
    else:
        out = do_extra(None, 0, 0, partner if G("PINX") else None)
    lacking, out = make_extra(out, [theirs], G("X01"), tuple(across_came[0, 1]) if G("PIN01") else (), flip=True)
    across_came[0, 0] = [lacking]
    if G("C0POS") == 0: out = product(out, 0)
    out = do_extra(out, 1, 0, (0, 1) if G("PIN0") else None)
    if G("C0POS") == 1: out = product(out, 0)
    out = do_extra(out, 1, 1, (1, 1))
    if G("C0POS") == 2: out = product(out, 0)
    for d in range(2, half_way):
        out = do_extra(out, d, 0, (d - 1, 0))
        out = product(out, d - 1)
        out = do_extra(out, d, 1, (d, 1))
    near, far = half_way - 1, half_way

    def swap_one(piece):
        return permute_rows(swap, [piece])[0]

    R3 = G("R3POS")
    def near_raw(out):
        return raw_rows(out, *came[near], True, *landing(near), G("F3"))

    swapped = []

    def far_extra(out, part, pins):
        extra, out, piece = make_extra(out, came[far][part], G(f"X4{part}"), pins, carry=True)
        came[far][part][0] = piece
        across_came[far, 1 - part] = [lax.ppermute(extra, "chan", across)]
        swapped.append(swap_one(piece))
        return out

    if R3 == 0: out, near_done, near_pair = near_raw(out)
    out = far_extra(out, 0, ())
    if R3 == 1: out, near_done, near_pair = near_raw(out)
    out = far_extra(out, 1, (swapped[0],) if G("PS0") == 1 else ())
    near_late = swap_one(near_pair)
    pins = (tuple(across_came[far, 1]) if G("PE4") == 1 else ()) + ((swapped[0],) if G("PS0") == 2 else ())

    slots = slots_of(near, 1) + slots_of(far, 0) + slots_of(far, 1)

    out, near_done, near_rows = came_rows(out, near_done, (), across_came[near, 0], across_came[near, 1], True, cost=G("F2"), pins=pins)
    near_rows = swap_one(near_rows)
    out, far_done = raw_rows(
        out,
        [came[far][0][0], swapped[0]],
        [came[far][1][0], swapped[1]],
        False,
        *landing(far),
        G("F0"),
        (near_done, near_late) if G("NL") else (near_done,),
        (True, False)[: 1 + G("NL")],
        slots_of(near, 0) + (slots if G("NL") else slots[len(slots_of(near, 1)) :]),
    )
    out, own, other = gate(out, [across_came[far, 0][0], across_came[far, 1][0]], G("GATE"))
    return came_rows(out, far_done, slots, [own, swap_one(own)], [other, swap_one(other)], False, (near_rows, near_late), G("F1"))[0]


def solution(mesh):
    rows_axis, groups = mesh.shape["rows"], mesh.shape["chan"]

    def local(frame_one, frame_two):
        rows_n, cols_n, chans = frame_two.shape
        ring = groups == 2 and rows_axis % 8 == 0 and rows_axis >= 16 and rows_n % 8 == 0 and cols_n % 32 == 0 and chans % LANES == 0
        return (ring_local if ring else gather_local)(frame_one, frame_two)

    in_specs = (P("rows", "chan"), P("rows", None, "chan"))
    out_specs = P(None, "chan", "rows")
    return jax.shard_map(local, mesh=mesh, in_specs=in_specs, out_specs=out_specs, check_vma=False)
```

```python
import functools

import jax
import jax.numpy as jnp
from jax import lax
from jax.experimental import pallas as pl
from jax.experimental.pallas import tpu as pltpu
from jax.sharding import PartitionSpec as P

LANES = 128
PARAMS = {'LAG': 2, 'F0': 10, 'F1': 0, 'PS0': 2, 'JA': 3, 'JB': 1, 'C0POS': 1, 'R3POS': 0, 'GATE': 30, 'F3': 10, 'F2': 10, 'NL': 0, 'PE4': 1, 'C2POS': 1, 'X00': 10, 'X01': 10, 'C0': 10, 'X10': 10, 'X11': 10, 'C1': 10, 'X20': 10, 'X21': 10, 'C2': 10, 'X30': 10, 'X31': 10, 'C3': 10, 'X40': 10, 'X41': 10, 'C4': 10}


def G(name):
    return PARAMS.get(name, 0)


VMEM_BYTES = 28 * 1024 * 1024


def pool_strip(strip):
    full = strip.astype(jnp.float32)
    rows_n, cols_n, chans = full.shape
    level_one = full.reshape(rows_n // 2, 2, cols_n // 2, 2, chans).mean(axis=(1, 3))
    level_two = level_one.reshape(rows_n // 4, 2, cols_n // 4, 2, chans).mean(axis=(1, 3))
    joined = jnp.concatenate(
        [full.reshape(-1, chans), level_one.reshape(-1, chans), level_two.reshape(-1, chans)],
        axis=0,
    )
    return joined.astype(jnp.bfloat16)


def gather_local(frame_one, frame_two):
    groups = lax.axis_size("chan")
    queries = lax.all_gather(frame_one, "chan", axis=0, tiled=False)
    channels = queries.shape[0] * queries.shape[2]
    factor = 1.0 / jnp.sqrt(jnp.float32(channels))
    pooled = pool_strip(frame_two)
    share = pooled.shape[0] // groups
    traded = lax.all_to_all(
        pooled.reshape(groups, share, pooled.shape[1]), "chan", split_axis=0, concat_axis=0, tiled=True
    )
    gathered = lax.all_gather(traded, "rows", axis=0, tiled=False)
    values = jnp.einsum("skpc,kqc->spq", gathered, queries, preferred_element_type=jnp.float32)
    return (values * factor).astype(jnp.bfloat16)


def pooled_levels(half, sums, sums_two):
    rows_n, cols_n, _ = half.shape
    means = []
    for row in range(rows_n // 2):
        sums[row] = half[2 * row].astype(jnp.float32) + half[2 * row + 1].astype(jnp.float32)
        left = sums[row, pl.ds(0, cols_n // 2, stride=2), :]
        right = sums[row, pl.ds(1, cols_n // 2, stride=2), :]
        means.append((left + right) * 0.25)
    means_two = []
    for row in range(rows_n // 4):
        sums_two[row] = means[2 * row] + means[2 * row + 1]
        left = sums_two[row, pl.ds(0, cols_n // 4, stride=2), :]
        right = sums_two[row, pl.ds(1, cols_n // 4, stride=2), :]
        means_two.append((left + right) * 0.25)
    return jnp.concatenate(means + means_two, axis=0)


def strips_in(refs):
    return [ref.at[index] for ref in refs for index in range(ref.shape[0])]


def extra_kernel(pieces, results, flip, meta, *refs):
    halves = strips_in(refs[:pieces])
    extra, sums, sums_two = refs[-2 - results], *refs[-2:]
    count, cols_n = extra.shape[1], halves[0].shape[1]
    upper = meta[0] == (1 if flip else 0)

    @pl.when(upper)
    def _():
        for index, half in enumerate(halves):
            extra[index] = pooled_levels(half, sums, sums_two).astype(extra.dtype)

    @pl.when(jnp.logical_not(upper))
    def _():
        for index, half in enumerate(halves):
            parts, left, row = [], count, 0
            while left > 0:
                parts.append(half[row].astype(jnp.float32)[: min(left, cols_n)])
                left, row = left - cols_n, row + 1
            extra[index] = jnp.concatenate(parts, axis=0).astype(extra.dtype)


def chunks(segments, step):
    todo, runs = list(segments), []
    while todo:
        run, room = [], step
        while todo and room > 0:
            ref, first, last = todo.pop(0)
            take = min(room, last - first)
            run.append((ref, first, first + take))
            room -= take
            if first + take < last:
                todo.insert(0, (ref, first + take, last))
        runs.append(run)
    return runs


def joined(run):
    parts = [ref[first:last].astype(jnp.float32) for ref, first, last in run]
    return parts[0] if len(parts) == 1 else jnp.concatenate(parts, axis=0)


def corr_kernel(factor, pieces, wide, slots, landing, pins, meta, *refs):
    own, other = strips_in(refs[: pieces[0]]), strips_in(refs[pieces[0] : sum(pieces[:2])])
    refs = refs[sum(pieces[:2]) :]
    came_own, came_other = strips_in(refs[: pieces[2]]), strips_in(refs[pieces[2] : pieces[2] + pieces[3]])
    queries, *refs = refs[pieces[2] + pieces[3] :]
    landed = refs.pop(0) if landing else None
    out, *refs = refs[1 + pins :]
    pair = refs.pop(0) if wide else None
    done, values, sums, sums_two, sems, land_sems = refs
    rows_n, cols_n, _ = own[0].shape
    count, width = came_own[0].shape[0], done.shape[2]
    raw = rows_n * cols_n
    ones = (rows_n // 2) * (cols_n // 2)

    copies = []
    for index, slot in enumerate(landing):
        copies.append(pltpu.make_async_copy(landed.at[index], out.at[meta[slot]], land_sems.at[index]))
        copies[-1].start()

    def times(left):
        return jnp.dot(left, queries[...], preferred_element_type=jnp.float32) * factor

    def store(index, at, part):
        done[index, at : at + part.shape[0]] = part[:, :width].astype(done.dtype)
        if wide:
            pair[index, at : at + part.shape[0]] = part[:, width:].astype(done.dtype)

    for index in range(len(own)):

        def raw_row(row):
            return jnp.concatenate([own[index][row], other[index][row]], axis=1)

        def came_rows():
            return jnp.concatenate([came_own[index][...], came_other[index][...]], axis=1)

        @pl.when(meta[0] == 0)
        def _():
            for row in range(rows_n):
                store(index, row * cols_n, times(raw_row(row)))
            store(index, raw, times(came_rows()))

        @pl.when(meta[0] != 0)
        def _():
            for row in range(count // cols_n, rows_n):
                values[row * cols_n : (row + 1) * cols_n] = times(raw_row(row))
            values[raw : raw + count] = times(came_rows())
            levels = [pooled_levels(half[index], sums, sums_two).astype(done.dtype) for half in (own, other)]
            lower = raw + count
            values[lower : lower + count] = times(jnp.concatenate(levels, axis=1))
            segments = [
                (values, count, raw),
                (values, raw, raw + ones),
                (values, lower, lower + ones),
                (values, raw + ones, raw + count),
                (values, lower + ones, lower + count),
            ]
            step = cols_n // 2
            for at, run in enumerate(chunks(segments, step)):
                store(index, at * step, joined(run))

        copies.append(pltpu.make_async_copy(done.at[index], out.at[meta[slots[index]]], sems.at[index]))
        copies[-1].start()
    for copy in copies:
        copy.wait()


def gate_kernel(*refs):
    pass


def first_open_row(total, raw):
    return (2 * raw - total) // 16 * 16


def raw_kernel(factor, arrays, wide, landing, leaving, slots, meta, *refs):
    own, other = strips_in(refs[:arrays]), strips_in(refs[arrays : 2 * arrays])
    queries, *refs = refs[2 * arrays :]
    landed = refs.pop(0) if landing else None
    leavers, refs = refs[: len(leaving)], refs[len(leaving) :]
    _, out, done, *refs = refs
    pair = refs.pop(0) if wide else None
    values, sums, sums_two, land_sems, sems = refs
    rows_n, cols_n, _ = own[0].shape
    count, width = done.shape[1] - rows_n * cols_n, done.shape[2]
    raw = rows_n * cols_n
    ones = (rows_n // 2) * (cols_n // 2)

    copies = []
    for index, slot in enumerate(landing):
        copies.append(pltpu.make_async_copy(landed.at[index], out.at[meta[slot]], land_sems.at[index]))
        copies[-1].start()
    total, cut = done.shape[1], first_open_row(done.shape[1], rows_n * cols_n)
    slots = list(slots)

    def leave(strip, whole):
        rows = pl.ds(0, total if whole else cut)
        number = len(copies) - len(landing)
        copies.append(pltpu.make_async_copy(strip.at[rows], out.at[meta[slots.pop(0)], rows], sems.at[number]))
        copies[-1].start()

    for strips, whole in zip(leavers, leaving):
        for index in range(strips.shape[0]):
            leave(strips.at[index], whole)

    def times(left):
        return jnp.dot(left, queries[...], preferred_element_type=jnp.float32) * factor

    def store(index, at, part):
        done[index, at : at + part.shape[0]] = part[:, :width].astype(done.dtype)
        if wide:
            pair[index, at : at + part.shape[0]] = part[:, width:].astype(done.dtype)

    for index, halves in enumerate(zip(own, other)):

        def raw_row(row):
            return jnp.concatenate([half[row] for half in halves], axis=1)

        @pl.when(meta[0] == 0)
        def _():
            for row in range(rows_n):
                store(index, row * cols_n, times(raw_row(row)))
            store(index, raw, jnp.zeros((count, values.shape[1]), jnp.float32))

        @pl.when(meta[0] != 0)
        def _():
            for row in range(count // cols_n, rows_n):
                values[row * cols_n : (row + 1) * cols_n] = times(raw_row(row))
            levels = [pooled_levels(half, sums, sums_two).astype(done.dtype) for half in halves]
            values[raw : raw + count] = times(jnp.concatenate(levels, axis=1))
            segments = [
                (values, count, raw),
                (values, raw, raw + ones),
                (values, raw, raw + ones),
                (values, raw + ones, raw + count),
                (values, raw + ones, raw + count),
            ]
            step = cols_n // 2
            for at, run in enumerate(chunks(segments, step)):
                store(index, at * step, joined(run))

        if slots:
            leave(done.at[index], False)
    for copy in copies:
        copy.wait()


def came_kernel(factor, arrays, wide, late, pins, slots, late_whole, meta, *refs):
    own, other = strips_in(refs[:arrays]), strips_in(refs[arrays : 2 * arrays])
    queries, *refs = refs[2 * arrays :]
    late_rows = refs.pop(0) if late else None
    refs = refs[2 + late + pins :]
    out, done, *refs = refs
    late_done = refs.pop(0) if late else None
    pair = refs.pop(0) if wide else None
    values, sems = refs
    count, width = own[0].shape[0], done.shape[2]
    raw = done.shape[1] - count
    ones = count * 4 // 5
    copies = []

    def leave(strip, whole=False):
        if slots:
            cut = 0 if whole else first_open_row(raw + count, raw)
            rows = pl.ds(cut, raw + count - cut)
            slot = meta[slots[len(copies)]]
            copies.append(pltpu.make_async_copy(strip.at[rows], out.at[slot, rows], sems.at[len(copies)]))
            copies[-1].start()

    def merge(strip, part):
        @pl.when(meta[0] == 0)
        def _():
            strip[raw : raw + count] = part.astype(done.dtype)

        @pl.when(meta[0] != 0)
        def _():
            values[...] = part
            at = raw - count
            for first, last, into in ((0, ones, at), (ones, count, at + 2 * ones)):
                start = into // 16 * 16
                end = -(-(into + last - first) // 16) * 16
                parts = [values[first:last]]
                if start < into:
                    parts.insert(0, strip[start : start + 16].astype(jnp.float32)[: into - start])
                over = end - (into + last - first)
                if over:
                    parts.append(strip[end - 16 : end].astype(jnp.float32)[16 - over :])
                strip[start:end] = jnp.concatenate(parts, axis=0).astype(done.dtype)

    if late:
        for index in range(late_done.shape[0]):
            merge(late_done.at[index], late_rows[index].astype(jnp.float32))
            leave(late_done.at[index], late_whole)
    for index, halves in enumerate(zip(own, other)):
        left = jnp.concatenate([half[...] for half in halves], axis=1)
        part = jnp.dot(left, queries[...], preferred_element_type=jnp.float32) * factor
        if wide:
            pair[index] = part[:, width:].astype(done.dtype)
        merge(done.at[index], part[:, :width])
        leave(done.at[index])
    for copy in copies:
        copy.wait()


def ring_local(frame_one, frame_two):
    rows_axis = lax.axis_size("rows")
    rows_n, cols_n, chans = frame_two.shape
    queries_n = frame_one.shape[0]
    half_rows = rows_n // 2
    raw = half_rows * cols_n
    count = (half_rows // 2) * (cols_n // 2) + (half_rows // 4) * (cols_n // 4)
    factor = float(1.0 / (2 * chans) ** 0.5)
    me, side = lax.axis_index("rows"), lax.axis_index("chan")

    chips = rows_axis // 2
    columns, half_way = chips // 2, chips // 2
    order = [2 * z for z in range(columns)] + [2 * z + 1 for z in reversed(range(columns))]
    ring = [(2 * order[p], 2 * order[(p + 1) % chips]) for p in range(chips)]
    ring += [(2 * order[p] + 1, 2 * order[p - 1] + 1) for p in range(chips)]
    swap = [(r, r ^ 1) for r in range(rows_axis)]
    across = [(0, 1), (1, 0)]

    core, column, line = me % 2, me // 4, (me // 2) % 2
    place = jnp.where(line == 0, column, chips - 1 - column)
    steps = jnp.arange(half_way + 1, dtype=jnp.int32)

    def strips_of(c):
        p = (place + jnp.where(c == 0, -steps, steps)) % chips
        chip = jnp.where(p < columns, 2 * p, 2 * (chips - 1 - p) + 1)
        return [2 * chip + c, 2 * chip + 1 - c]

    meta = jnp.concatenate([side[None], *strips_of(core), *strips_of(1 - core)]).astype(jnp.int32)

    def slots_of(d, other_core):
        first = 1 + (2 * other_core) * (half_way + 1) + d
        return (first,) if d in (0, half_way) else (first, first + half_way + 1)

    in_vmem = pl.BlockSpec(memory_space=pltpu.VMEM)
    anywhere = pl.BlockSpec(memory_space=pl.ANY)
    scalars = pl.BlockSpec(memory_space=pltpu.SMEM)
    out_type = jax.ShapeDtypeStruct((rows_axis, raw + count, queries_n), frame_two.dtype)
    pooling = [
        pltpu.VMEM((half_rows // 2, cols_n, chans), jnp.float32),
        pltpu.VMEM((half_rows // 4, cols_n // 2, chans), jnp.float32),
    ]
    params = pltpu.CompilerParams(vmem_limit_bytes=VMEM_BYTES)
    def modelled(us):
        return pl.CostEstimate(flops=int(us * 10**9) + 1000, bytes_accessed=1000, transcendentals=0)


    def make_extra(out, halves, cost=0, pins=(), flip=False, carry=False, passed=None):
        strips = sum(half.shape[0] for half in halves)
        handed = () if out is None else (out,)
        carried = tuple(halves) if carry else ()
        aliases = {1 + len(halves): 1} if handed else {}
        aliases.update({1 + index: 2 + index for index in range(len(carried))})
        if passed is not None:
            pins, carried = (passed, *pins), (passed,)
            aliases[1 + len(halves) + len(handed)] = 2
        return pl.pallas_call(
            functools.partial(extra_kernel, len(halves), 2 + len(carried), flip),
            out_shape=(jax.ShapeDtypeStruct((strips, count, chans), frame_two.dtype), out_type)
            + tuple(jax.ShapeDtypeStruct(half.shape, half.dtype) for half in carried),
            in_specs=[scalars] + [in_vmem] * len(halves) + [anywhere] * len(handed + pins),
            out_specs=(in_vmem, anywhere) + (in_vmem if carry else anywhere,) * len(carried),
            scratch_shapes=pooling,
            input_output_aliases=aliases,
            compiler_params=params,
            cost_estimate=modelled(cost),
            name="extra",
        )(meta, *halves, *handed, *pins)

    def correlate(out, slots, own, other, came_own, came_other, landing=(), landed=None, cost=0, pins=()):
        parts = (own, other, came_own, came_other)
        strips = sum(piece.shape[0] for piece in own)
        operands = [*own, *other, *came_own, *came_other, queries_wide]
        pair_type = jax.ShapeDtypeStruct((strips, raw + count, queries_n), frame_two.dtype)
        return pl.pallas_call(
            functools.partial(corr_kernel, factor, tuple(len(part) for part in parts), True, slots, landing, len(pins)),
            out_shape=(out_type, pair_type),
            in_specs=[scalars] + [in_vmem] * len(operands) + [anywhere] * (1 + bool(landing) + len(pins)),
            out_specs=(anywhere, in_vmem),
            scratch_shapes=[
                pltpu.VMEM((strips, raw + count, queries_n), frame_two.dtype),
                pltpu.VMEM((raw + 2 * count, 2 * queries_n), jnp.float32),
                *pooling,
                pltpu.SemaphoreType.DMA((strips,)),
                pltpu.SemaphoreType.DMA((max(1, len(landing)),)),
            ],
            input_output_aliases={1 + len(operands) + bool(landing): 0},
            compiler_params=params,
            cost_estimate=modelled(cost),
            name="correlate",
        )(meta, *operands, *([landed] if landing else []), out, *pins)

    def product_type(strips, pixels):
        return jax.ShapeDtypeStruct((strips, pixels, queries_n), frame_two.dtype)

    def raw_rows(out, own, other, wide, landing=(), landed=None, cost=0, leavers=(), leaving=(), slots=(), pins=()):
        operands = [*own, *other, queries_wide if wide else queries]
        strips = sum(half.shape[0] for half in own)
        passive = ([landed] if landing else []) + list(leavers)
        pins = tuple(pins)
        return pl.pallas_call(
            functools.partial(raw_kernel, factor, len(own), wide, landing, leaving, slots),
            out_shape=(out_type,) + (product_type(strips, raw + count),) * (1 + wide),
            in_specs=[scalars] + [in_vmem] * len(operands) + [anywhere] * (1 + len(passive)),
            out_specs=(anywhere,) + (in_vmem,) * (1 + wide),
            scratch_shapes=[
                pltpu.VMEM((raw + count, queries_n * (1 + wide)), jnp.float32),
                *pooling,
                pltpu.SemaphoreType.DMA((max(1, len(landing)),)),
                pltpu.SemaphoreType.DMA((max(1, len(slots)),)),
            ],
            input_output_aliases={1 + len(operands) + len(passive): 0},
            compiler_params=params,
            cost_estimate=modelled(cost),
            name="raw_rows",
        )(meta, *operands, *passive, out)

    def came_rows(out, done, slots, own, other, wide, late=(), cost=0, pins=()):
        operands = [*own, *other, queries_wide if wide else queries, *late[:1]]
        first = 1 + len(operands)
        inout = [out, done, *late[1:]]
        extra_types = (product_type(done.shape[0], count),) if wide else ()
        return pl.pallas_call(
            functools.partial(came_kernel, factor, len(own), wide, len(late) // 2, len(pins), slots, not G("NL")),
            out_shape=tuple(jax.ShapeDtypeStruct(array.shape, array.dtype) for array in inout) + extra_types,
            in_specs=[scalars] + [in_vmem] * len(operands) + [anywhere] + [in_vmem] * (len(inout) - 1) + [anywhere] * len(pins),
            out_specs=(anywhere,) + (in_vmem,) * (len(inout) - 1 + wide),
            scratch_shapes=[
                pltpu.VMEM((count, queries_n), jnp.float32),
                pltpu.SemaphoreType.DMA((max(1, len(slots)),)),
            ],
            input_output_aliases={first + index: index for index in range(len(inout))},
            compiler_params=params,
            cost_estimate=modelled(cost),
            name="came_rows",
        )(meta, *operands, *inout, *pins)

    def gate(out, pins, cost):
        handed = (out, *pins)
        return pl.pallas_call(
            gate_kernel,
            out_shape=tuple(jax.ShapeDtypeStruct(array.shape, array.dtype) for array in handed),
            in_specs=[anywhere] * len(handed),
            out_specs=(anywhere,) * len(handed),
            input_output_aliases={index: index for index in range(len(handed))},
            compiler_params=params,
            cost_estimate=modelled(cost),
            name="gate",
        )(*handed)

    mine = lax.dynamic_slice_in_dim(frame_two, side * half_rows, half_rows, axis=0)[None]
    theirs = lax.dynamic_slice_in_dim(frame_two, (1 - side) * half_rows, half_rows, axis=0)[None]
    if G("XQ"):
        sent = jnp.concatenate([theirs.reshape(raw, chans), frame_one], axis=0)
        got = lax.ppermute(sent, "chan", across)
        partner, queries_other = got[:raw].reshape(theirs.shape), got[raw:]
    else:
        partner = lax.ppermute(theirs, "chan", across)
        queries_other = lax.ppermute(frame_one, "chan", across)
    def all_queries(mine, theirs):
        own_core = jnp.concatenate([mine.T, theirs.T], axis=0)
        return own_core, jnp.concatenate([own_core, lax.ppermute(own_core, "rows", swap)], axis=1)

    if not G("QC"): queries, queries_wide = all_queries(frame_one, queries_other)

    def permute_rows(pairs, pieces):
        return [lax.ppermute(piece, "rows", pairs) for piece in pieces]

    def whole(pieces):
        return pieces if len(pieces) == 1 else [jnp.concatenate(pieces, axis=0)]

    came = {0: ([mine], [partner])}
    moving = [[half, *permute_rows(swap, [half])] for half in (mine, partner)]
    join = [G("JA"), G("JB")]
    for d in range(1, half_way + 1):
        if d == half_way:
            moving = [[pieces[0][:1]] for pieces in moving]
        if d == half_way - 1 and G("BSPL"):
            moving[1] = [moving[1][0][:1], moving[1][0][1:]]
        moving = [whole(pieces) if d == join[part] else pieces for part, pieces in enumerate(moving)]
        if d == 1:
            ring_first = moving[1][-1]
        moving = [permute_rows(ring, pieces) for pieces in moving]
        came[d] = tuple(moving)
    across_came = {}

    def do_extra(out, d, part, pin=None):
        pins = () if pin is None else tuple(across_came[pin]) if isinstance(pin, tuple) else (pin,)
        across_came[d, 1 - part] = []
        groups = [[piece] for piece in came[d][part]] if part and d == half_way - 1 else [came[d][part]]
        for pieces in groups:
            extra, out = make_extra(out, pieces, G(f"X{d}{part}"), pins)
            across_came[d, 1 - part].append(lax.ppermute(extra, "chan", across))
            pins = ()
        return out

    lag = G("LAG")
    waiting = []

    def landing(now):
        if waiting and waiting[0][0] <= now:
            return waiting.pop(0)[1:]
        return (), None

    def product(out, d, pins=(), now=None):
        out, pair = correlate(out, slots_of(d, 0), *came[d], across_came[d, 0], across_came[d, 1], *landing(d if now is None else now), G(f"C{d}"), pins)
        waiting.append((d + lag, slots_of(d, 1), permute_rows(swap, [pair])[0]))
        return out

    if G("QC"):
        extra, out, sent = make_extra(None, came[0][0], G("X00"), ({1: partner, 2: ring_first}[G("PINX")],) if G("PINX") else (), passed=frame_one)
        across_came[0, 1] = [lax.ppermute(extra, "chan", across)]
        queries, queries_wide = all_queries(frame_one, lax.ppermute(sent, "chan", across))
    else:
        out = do_extra(None, 0, 0, partner if G("PINX") else None)
    lacking, out = make_extra(out, [theirs], G("X01"), tuple(across_came[0, 1]) if G("PIN01") else (), flip=True)
    across_came[0, 0] = [lacking]
    last = None
    order_of = [(1, 0), (2, 0), (1, 1)]
    for d in range(3, half_way):
        order_of += [(d, 0), (d - 1, 1)]
    order_of += [(half_way - 1, 1)]
    ready = 0
    for d, part in order_of:
        if part and d == half_way - 1 and G("C2POS") == 0:
            out = product(out, d - 1, now=half_way - 1)
        out = do_extra(out, d, part, last)
        last = (d, 1 - part)
        if G("C0POS") == 0 and (d, part) == (1, 0):
            out = product(out, 0)
        if part and d == 1 and G("C0POS") == 1:
            out = product(out, 0)
        if part == 0 and d >= 3:
            out = product(out, d - 2)
    near, far = half_way - 1, half_way

    def swap_one(piece):
        return permute_rows(swap, [piece])[0]

    R3 = G("R3POS")
    def near_raw(out):
        return raw_rows(out, *came[near], True, *landing(near), G("F3"))

    swapped = []

    def far_extra(out, part, pins):
        extra, out, piece = make_extra(out, came[far][part], G(f"X4{part}"), pins, carry=True)
        came[far][part][0] = piece
        across_came[far, 1 - part] = [lax.ppermute(extra, "chan", across)]
        swapped.append(swap_one(piece))
        return out

    if R3 == 0: out, near_done, near_pair = near_raw(out)
    if G("C2POS") == 1: out = product(out, near - 1, now=near)
    out = far_extra(out, 0, ())
    if R3 == 1: out, near_done, near_pair = near_raw(out)
    out = far_extra(out, 1, (swapped[0],) if G("PS0") == 1 else ())
    near_late = swap_one(near_pair)
    pins = (tuple(across_came[far, 1]) if G("PE4") == 1 else ()) + ((swapped[0],) if G("PS0") == 2 else ())

    slots = slots_of(near, 1) + slots_of(far, 0) + slots_of(far, 1)

    out, near_done, near_rows = came_rows(out, near_done, (), across_came[near, 0], across_came[near, 1], True, cost=G("F2"), pins=pins)
    near_rows = swap_one(near_rows)
    out, far_done = raw_rows(
        out,
        [came[far][0][0], swapped[0]],
        [came[far][1][0], swapped[1]],
        False,
        *landing(far),
        G("F0"),
        (near_done, near_late) if G("NL") else (near_done,),
        (True, False)[: 1 + G("NL")],
        slots_of(near, 0) + (slots if G("NL") else slots[len(slots_of(near, 1)) :]),
    )
    out, own, other = gate(out, [across_came[far, 0][0], across_came[far, 1][0]], G("GATE"))
    return came_rows(out, far_done, slots, [own, swap_one(own)], [other, swap_one(other)], False, (near_rows, near_late), G("F1"))[0]


def solution(mesh):
    rows_axis, groups = mesh.shape["rows"], mesh.shape["chan"]

    def local(frame_one, frame_two):
        rows_n, cols_n, chans = frame_two.shape
        ring = groups == 2 and rows_axis % 8 == 0 and rows_axis >= 16 and rows_n % 8 == 0 and cols_n % 32 == 0 and chans % LANES == 0
        return (ring_local if ring else gather_local)(frame_one, frame_two)

    in_specs = (P("rows", "chan"), P("rows", None, "chan"))
    out_specs = P(None, "chan", "rows")
    return jax.shard_map(local, mesh=mesh, in_specs=in_specs, out_specs=out_specs, check_vma=False)
```

```python
import functools

import jax
import jax.numpy as jnp
from jax import lax
from jax.experimental import pallas as pl
from jax.experimental.pallas import tpu as pltpu
from jax.sharding import PartitionSpec as P

LANES = 128
PARAMS = {'LAG': 2, 'F0': 10, 'F1': 0, 'PS0': 1, 'JA': 3, 'JB': 1, 'C0POS': 2, 'GATE': 30, 'F3': 10, 'F2': 22, 'NL': 0, 'PE4': 0, 'CP2': 1, 'P4': 0, 'P3': 1, 'X00': 10, 'X01': 10, 'C0': 10, 'X10': 10, 'X11': 10, 'C1': 10, 'X20': 10, 'X21': 10, 'C2': 10, 'X30': 10, 'X31': 10, 'C3': 10, 'X40': 10, 'X41': 10, 'C4': 10}


def G(name):
    return PARAMS.get(name, 0)


VMEM_BYTES = 28 * 1024 * 1024


def pool_strip(strip):
    full = strip.astype(jnp.float32)
    rows_n, cols_n, chans = full.shape
    level_one = full.reshape(rows_n // 2, 2, cols_n // 2, 2, chans).mean(axis=(1, 3))
    level_two = level_one.reshape(rows_n // 4, 2, cols_n // 4, 2, chans).mean(axis=(1, 3))
    joined = jnp.concatenate(
        [full.reshape(-1, chans), level_one.reshape(-1, chans), level_two.reshape(-1, chans)],
        axis=0,
    )
    return joined.astype(jnp.bfloat16)


def gather_local(frame_one, frame_two):
    groups = lax.axis_size("chan")
    queries = lax.all_gather(frame_one, "chan", axis=0, tiled=False)
    channels = queries.shape[0] * queries.shape[2]
    factor = 1.0 / jnp.sqrt(jnp.float32(channels))
    pooled = pool_strip(frame_two)
    share = pooled.shape[0] // groups
    traded = lax.all_to_all(
        pooled.reshape(groups, share, pooled.shape[1]), "chan", split_axis=0, concat_axis=0, tiled=True
    )
    gathered = lax.all_gather(traded, "rows", axis=0, tiled=False)
    values = jnp.einsum("skpc,kqc->spq", gathered, queries, preferred_element_type=jnp.float32)
    return (values * factor).astype(jnp.bfloat16)


def pooled_levels(half, sums, sums_two):
    rows_n, cols_n, _ = half.shape
    means = []
    for row in range(rows_n // 2):
        sums[row] = half[2 * row].astype(jnp.float32) + half[2 * row + 1].astype(jnp.float32)
        left = sums[row, pl.ds(0, cols_n // 2, stride=2), :]
        right = sums[row, pl.ds(1, cols_n // 2, stride=2), :]
        means.append((left + right) * 0.25)
    means_two = []
    for row in range(rows_n // 4):
        sums_two[row] = means[2 * row] + means[2 * row + 1]
        left = sums_two[row, pl.ds(0, cols_n // 4, stride=2), :]
        right = sums_two[row, pl.ds(1, cols_n // 4, stride=2), :]
        means_two.append((left + right) * 0.25)
    return jnp.concatenate(means + means_two, axis=0)


def strips_in(refs):
    return [ref.at[index] for ref in refs for index in range(ref.shape[0])]


def extra_kernel(pieces, results, flip, meta, *refs):
    halves = strips_in(refs[:pieces])
    extra, sums, sums_two = refs[-2 - results], *refs[-2:]
    count, cols_n = extra.shape[1], halves[0].shape[1]
    upper = meta[0] == (1 if flip else 0)

    @pl.when(upper)
    def _():
        for index, half in enumerate(halves):
            extra[index] = pooled_levels(half, sums, sums_two).astype(extra.dtype)

    @pl.when(jnp.logical_not(upper))
    def _():
        for index, half in enumerate(halves):
            parts, left, row = [], count, 0
            while left > 0:
                parts.append(half[row].astype(jnp.float32)[: min(left, cols_n)])
                left, row = left - cols_n, row + 1
            extra[index] = jnp.concatenate(parts, axis=0).astype(extra.dtype)


def chunks(segments, step):
    todo, runs = list(segments), []
    while todo:
        run, room = [], step
        while todo and room > 0:
            ref, first, last = todo.pop(0)
            take = min(room, last - first)
            run.append((ref, first, first + take))
            room -= take
            if first + take < last:
                todo.insert(0, (ref, first + take, last))
        runs.append(run)
    return runs


def joined(run):
    parts = [ref[first:last].astype(jnp.float32) for ref, first, last in run]
    return parts[0] if len(parts) == 1 else jnp.concatenate(parts, axis=0)


def corr_kernel(factor, pieces, wide, slots, landing, pins, meta, *refs):
    own, other = strips_in(refs[: pieces[0]]), strips_in(refs[pieces[0] : sum(pieces[:2])])
    refs = refs[sum(pieces[:2]) :]
    came_own, came_other = strips_in(refs[: pieces[2]]), strips_in(refs[pieces[2] : pieces[2] + pieces[3]])
    queries, *refs = refs[pieces[2] + pieces[3] :]
    landed = refs.pop(0) if landing else None
    out, *refs = refs[1 + pins :]
    pair = refs.pop(0) if wide else None
    done, values, sums, sums_two, sems, land_sems = refs
    rows_n, cols_n, _ = own[0].shape
    count, width = came_own[0].shape[0], done.shape[2]
    raw = rows_n * cols_n
    ones = (rows_n // 2) * (cols_n // 2)

    copies = []
    for index, slot in enumerate(landing):
        copies.append(pltpu.make_async_copy(landed.at[index], out.at[meta[slot]], land_sems.at[index]))
        copies[-1].start()

    def times(left):
        return jnp.dot(left, queries[...], preferred_element_type=jnp.float32) * factor

    def store(index, at, part):
        done[index, at : at + part.shape[0]] = part[:, :width].astype(done.dtype)
        if wide:
            pair[index, at : at + part.shape[0]] = part[:, width:].astype(done.dtype)

    for index in range(len(own)):

        def raw_row(row):
            return jnp.concatenate([own[index][row], other[index][row]], axis=1)

        def came_rows():
            return jnp.concatenate([came_own[index][...], came_other[index][...]], axis=1)

        @pl.when(meta[0] == 0)
        def _():
            for row in range(rows_n):
                store(index, row * cols_n, times(raw_row(row)))
            store(index, raw, times(came_rows()))

        @pl.when(meta[0] != 0)
        def _():
            for row in range(count // cols_n, rows_n):
                values[row * cols_n : (row + 1) * cols_n] = times(raw_row(row))
            values[raw : raw + count] = times(came_rows())
            levels = [pooled_levels(half[index], sums, sums_two).astype(done.dtype) for half in (own, other)]
            lower = raw + count
            values[lower : lower + count] = times(jnp.concatenate(levels, axis=1))
            segments = [
                (values, count, raw),
                (values, raw, raw + ones),
                (values, lower, lower + ones),
                (values, raw + ones, raw + count),
                (values, lower + ones, lower + count),
            ]
            step = cols_n // 2
            for at, run in enumerate(chunks(segments, step)):
                store(index, at * step, joined(run))

        copies.append(pltpu.make_async_copy(done.at[index], out.at[meta[slots[index]]], sems.at[index]))
        copies[-1].start()
    for copy in copies:
        copy.wait()


def gate_kernel(*refs):
    pass


def first_open_row(total, raw):
    return (2 * raw - total) // 16 * 16


def raw_kernel(factor, arrays, wide, landing, leaving, slots, meta, *refs):
    own, other = strips_in(refs[:arrays]), strips_in(refs[arrays : 2 * arrays])
    queries, *refs = refs[2 * arrays :]
    landed = refs.pop(0) if landing else None
    leavers, refs = refs[: len(leaving)], refs[len(leaving) :]
    _, out, done, *refs = refs
    pair = refs.pop(0) if wide else None
    values, sums, sums_two, land_sems, sems = refs
    rows_n, cols_n, _ = own[0].shape
    count, width = done.shape[1] - rows_n * cols_n, done.shape[2]
    raw = rows_n * cols_n
    ones = (rows_n // 2) * (cols_n // 2)

    copies = []
    for index, slot in enumerate(landing):
        copies.append(pltpu.make_async_copy(landed.at[index], out.at[meta[slot]], land_sems.at[index]))
        copies[-1].start()
    total, cut = done.shape[1], first_open_row(done.shape[1], rows_n * cols_n)
    slots = list(slots)

    def leave(strip, whole):
        rows = pl.ds(0, total if whole else cut)
        number = len(copies) - len(landing)
        copies.append(pltpu.make_async_copy(strip.at[rows], out.at[meta[slots.pop(0)], rows], sems.at[number]))
        copies[-1].start()

    for strips, whole in zip(leavers, leaving):
        for index in range(strips.shape[0] if whole is not None else 0):
            leave(strips.at[index], whole)

    def times(left):
        return jnp.dot(left, queries[...], preferred_element_type=jnp.float32) * factor

    def store(index, at, part):
        done[index, at : at + part.shape[0]] = part[:, :width].astype(done.dtype)
        if wide:
            pair[index, at : at + part.shape[0]] = part[:, width:].astype(done.dtype)

    for index, halves in enumerate(zip(own, other)):

        def raw_row(row):
            return jnp.concatenate([half[row] for half in halves], axis=1)

        @pl.when(meta[0] == 0)
        def _():
            for row in range(rows_n):
                store(index, row * cols_n, times(raw_row(row)))
            store(index, raw, jnp.zeros((count, values.shape[1]), jnp.float32))

        @pl.when(meta[0] != 0)
        def _():
            for row in range(count // cols_n, rows_n):
                values[row * cols_n : (row + 1) * cols_n] = times(raw_row(row))
            levels = [pooled_levels(half, sums, sums_two).astype(done.dtype) for half in halves]
            values[raw : raw + count] = times(jnp.concatenate(levels, axis=1))
            segments = [
                (values, count, raw),
                (values, raw, raw + ones),
                (values, raw, raw + ones),
                (values, raw + ones, raw + count),
                (values, raw + ones, raw + count),
            ]
            step = cols_n // 2
            for at, run in enumerate(chunks(segments, step)):
                store(index, at * step, joined(run))

        if slots:
            leave(done.at[index], False)
    for copy in copies:
        copy.wait()


def came_kernel(factor, arrays, wide, late, pins, slots, late_whole, meta, *refs):
    own, other = strips_in(refs[:arrays]), strips_in(refs[arrays : 2 * arrays])
    queries, *refs = refs[2 * arrays :]
    late_rows = refs.pop(0) if late else None
    refs = refs[2 + late + pins :]
    out, done, *refs = refs
    late_done = refs.pop(0) if late else None
    pair = refs.pop(0) if wide else None
    values, sems = refs
    count, width = own[0].shape[0], done.shape[2]
    raw = done.shape[1] - count
    ones = count * 4 // 5
    copies = []

    def leave(strip, whole=False):
        if slots:
            cut = 0 if whole else first_open_row(raw + count, raw)
            rows = pl.ds(cut, raw + count - cut)
            slot = meta[slots[len(copies)]]
            copies.append(pltpu.make_async_copy(strip.at[rows], out.at[slot, rows], sems.at[len(copies)]))
            copies[-1].start()

    def merge(strip, part):
        @pl.when(meta[0] == 0)
        def _():
            strip[raw : raw + count] = part.astype(done.dtype)

        @pl.when(meta[0] != 0)
        def _():
            values[...] = part
            at = raw - count
            for first, last, into in ((0, ones, at), (ones, count, at + 2 * ones)):
                start = into // 16 * 16
                end = -(-(into + last - first) // 16) * 16
                parts = [values[first:last]]
                if start < into:
                    parts.insert(0, strip[start : start + 16].astype(jnp.float32)[: into - start])
                over = end - (into + last - first)
                if over:
                    parts.append(strip[end - 16 : end].astype(jnp.float32)[16 - over :])
                strip[start:end] = jnp.concatenate(parts, axis=0).astype(done.dtype)

    if late:
        for index in range(late_done.shape[0]):
            merge(late_done.at[index], late_rows[index].astype(jnp.float32))
            leave(late_done.at[index], late_whole)
    for index, halves in enumerate(zip(own, other)):
        left = jnp.concatenate([half[...] for half in halves], axis=1)
        part = jnp.dot(left, queries[...], preferred_element_type=jnp.float32) * factor
        if wide:
            pair[index] = part[:, width:].astype(done.dtype)
        merge(done.at[index], part[:, :width])
        leave(done.at[index])
    for copy in copies:
        copy.wait()


def ring_local(frame_one, frame_two):
    rows_axis = lax.axis_size("rows")
    rows_n, cols_n, chans = frame_two.shape
    queries_n = frame_one.shape[0]
    half_rows = rows_n // 2
    raw = half_rows * cols_n
    count = (half_rows // 2) * (cols_n // 2) + (half_rows // 4) * (cols_n // 4)
    factor = float(1.0 / (2 * chans) ** 0.5)
    me, side = lax.axis_index("rows"), lax.axis_index("chan")

    chips = rows_axis // 2
    columns, half_way = chips // 2, chips // 2
    order = [2 * z for z in range(columns)] + [2 * z + 1 for z in reversed(range(columns))]
    ring = [(2 * order[p], 2 * order[(p + 1) % chips]) for p in range(chips)]
    ring += [(2 * order[p] + 1, 2 * order[p - 1] + 1) for p in range(chips)]
    swap = [(r, r ^ 1) for r in range(rows_axis)]
    across = [(0, 1), (1, 0)]

    core, column, line = me % 2, me // 4, (me // 2) % 2
    place = jnp.where(line == 0, column, chips - 1 - column)
    steps = jnp.arange(half_way + 1, dtype=jnp.int32)

    def strips_of(c):
        p = (place + jnp.where(c == 0, -steps, steps)) % chips
        chip = jnp.where(p < columns, 2 * p, 2 * (chips - 1 - p) + 1)
        return [2 * chip + c, 2 * chip + 1 - c]

    meta = jnp.concatenate([side[None], *strips_of(core), *strips_of(1 - core)]).astype(jnp.int32)

    def slots_of(d, other_core):
        first = 1 + (2 * other_core) * (half_way + 1) + d
        return (first,) if d in (0, half_way) else (first, first + half_way + 1)

    in_vmem = pl.BlockSpec(memory_space=pltpu.VMEM)
    anywhere = pl.BlockSpec(memory_space=pl.ANY)
    scalars = pl.BlockSpec(memory_space=pltpu.SMEM)
    out_type = jax.ShapeDtypeStruct((rows_axis, raw + count, queries_n), frame_two.dtype)
    pooling = [
        pltpu.VMEM((half_rows // 2, cols_n, chans), jnp.float32),
        pltpu.VMEM((half_rows // 4, cols_n // 2, chans), jnp.float32),
    ]
    params = pltpu.CompilerParams(vmem_limit_bytes=VMEM_BYTES)
    def modelled(us):
        return pl.CostEstimate(flops=int(us * 10**9) + 1000, bytes_accessed=1000, transcendentals=0)


    def make_extra(out, halves, cost=0, pins=(), flip=False, carry=False, passed=None):
        strips = sum(half.shape[0] for half in halves)
        handed = () if out is None else (out,)
        carried = tuple(halves) if carry else ()
        aliases = {1 + len(halves): 1} if handed else {}
        aliases.update({1 + index: 2 + index for index in range(len(carried))})
        if passed is not None:
            pins, carried = (passed, *pins), (passed,)
            aliases[1 + len(halves) + len(handed)] = 2
        return pl.pallas_call(
            functools.partial(extra_kernel, len(halves), 2 + len(carried), flip),
            out_shape=(jax.ShapeDtypeStruct((strips, count, chans), frame_two.dtype), out_type)
            + tuple(jax.ShapeDtypeStruct(half.shape, half.dtype) for half in carried),
            in_specs=[scalars] + [in_vmem] * len(halves) + [anywhere] * len(handed + pins),
            out_specs=(in_vmem, anywhere) + (in_vmem if carry else anywhere,) * len(carried),
            scratch_shapes=pooling,
            input_output_aliases=aliases,
            compiler_params=params,
            cost_estimate=modelled(cost),
            name="extra",
        )(meta, *halves, *handed, *pins)

    def correlate(out, slots, own, other, came_own, came_other, landing=(), landed=None, cost=0, pins=()):
        parts = (own, other, came_own, came_other)
        strips = sum(piece.shape[0] for piece in own)
        operands = [*own, *other, *came_own, *came_other, queries_wide]
        pair_type = jax.ShapeDtypeStruct((strips, raw + count, queries_n), frame_two.dtype)
        return pl.pallas_call(
            functools.partial(corr_kernel, factor, tuple(len(part) for part in parts), True, slots, landing, len(pins)),
            out_shape=(out_type, pair_type),
            in_specs=[scalars] + [in_vmem] * len(operands) + [anywhere] * (1 + bool(landing) + len(pins)),
            out_specs=(anywhere, in_vmem),
            scratch_shapes=[
                pltpu.VMEM((strips, raw + count, queries_n), frame_two.dtype),
                pltpu.VMEM((raw + 2 * count, 2 * queries_n), jnp.float32),
                *pooling,
                pltpu.SemaphoreType.DMA((strips,)),
                pltpu.SemaphoreType.DMA((max(1, len(landing)),)),
            ],
            input_output_aliases={1 + len(operands) + bool(landing): 0},
            compiler_params=params,
            cost_estimate=modelled(cost),
            name="correlate",
        )(meta, *operands, *([landed] if landing else []), out, *pins)

    def product_type(strips, pixels):
        return jax.ShapeDtypeStruct((strips, pixels, queries_n), frame_two.dtype)

    def raw_rows(out, own, other, wide, landing=(), landed=None, cost=0, leavers=(), leaving=(), slots=(), pins=()):
        operands = [*own, *other, queries_wide if wide else queries]
        strips = sum(half.shape[0] for half in own)
        passive = ([landed] if landing else []) + list(leavers)
        pins = tuple(pins)
        return pl.pallas_call(
            functools.partial(raw_kernel, factor, len(own), wide, landing, leaving, slots),
            out_shape=(out_type,) + (product_type(strips, raw + count),) * (1 + wide),
            in_specs=[scalars] + [in_vmem] * len(operands) + [anywhere] * (1 + len(passive)),
            out_specs=(anywhere,) + (in_vmem,) * (1 + wide),
            scratch_shapes=[
                pltpu.VMEM((raw + count, queries_n * (1 + wide)), jnp.float32),
                *pooling,
                pltpu.SemaphoreType.DMA((max(1, len(landing)),)),
                pltpu.SemaphoreType.DMA((max(1, len(slots)),)),
            ],
            input_output_aliases={1 + len(operands) + len(passive): 0},
            compiler_params=params,
            cost_estimate=modelled(cost),
            name="raw_rows",
        )(meta, *operands, *passive, out)

    def came_rows(out, done, slots, own, other, wide, late=(), cost=0, pins=()):
        operands = [*own, *other, queries_wide if wide else queries, *late[:1]]
        first = 1 + len(operands)
        inout = [out, done, *late[1:]]
        extra_types = (product_type(done.shape[0], count),) if wide else ()
        return pl.pallas_call(
            functools.partial(came_kernel, factor, len(own), wide, len(late) // 2, len(pins), slots, not G("NL")),
            out_shape=tuple(jax.ShapeDtypeStruct(array.shape, array.dtype) for array in inout) + extra_types,
            in_specs=[scalars] + [in_vmem] * len(operands) + [anywhere] + [in_vmem] * (len(inout) - 1) + [anywhere] * len(pins),
            out_specs=(anywhere,) + (in_vmem,) * (len(inout) - 1 + wide),
            scratch_shapes=[
                pltpu.VMEM((count, queries_n), jnp.float32),
                pltpu.SemaphoreType.DMA((max(1, len(slots)),)),
            ],
            input_output_aliases={first + index: index for index in range(len(inout))},
            compiler_params=params,
            cost_estimate=modelled(cost),
            name="came_rows",
        )(meta, *operands, *inout, *pins)

    def gate(out, pins, cost):
        handed = (out, *pins)
        return pl.pallas_call(
            gate_kernel,
            out_shape=tuple(jax.ShapeDtypeStruct(array.shape, array.dtype) for array in handed),
            in_specs=[anywhere] * len(handed),
            out_specs=(anywhere,) * len(handed),
            input_output_aliases={index: index for index in range(len(handed))},
            compiler_params=params,
            cost_estimate=modelled(cost),
            name="gate",
        )(*handed)

    mine = lax.dynamic_slice_in_dim(frame_two, side * half_rows, half_rows, axis=0)[None]
    theirs = lax.dynamic_slice_in_dim(frame_two, (1 - side) * half_rows, half_rows, axis=0)[None]
    if G("XQ"):
        sent = jnp.concatenate([theirs.reshape(raw, chans), frame_one], axis=0)
        got = lax.ppermute(sent, "chan", across)
        partner, queries_other = got[:raw].reshape(theirs.shape), got[raw:]
    else:
        partner = lax.ppermute(theirs, "chan", across)
        queries_other = lax.ppermute(frame_one, "chan", across)
    def all_queries(mine, theirs):
        own_core = jnp.concatenate([mine.T, theirs.T], axis=0)
        return own_core, jnp.concatenate([own_core, lax.ppermute(own_core, "rows", swap)], axis=1)

    if not G("QC"): queries, queries_wide = all_queries(frame_one, queries_other)

    def permute_rows(pairs, pieces):
        return [lax.ppermute(piece, "rows", pairs) for piece in pieces]

    def whole(pieces):
        return pieces if len(pieces) == 1 else [jnp.concatenate(pieces, axis=0)]

    came = {0: ([mine], [partner])}
    moving = [[half, *permute_rows(swap, [half])] for half in (mine, partner)]
    join = [G("JA"), G("JB")]
    for d in range(1, half_way + 1):
        if d == half_way:
            moving = [[pieces[0][:1]] for pieces in moving]
        if d == half_way - 1 and G("BSPL"):
            moving[1] = [moving[1][0][:1], moving[1][0][1:]]
        moving = [whole(pieces) if d == join[part] else pieces for part, pieces in enumerate(moving)]
        if d == 1:
            ring_first = moving[1][-1]
        moving = [permute_rows(ring, pieces) for pieces in moving]
        came[d] = tuple(moving)
    across_came = {}

    def do_extra(out, d, part, pin=None):
        pins = () if pin is None else tuple(across_came[pin]) if isinstance(pin, tuple) else (pin,)
        across_came[d, 1 - part] = []
        groups = [[piece] for piece in came[d][part]] if part and d == half_way - 1 else [came[d][part]]
        for pieces in groups:
            extra, out = make_extra(out, pieces, G(f"X{d}{part}"), pins)
            across_came[d, 1 - part].append(lax.ppermute(extra, "chan", across))
            pins = ()
        return out

    lag = G("LAG")
    waiting = []

    def landing(now):
        if waiting and waiting[0][0] <= now:
            return waiting.pop(0)[1:]
        return (), None

    def product(out, d, pins=(), now=None):
        out, pair = correlate(out, slots_of(d, 0), *came[d], across_came[d, 0], across_came[d, 1], *landing(d if now is None else now), G(f"C{d}"), pins)
        waiting.append((d + lag, slots_of(d, 1), permute_rows(swap, [pair])[0]))
        return out

    if G("QC"):
        extra, out, sent = make_extra(None, came[0][0], G("X00"), ({1: partner, 2: ring_first}[G("PINX")],) if G("PINX") else (), passed=frame_one)
        across_came[0, 1] = [lax.ppermute(extra, "chan", across)]
        queries, queries_wide = all_queries(frame_one, lax.ppermute(sent, "chan", across))
    else:
        out = do_extra(None, 0, 0, partner if G("PINX") else None)
    lacking, out = make_extra(out, [theirs], G("X01"), tuple(across_came[0, 1]) if G("PIN01") else (), flip=True)
    across_came[0, 0] = [lacking]
    near, far = half_way - 1, half_way

    def swap_one(piece):
        return permute_rows(swap, [piece])[0]

    def near_raw(out):
        return raw_rows(out, *came[near], True, *landing(near), G("F3"))

    swapped = []

    def far_extra(out, part, pins):
        extra, out, piece = make_extra(out, came[far][part], G(f"X4{part}"), pins, carry=True)
        came[far][part][0] = piece
        across_came[far, 1 - part] = [lax.ppermute(extra, "chan", across)]
        swapped.append(swap_one(piece))
        return out

    out = do_extra(out, 1, 0)
    out = do_extra(out, 2, 0, (1, 1))
    out = do_extra(out, 1, 1, (2, 1))
    out = product(out, 0)
    for d in range(3, far):
        out = do_extra(out, d, 0, (d - 2, 0))
        out = product(out, d - 2)
        out = do_extra(out, d - 1, 1, (d, 1))
    if G("CP2") == 0: out = product(out, near - 1, now=near)
    out = far_extra(out, 0, tuple(across_came[near - 1, 0]) if G("P4") else ())
    if G("CP2") == 1: out = product(out, near - 1, now=near)
    out = do_extra(out, near, 1, (far, 1) if G("P3") else None)
    out, near_done, near_pair = near_raw(out)
    out = far_extra(out, 1, (swapped[0],) if G("PS0") == 1 else ())
    near_late = swap_one(near_pair)
    pins = (tuple(across_came[far, 1]) if G("PE4") == 1 else ()) + ((swapped[0],) if G("PS0") == 2 else ())

    slots = slots_of(near, 1) + slots_of(far, 0) + slots_of(far, 1)

    out, near_done, near_rows = came_rows(out, near_done, (), across_came[near, 0], across_came[near, 1], True, cost=G("F2"), pins=pins)
    near_rows = swap_one(near_rows)
    out, far_done = raw_rows(
        out,
        [came[far][0][0], swapped[0]],
        [came[far][1][0], swapped[1]],
        False,
        *landing(far),
        G("F0"),
        (near_done, near_late),
        (True, False if G("NL") else None),
        slots_of(near, 0) + (slots if G("NL") else slots[len(slots_of(near, 1)) :]),
    )
    out, own, other = gate(out, [across_came[far, 0][0], across_came[far, 1][0]], G("GATE"))
    return came_rows(out, far_done, slots, [own, swap_one(own)], [other, swap_one(other)], False, (near_rows, near_late), G("F1"))[0]


def solution(mesh):
    rows_axis, groups = mesh.shape["rows"], mesh.shape["chan"]

    def local(frame_one, frame_two):
        rows_n, cols_n, chans = frame_two.shape
        ring = groups == 2 and rows_axis % 8 == 0 and rows_axis >= 16 and rows_n % 8 == 0 and cols_n % 32 == 0 and chans % LANES == 0
        return (ring_local if ring else gather_local)(frame_one, frame_two)

    in_specs = (P("rows", "chan"), P("rows", None, "chan"))
    out_specs = P(None, "chan", "rows")
    return jax.shard_map(local, mesh=mesh, in_specs=in_specs, out_specs=out_specs, check_vma=False)
```

```python
import functools

import jax
import jax.numpy as jnp
from jax import lax
from jax.experimental import pallas as pl
from jax.experimental.pallas import tpu as pltpu
from jax.sharding import PartitionSpec as P

LANES = 128
PARAMS = {'LAG': 2, 'F0': 10, 'F1': 0, 'PS0': 2, 'JA': 3, 'JB': 1, 'C0POS': 2, 'GATE': 30, 'F3': 10, 'F2': 22, 'NL': 1, 'PE4': 0, 'P4': 0, 'P3': 1, 'CPOS': 1, 'LC': 1, 'BSPL': 0, 'X00': 10, 'X01': 10, 'C0': 10, 'X10': 10, 'X11': 10, 'C1': 10, 'X20': 10, 'X21': 10, 'C2': 10, 'X30': 10, 'X31': 10, 'C3': 10, 'X40': 10, 'X41': 10, 'C4': 10}


def G(name):
    return PARAMS.get(name, 0)


VMEM_BYTES = 28 * 1024 * 1024


def pool_strip(strip):
    full = strip.astype(jnp.float32)
    rows_n, cols_n, chans = full.shape
    level_one = full.reshape(rows_n // 2, 2, cols_n // 2, 2, chans).mean(axis=(1, 3))
    level_two = level_one.reshape(rows_n // 4, 2, cols_n // 4, 2, chans).mean(axis=(1, 3))
    joined = jnp.concatenate(
        [full.reshape(-1, chans), level_one.reshape(-1, chans), level_two.reshape(-1, chans)],
        axis=0,
    )
    return joined.astype(jnp.bfloat16)


def gather_local(frame_one, frame_two):
    groups = lax.axis_size("chan")
    queries = lax.all_gather(frame_one, "chan", axis=0, tiled=False)
    channels = queries.shape[0] * queries.shape[2]
    factor = 1.0 / jnp.sqrt(jnp.float32(channels))
    pooled = pool_strip(frame_two)
    share = pooled.shape[0] // groups
    traded = lax.all_to_all(
        pooled.reshape(groups, share, pooled.shape[1]), "chan", split_axis=0, concat_axis=0, tiled=True
    )
    gathered = lax.all_gather(traded, "rows", axis=0, tiled=False)
    values = jnp.einsum("skpc,kqc->spq", gathered, queries, preferred_element_type=jnp.float32)
    return (values * factor).astype(jnp.bfloat16)


def pooled_levels(half, sums, sums_two):
    rows_n, cols_n, _ = half.shape
    means = []
    for row in range(rows_n // 2):
        sums[row] = half[2 * row].astype(jnp.float32) + half[2 * row + 1].astype(jnp.float32)
        left = sums[row, pl.ds(0, cols_n // 2, stride=2), :]
        right = sums[row, pl.ds(1, cols_n // 2, stride=2), :]
        means.append((left + right) * 0.25)
    means_two = []
    for row in range(rows_n // 4):
        sums_two[row] = means[2 * row] + means[2 * row + 1]
        left = sums_two[row, pl.ds(0, cols_n // 4, stride=2), :]
        right = sums_two[row, pl.ds(1, cols_n // 4, stride=2), :]
        means_two.append((left + right) * 0.25)
    return jnp.concatenate(means + means_two, axis=0)


def strips_in(refs):
    return [ref.at[index] for ref in refs for index in range(ref.shape[0])]


def extra_kernel(pieces, results, flip, meta, *refs):
    halves = strips_in(refs[:pieces])
    extra, sums, sums_two = refs[-2 - results], *refs[-2:]
    count, cols_n = extra.shape[1], halves[0].shape[1]
    upper = meta[0] == (1 if flip else 0)

    @pl.when(upper)
    def _():
        for index, half in enumerate(halves):
            extra[index] = pooled_levels(half, sums, sums_two).astype(extra.dtype)

    @pl.when(jnp.logical_not(upper))
    def _():
        for index, half in enumerate(halves):
            parts, left, row = [], count, 0
            while left > 0:
                parts.append(half[row].astype(jnp.float32)[: min(left, cols_n)])
                left, row = left - cols_n, row + 1
            extra[index] = jnp.concatenate(parts, axis=0).astype(extra.dtype)


def chunks(segments, step):
    todo, runs = list(segments), []
    while todo:
        run, room = [], step
        while todo and room > 0:
            ref, first, last = todo.pop(0)
            take = min(room, last - first)
            run.append((ref, first, first + take))
            room -= take
            if first + take < last:
                todo.insert(0, (ref, first + take, last))
        runs.append(run)
    return runs


def joined(run):
    parts = [ref[first:last].astype(jnp.float32) for ref, first, last in run]
    return parts[0] if len(parts) == 1 else jnp.concatenate(parts, axis=0)


def corr_kernel(factor, pieces, wide, slots, landing, pins, meta, *refs):
    own, other = strips_in(refs[: pieces[0]]), strips_in(refs[pieces[0] : sum(pieces[:2])])
    refs = refs[sum(pieces[:2]) :]
    came_own, came_other = strips_in(refs[: pieces[2]]), strips_in(refs[pieces[2] : pieces[2] + pieces[3]])
    queries, *refs = refs[pieces[2] + pieces[3] :]
    landed = refs.pop(0) if landing else None
    out, *refs = refs[1 + pins :]
    pair = refs.pop(0) if wide else None
    done, values, sums, sums_two, sems, land_sems = refs
    rows_n, cols_n, _ = own[0].shape
    count, width = came_own[0].shape[0], done.shape[2]
    raw = rows_n * cols_n
    ones = (rows_n // 2) * (cols_n // 2)

    copies = []
    for index, slot in enumerate(landing):
        copies.append(pltpu.make_async_copy(landed.at[index], out.at[meta[slot]], land_sems.at[index]))
        copies[-1].start()

    def times(left):
        return jnp.dot(left, queries[...], preferred_element_type=jnp.float32) * factor

    def store(index, at, part):
        done[index, at : at + part.shape[0]] = part[:, :width].astype(done.dtype)
        if wide:
            pair[index, at : at + part.shape[0]] = part[:, width:].astype(done.dtype)

    for index in range(len(own)):

        def raw_row(row):
            return jnp.concatenate([own[index][row], other[index][row]], axis=1)

        def came_rows():
            return jnp.concatenate([came_own[index][...], came_other[index][...]], axis=1)

        @pl.when(meta[0] == 0)
        def _():
            for row in range(rows_n):
                store(index, row * cols_n, times(raw_row(row)))
            store(index, raw, times(came_rows()))

        @pl.when(meta[0] != 0)
        def _():
            for row in range(count // cols_n, rows_n):
                values[row * cols_n : (row + 1) * cols_n] = times(raw_row(row))
            values[raw : raw + count] = times(came_rows())
            levels = [pooled_levels(half[index], sums, sums_two).astype(done.dtype) for half in (own, other)]
            lower = raw + count
            values[lower : lower + count] = times(jnp.concatenate(levels, axis=1))
            segments = [
                (values, count, raw),
                (values, raw, raw + ones),
                (values, lower, lower + ones),
                (values, raw + ones, raw + count),
                (values, lower + ones, lower + count),
            ]
            step = cols_n // 2
            for at, run in enumerate(chunks(segments, step)):
                store(index, at * step, joined(run))

        copies.append(pltpu.make_async_copy(done.at[index], out.at[meta[slots[index]]], sems.at[index]))
        copies[-1].start()
    for copy in copies:
        copy.wait()


def gate_kernel(*refs):
    pass


def first_open_row(total, raw):
    return (2 * raw - total) // 16 * 16


def raw_kernel(factor, arrays, wide, landing, leaving, slots, meta, *refs):
    own, other = strips_in(refs[: arrays[0]]), strips_in(refs[arrays[0] : sum(arrays)])
    queries, *refs = refs[sum(arrays) :]
    landed = refs.pop(0) if landing else None
    leavers, refs = refs[: len(leaving)], refs[len(leaving) :]
    _, out, done, *refs = refs
    pair = refs.pop(0) if wide else None
    values, sums, sums_two, land_sems, sems = refs
    rows_n, cols_n, _ = own[0].shape
    count, width = done.shape[1] - rows_n * cols_n, done.shape[2]
    raw = rows_n * cols_n
    ones = (rows_n // 2) * (cols_n // 2)

    copies = []
    for index, slot in enumerate(landing):
        copies.append(pltpu.make_async_copy(landed.at[index], out.at[meta[slot]], land_sems.at[index]))
        copies[-1].start()
    total, cut = done.shape[1], first_open_row(done.shape[1], rows_n * cols_n)
    slots = list(slots)

    def leave(strip, whole):
        rows = pl.ds(0, total if whole else cut)
        number = len(copies) - len(landing)
        copies.append(pltpu.make_async_copy(strip.at[rows], out.at[meta[slots.pop(0)], rows], sems.at[number]))
        copies[-1].start()

    for strips, whole in zip(leavers, leaving):
        for index in range(strips.shape[0] if whole is not None else 0):
            leave(strips.at[index], whole)

    def times(left):
        return jnp.dot(left, queries[...], preferred_element_type=jnp.float32) * factor

    def store(index, at, part):
        done[index, at : at + part.shape[0]] = part[:, :width].astype(done.dtype)
        if wide:
            pair[index, at : at + part.shape[0]] = part[:, width:].astype(done.dtype)

    for index, halves in enumerate(zip(own, other)):

        def raw_row(row):
            return jnp.concatenate([half[row] for half in halves], axis=1)

        @pl.when(meta[0] == 0)
        def _():
            for row in range(rows_n):
                store(index, row * cols_n, times(raw_row(row)))
            store(index, raw, jnp.zeros((count, values.shape[1]), jnp.float32))

        @pl.when(meta[0] != 0)
        def _():
            for row in range(count // cols_n, rows_n):
                values[row * cols_n : (row + 1) * cols_n] = times(raw_row(row))
            levels = [pooled_levels(half, sums, sums_two).astype(done.dtype) for half in halves]
            values[raw : raw + count] = times(jnp.concatenate(levels, axis=1))
            segments = [
                (values, count, raw),
                (values, raw, raw + ones),
                (values, raw, raw + ones),
                (values, raw + ones, raw + count),
                (values, raw + ones, raw + count),
            ]
            step = cols_n // 2
            for at, run in enumerate(chunks(segments, step)):
                store(index, at * step, joined(run))

        if slots:
            leave(done.at[index], False)
    for copy in copies:
        copy.wait()


def came_kernel(factor, arrays, wide, late, pins, slots, late_whole, landing, meta, *refs):
    own, other = strips_in(refs[: arrays[0]]), strips_in(refs[arrays[0] : sum(arrays)])
    queries, *refs = refs[sum(arrays) :]
    late_rows = refs.pop(0) if late else None
    refs = refs[2 + late :]
    landed = refs[0] if landing else None
    refs = refs[pins:]
    out, done, *refs = refs
    late_done = refs.pop(0) if late else None
    pair = refs.pop(0) if wide else None
    values, sems, land_sems = refs
    count, width = own[0].shape[0], done.shape[2]
    raw = done.shape[1] - count
    ones = count * 4 // 5
    copies, landings = [], []
    for index, slot in enumerate(landing):
        landings.append(pltpu.make_async_copy(landed.at[index], out.at[meta[slot]], land_sems.at[index]))
        landings[-1].start()

    def leave(strip, whole=False):
        if slots:
            cut = 0 if whole else first_open_row(raw + count, raw)
            rows = pl.ds(cut, raw + count - cut)
            slot = meta[slots[len(copies)]]
            copies.append(pltpu.make_async_copy(strip.at[rows], out.at[slot, rows], sems.at[len(copies)]))
            copies[-1].start()

    def merge(strip, part):
        @pl.when(meta[0] == 0)
        def _():
            strip[raw : raw + count] = part.astype(done.dtype)

        @pl.when(meta[0] != 0)
        def _():
            values[...] = part
            at = raw - count
            for first, last, into in ((0, ones, at), (ones, count, at + 2 * ones)):
                start = into // 16 * 16
                end = -(-(into + last - first) // 16) * 16
                parts = [values[first:last]]
                if start < into:
                    parts.insert(0, strip[start : start + 16].astype(jnp.float32)[: into - start])
                over = end - (into + last - first)
                if over:
                    parts.append(strip[end - 16 : end].astype(jnp.float32)[16 - over :])
                strip[start:end] = jnp.concatenate(parts, axis=0).astype(done.dtype)

    if late:
        for index in range(late_done.shape[0]):
            merge(late_done.at[index], late_rows[index].astype(jnp.float32))
            leave(late_done.at[index], late_whole)
    for index, halves in enumerate(zip(own, other)):
        left = jnp.concatenate([half[...] for half in halves], axis=1)
        part = jnp.dot(left, queries[...], preferred_element_type=jnp.float32) * factor
        if wide:
            pair[index] = part[:, width:].astype(done.dtype)
        merge(done.at[index], part[:, :width])
        leave(done.at[index])
    for copy in copies + landings:
        copy.wait()


def ring_local(frame_one, frame_two):
    rows_axis = lax.axis_size("rows")
    rows_n, cols_n, chans = frame_two.shape
    queries_n = frame_one.shape[0]
    half_rows = rows_n // 2
    raw = half_rows * cols_n
    count = (half_rows // 2) * (cols_n // 2) + (half_rows // 4) * (cols_n // 4)
    factor = float(1.0 / (2 * chans) ** 0.5)
    me, side = lax.axis_index("rows"), lax.axis_index("chan")

    chips = rows_axis // 2
    columns, half_way = chips // 2, chips // 2
    order = [2 * z for z in range(columns)] + [2 * z + 1 for z in reversed(range(columns))]
    ring = [(2 * order[p], 2 * order[(p + 1) % chips]) for p in range(chips)]
    ring += [(2 * order[p] + 1, 2 * order[p - 1] + 1) for p in range(chips)]
    swap = [(r, r ^ 1) for r in range(rows_axis)]
    across = [(0, 1), (1, 0)]

    core, column, line = me % 2, me // 4, (me // 2) % 2
    place = jnp.where(line == 0, column, chips - 1 - column)
    steps = jnp.arange(half_way + 1, dtype=jnp.int32)

    def strips_of(c):
        p = (place + jnp.where(c == 0, -steps, steps)) % chips
        chip = jnp.where(p < columns, 2 * p, 2 * (chips - 1 - p) + 1)
        return [2 * chip + c, 2 * chip + 1 - c]

    meta = jnp.concatenate([side[None], *strips_of(core), *strips_of(1 - core)]).astype(jnp.int32)

    def slots_of(d, other_core):
        first = 1 + (2 * other_core) * (half_way + 1) + d
        return (first,) if d in (0, half_way) else (first, first + half_way + 1)

    in_vmem = pl.BlockSpec(memory_space=pltpu.VMEM)
    anywhere = pl.BlockSpec(memory_space=pl.ANY)
    scalars = pl.BlockSpec(memory_space=pltpu.SMEM)
    out_type = jax.ShapeDtypeStruct((rows_axis, raw + count, queries_n), frame_two.dtype)
    pooling = [
        pltpu.VMEM((half_rows // 2, cols_n, chans), jnp.float32),
        pltpu.VMEM((half_rows // 4, cols_n // 2, chans), jnp.float32),
    ]
    params = pltpu.CompilerParams(vmem_limit_bytes=VMEM_BYTES)
    def modelled(us):
        return pl.CostEstimate(flops=int(us * 10**9) + 1000, bytes_accessed=1000, transcendentals=0)


    def make_extra(out, halves, cost=0, pins=(), flip=False, carry=False, passed=None):
        strips = sum(half.shape[0] for half in halves)
        handed = () if out is None else (out,)
        carried = tuple(halves) if carry else ()
        aliases = {1 + len(halves): 1} if handed else {}
        aliases.update({1 + index: 2 + index for index in range(len(carried))})
        if passed is not None:
            pins, carried = (passed, *pins), (passed,)
            aliases[1 + len(halves) + len(handed)] = 2
        return pl.pallas_call(
            functools.partial(extra_kernel, len(halves), 2 + len(carried), flip),
            out_shape=(jax.ShapeDtypeStruct((strips, count, chans), frame_two.dtype), out_type)
            + tuple(jax.ShapeDtypeStruct(half.shape, half.dtype) for half in carried),
            in_specs=[scalars] + [in_vmem] * len(halves) + [anywhere] * len(handed + pins),
            out_specs=(in_vmem, anywhere) + (in_vmem if carry else anywhere,) * len(carried),
            scratch_shapes=pooling,
            input_output_aliases=aliases,
            compiler_params=params,
            cost_estimate=modelled(cost),
            name="extra",
        )(meta, *halves, *handed, *pins)

    def correlate(out, slots, own, other, came_own, came_other, landing=(), landed=None, cost=0, pins=()):
        parts = (own, other, came_own, came_other)
        strips = sum(piece.shape[0] for piece in own)
        operands = [*own, *other, *came_own, *came_other, queries_wide]
        pair_type = jax.ShapeDtypeStruct((strips, raw + count, queries_n), frame_two.dtype)
        return pl.pallas_call(
            functools.partial(corr_kernel, factor, tuple(len(part) for part in parts), True, slots, landing, len(pins)),
            out_shape=(out_type, pair_type),
            in_specs=[scalars] + [in_vmem] * len(operands) + [anywhere] * (1 + bool(landing) + len(pins)),
            out_specs=(anywhere, in_vmem),
            scratch_shapes=[
                pltpu.VMEM((strips, raw + count, queries_n), frame_two.dtype),
                pltpu.VMEM((raw + 2 * count, 2 * queries_n), jnp.float32),
                *pooling,
                pltpu.SemaphoreType.DMA((strips,)),
                pltpu.SemaphoreType.DMA((max(1, len(landing)),)),
            ],
            input_output_aliases={1 + len(operands) + bool(landing): 0},
            compiler_params=params,
            cost_estimate=modelled(cost),
            name="correlate",
        )(meta, *operands, *([landed] if landing else []), out, *pins)

    def product_type(strips, pixels):
        return jax.ShapeDtypeStruct((strips, pixels, queries_n), frame_two.dtype)

    def raw_rows(out, own, other, wide, landing=(), landed=None, cost=0, leavers=(), leaving=(), slots=(), pins=()):
        operands = [*own, *other, queries_wide if wide else queries]
        strips = sum(half.shape[0] for half in own)
        passive = ([landed] if landing else []) + list(leavers)
        pins = tuple(pins)
        return pl.pallas_call(
            functools.partial(raw_kernel, factor, (len(own), len(other)), wide, landing, leaving, slots),
            out_shape=(out_type,) + (product_type(strips, raw + count),) * (1 + wide),
            in_specs=[scalars] + [in_vmem] * len(operands) + [anywhere] * (1 + len(passive)),
            out_specs=(anywhere,) + (in_vmem,) * (1 + wide),
            scratch_shapes=[
                pltpu.VMEM((raw + count, queries_n * (1 + wide)), jnp.float32),
                *pooling,
                pltpu.SemaphoreType.DMA((max(1, len(landing)),)),
                pltpu.SemaphoreType.DMA((max(1, len(slots)),)),
            ],
            input_output_aliases={1 + len(operands) + len(passive): 0},
            compiler_params=params,
            cost_estimate=modelled(cost),
            name="raw_rows",
        )(meta, *operands, *passive, out)

    def came_rows(out, done, slots, own, other, wide, late=(), cost=0, pins=(), landing=()):
        operands = [*own, *other, queries_wide if wide else queries, *late[:1]]
        first = 1 + len(operands)
        inout = [out, done, *late[1:]]
        extra_types = (product_type(done.shape[0], count),) if wide else ()
        return pl.pallas_call(
            functools.partial(came_kernel, factor, (len(own), len(other)), wide, len(late) // 2, len(pins), slots, not G("NL"), landing),
            out_shape=tuple(jax.ShapeDtypeStruct(array.shape, array.dtype) for array in inout) + extra_types,
            in_specs=[scalars] + [in_vmem] * len(operands) + [anywhere] + [in_vmem] * (len(inout) - 1) + [anywhere] * len(pins),
            out_specs=(anywhere,) + (in_vmem,) * (len(inout) - 1 + wide),
            scratch_shapes=[
                pltpu.VMEM((count, queries_n), jnp.float32),
                pltpu.SemaphoreType.DMA((max(1, len(slots)),)),
                pltpu.SemaphoreType.DMA((max(1, len(landing)),)),
            ],
            input_output_aliases={first + index: index for index in range(len(inout))},
            compiler_params=params,
            cost_estimate=modelled(cost),
            name="came_rows",
        )(meta, *operands, *inout, *pins)

    def gate(out, pins, cost):
        handed = (out, *pins)
        return pl.pallas_call(
            gate_kernel,
            out_shape=tuple(jax.ShapeDtypeStruct(array.shape, array.dtype) for array in handed),
            in_specs=[anywhere] * len(handed),
            out_specs=(anywhere,) * len(handed),
            input_output_aliases={index: index for index in range(len(handed))},
            compiler_params=params,
            cost_estimate=modelled(cost),
            name="gate",
        )(*handed)

    mine = lax.dynamic_slice_in_dim(frame_two, side * half_rows, half_rows, axis=0)[None]
    theirs = lax.dynamic_slice_in_dim(frame_two, (1 - side) * half_rows, half_rows, axis=0)[None]
    if G("XQ"):
        sent = jnp.concatenate([theirs.reshape(raw, chans), frame_one], axis=0)
        got = lax.ppermute(sent, "chan", across)
        partner, queries_other = got[:raw].reshape(theirs.shape), got[raw:]
    else:
        partner = lax.ppermute(theirs, "chan", across)
        queries_other = lax.ppermute(frame_one, "chan", across)
    def all_queries(mine, theirs):
        own_core = jnp.concatenate([mine.T, theirs.T], axis=0)
        return own_core, jnp.concatenate([own_core, lax.ppermute(own_core, "rows", swap)], axis=1)

    if not G("QC"): queries, queries_wide = all_queries(frame_one, queries_other)

    def permute_rows(pairs, pieces):
        return [lax.ppermute(piece, "rows", pairs) for piece in pieces]

    def whole(pieces):
        return pieces if len(pieces) == 1 else [jnp.concatenate(pieces, axis=0)]

    came = {0: ([mine], [partner])}
    moving = [[half, *permute_rows(swap, [half])] for half in (mine, partner)]
    join = [G("JA"), G("JB")]
    for d in range(1, half_way + 1):
        if d == half_way:
            moving = [[pieces[0][:1]] for pieces in moving]
        if d == half_way - 1 and G("BSPL"):
            moving[1] = [moving[1][0][:1], moving[1][0][1:]]
        moving = [whole(pieces) if d == join[part] else pieces for part, pieces in enumerate(moving)]
        if d == 1:
            ring_first = moving[1][-1]
        moving = [permute_rows(ring, pieces) for pieces in moving]
        came[d] = tuple(moving)
    across_came = {}

    def do_extra(out, d, part, pin=None):
        pins = () if pin is None else tuple(across_came[pin]) if isinstance(pin, tuple) else (pin,)
        across_came[d, 1 - part] = []
        groups = [[piece] for piece in came[d][part]] if part and d == half_way - 1 else [came[d][part]]
        for pieces in groups:
            extra, out = make_extra(out, pieces, G(f"X{d}{part}"), pins)
            across_came[d, 1 - part].append(lax.ppermute(extra, "chan", across))
            pins = ()
        return out

    lag = G("LAG")
    waiting = []

    def landing(now):
        if waiting and waiting[0][0] <= now:
            return waiting.pop(0)[1:]
        return (), None

    def product(out, d, pins=(), now=None):
        out, pair = correlate(out, slots_of(d, 0), *came[d], across_came[d, 0], across_came[d, 1], *landing(d if now is None else now), G(f"C{d}"), pins)
        waiting.append((d + lag, slots_of(d, 1), permute_rows(swap, [pair])[0]))
        return out

    if G("QC"):
        extra, out, sent = make_extra(None, came[0][0], G("X00"), ({1: partner, 2: ring_first}[G("PINX")],) if G("PINX") else (), passed=frame_one)
        across_came[0, 1] = [lax.ppermute(extra, "chan", across)]
        queries, queries_wide = all_queries(frame_one, lax.ppermute(sent, "chan", across))
    else:
        out = do_extra(None, 0, 0, partner if G("PINX") else None)
    lacking, out = make_extra(out, [theirs], G("X01"), tuple(across_came[0, 1]) if G("PIN01") else (), flip=True)
    across_came[0, 0] = [lacking]
    near, far = half_way - 1, half_way

    def swap_one(piece):
        return permute_rows(swap, [piece])[0]

    def near_raw(out):
        return raw_rows(out, *came[near], True, *landing(near), G("F3"))

    swapped = []

    def far_extra(out, part, pins):
        extra, out, piece = make_extra(out, came[far][part], G(f"X4{part}"), pins, carry=True)
        came[far][part][0] = piece
        across_came[far, 1 - part] = [lax.ppermute(extra, "chan", across)]
        swapped.append(swap_one(piece))
        return out

    out = do_extra(out, 1, 0)
    out = do_extra(out, 2, 0, (1, 1))
    out = do_extra(out, 1, 1, (2, 1))
    out = product(out, 0)
    for d in range(3, far):
        out = do_extra(out, d, 0, (d - 2, 0))
        out = product(out, d - 2)
        out = do_extra(out, d - 1, 1, (d, 1))
    out = far_extra(out, 0, tuple(across_came[near - 1, 0]) if G("P4") else ())
    across_came[near, 0] = []
    for index, piece in enumerate(came[near][1]):
        if index == len(came[near][1]) - G("CPOS"):
            out = product(out, near - 1, now=near)
        extra, out = make_extra(out, [piece], G("X31"), tuple(across_came[far, 1]) if G("P3") == index + 1 else ())
        across_came[near, 0].append(lax.ppermute(extra, "chan", across))
    out, near_done, near_pair = near_raw(out)
    out = far_extra(out, 1, (swapped[0],) if G("PS0") == 1 else ())
    near_late = swap_one(near_pair)
    pins = (tuple(across_came[far, 1]) if G("PE4") == 1 else ()) + ((swapped[0],) if G("PS0") == 2 else ())

    slots = slots_of(near, 1) + slots_of(far, 0) + slots_of(far, 1)

    landing_now, landed_now = landing(far) if G("LC") else ((), None)
    pins = ((landed_now,) if landing_now else ()) + pins
    out, near_done, near_rows = came_rows(
        out, near_done, (), across_came[near, 0], across_came[near, 1], True, cost=G("F2"), pins=pins, landing=landing_now
    )
    near_rows = swap_one(near_rows)
    out, far_done = raw_rows(
        out,
        [came[far][0][0], swapped[0]],
        [came[far][1][0], swapped[1]],
        False,
        *landing(far),
        G("F0"),
        (near_done, near_late),
        (True, False if G("NL") else None),
        slots_of(near, 0) + (slots if G("NL") else slots[len(slots_of(near, 1)) :]),
    )
    out, own, other = gate(out, [across_came[far, 0][0], across_came[far, 1][0]], G("GATE"))
    return came_rows(out, far_done, slots, [own, swap_one(own)], [other, swap_one(other)], False, (near_rows, near_late), G("F1"))[0]


def solution(mesh):
    rows_axis, groups = mesh.shape["rows"], mesh.shape["chan"]

    def local(frame_one, frame_two):
        rows_n, cols_n, chans = frame_two.shape
        ring = groups == 2 and rows_axis % 8 == 0 and rows_axis >= 16 and rows_n % 8 == 0 and cols_n % 32 == 0 and chans % LANES == 0
        return (ring_local if ring else gather_local)(frame_one, frame_two)

    in_specs = (P("rows", "chan"), P("rows", None, "chan"))
    out_specs = P(None, "chan", "rows")
    return jax.shard_map(local, mesh=mesh, in_specs=in_specs, out_specs=out_specs, check_vma=False)
```

```python
import functools

import jax
import jax.numpy as jnp
from jax import lax
from jax.experimental import pallas as pl
from jax.experimental.pallas import tpu as pltpu
from jax.sharding import PartitionSpec as P

LANES = 128
PARAMS = {'LAG': 2, 'F0': 10, 'F1': 0, 'PS0': 2, 'JA': 3, 'JB': 1, 'C0POS': 2, 'GATE': 30, 'F3': 0, 'F2': 22, 'NL': 1, 'PE4': 0, 'P4': 0, 'P3': 1, 'CPOS': 1, 'LC': 0, 'BSPL': 1, 'ONEX': 1, 'X00': 10, 'X01': 10, 'C0': 10, 'X10': 10, 'X11': 10, 'C1': 10, 'X20': 10, 'X21': 10, 'C2': 3, 'X30': 10, 'X31': 3, 'C3': 10, 'X40': 10, 'X41': 10, 'C4': 10}


def G(name):
    return PARAMS.get(name, 0)


VMEM_BYTES = 28 * 1024 * 1024


def pool_strip(strip):
    full = strip.astype(jnp.float32)
    rows_n, cols_n, chans = full.shape
    level_one = full.reshape(rows_n // 2, 2, cols_n // 2, 2, chans).mean(axis=(1, 3))
    level_two = level_one.reshape(rows_n // 4, 2, cols_n // 4, 2, chans).mean(axis=(1, 3))
    joined = jnp.concatenate(
        [full.reshape(-1, chans), level_one.reshape(-1, chans), level_two.reshape(-1, chans)],
        axis=0,
    )
    return joined.astype(jnp.bfloat16)


def gather_local(frame_one, frame_two):
    groups = lax.axis_size("chan")
    queries = lax.all_gather(frame_one, "chan", axis=0, tiled=False)
    channels = queries.shape[0] * queries.shape[2]
    factor = 1.0 / jnp.sqrt(jnp.float32(channels))
    pooled = pool_strip(frame_two)
    share = pooled.shape[0] // groups
    traded = lax.all_to_all(
        pooled.reshape(groups, share, pooled.shape[1]), "chan", split_axis=0, concat_axis=0, tiled=True
    )
    gathered = lax.all_gather(traded, "rows", axis=0, tiled=False)
    values = jnp.einsum("skpc,kqc->spq", gathered, queries, preferred_element_type=jnp.float32)
    return (values * factor).astype(jnp.bfloat16)


def pooled_levels(half, sums, sums_two):
    rows_n, cols_n, _ = half.shape
    means = []
    for row in range(rows_n // 2):
        sums[row] = half[2 * row].astype(jnp.float32) + half[2 * row + 1].astype(jnp.float32)
        left = sums[row, pl.ds(0, cols_n // 2, stride=2), :]
        right = sums[row, pl.ds(1, cols_n // 2, stride=2), :]
        means.append((left + right) * 0.25)
    means_two = []
    for row in range(rows_n // 4):
        sums_two[row] = means[2 * row] + means[2 * row + 1]
        left = sums_two[row, pl.ds(0, cols_n // 4, stride=2), :]
        right = sums_two[row, pl.ds(1, cols_n // 4, stride=2), :]
        means_two.append((left + right) * 0.25)
    return jnp.concatenate(means + means_two, axis=0)


def strips_in(refs):
    return [ref.at[index] for ref in refs for index in range(ref.shape[0])]


def extra_kernel(pieces, results, flip, meta, *refs):
    halves = strips_in(refs[:pieces])
    extra, sums, sums_two = refs[-2 - results], *refs[-2:]
    count, cols_n = extra.shape[1], halves[0].shape[1]
    upper = meta[0] == (1 if flip else 0)

    @pl.when(upper)
    def _():
        for index, half in enumerate(halves):
            extra[index] = pooled_levels(half, sums, sums_two).astype(extra.dtype)

    @pl.when(jnp.logical_not(upper))
    def _():
        for index, half in enumerate(halves):
            parts, left, row = [], count, 0
            while left > 0:
                parts.append(half[row].astype(jnp.float32)[: min(left, cols_n)])
                left, row = left - cols_n, row + 1
            extra[index] = jnp.concatenate(parts, axis=0).astype(extra.dtype)


def chunks(segments, step):
    todo, runs = list(segments), []
    while todo:
        run, room = [], step
        while todo and room > 0:
            ref, first, last = todo.pop(0)
            take = min(room, last - first)
            run.append((ref, first, first + take))
            room -= take
            if first + take < last:
                todo.insert(0, (ref, first + take, last))
        runs.append(run)
    return runs


def joined(run):
    parts = [ref[first:last].astype(jnp.float32) for ref, first, last in run]
    return parts[0] if len(parts) == 1 else jnp.concatenate(parts, axis=0)


def corr_kernel(factor, pieces, wide, slots, landing, pins, meta, *refs):
    own, other = strips_in(refs[: pieces[0]]), strips_in(refs[pieces[0] : sum(pieces[:2])])
    refs = refs[sum(pieces[:2]) :]
    came_own, came_other = strips_in(refs[: pieces[2]]), strips_in(refs[pieces[2] : pieces[2] + pieces[3]])
    queries, *refs = refs[pieces[2] + pieces[3] :]
    landed = refs.pop(0) if landing else None
    out, *refs = refs[1 + pins :]
    pair = refs.pop(0) if wide else None
    done, values, sums, sums_two, sems, land_sems = refs
    rows_n, cols_n, _ = own[0].shape
    count, width = came_own[0].shape[0], done.shape[2]
    raw = rows_n * cols_n
    ones = (rows_n // 2) * (cols_n // 2)

    copies = []
    for index, slot in enumerate(landing):
        copies.append(pltpu.make_async_copy(landed.at[index], out.at[meta[slot]], land_sems.at[index]))
        copies[-1].start()

    def times(left):
        return jnp.dot(left, queries[...], preferred_element_type=jnp.float32) * factor

    def store(index, at, part):
        done[index, at : at + part.shape[0]] = part[:, :width].astype(done.dtype)
        if wide:
            pair[index, at : at + part.shape[0]] = part[:, width:].astype(done.dtype)

    for index in range(len(own)):

        def raw_row(row):
            return jnp.concatenate([own[index][row], other[index][row]], axis=1)

        def came_rows():
            return jnp.concatenate([came_own[index][...], came_other[index][...]], axis=1)

        @pl.when(meta[0] == 0)
        def _():
            for row in range(rows_n):
                store(index, row * cols_n, times(raw_row(row)))
            store(index, raw, times(came_rows()))

        @pl.when(meta[0] != 0)
        def _():
            for row in range(count // cols_n, rows_n):
                values[row * cols_n : (row + 1) * cols_n] = times(raw_row(row))
            values[raw : raw + count] = times(came_rows())
            levels = [pooled_levels(half[index], sums, sums_two).astype(done.dtype) for half in (own, other)]
            lower = raw + count
            values[lower : lower + count] = times(jnp.concatenate(levels, axis=1))
            segments = [
                (values, count, raw),
                (values, raw, raw + ones),
                (values, lower, lower + ones),
                (values, raw + ones, raw + count),
                (values, lower + ones, lower + count),
            ]
            step = cols_n // 2
            for at, run in enumerate(chunks(segments, step)):
                store(index, at * step, joined(run))

        copies.append(pltpu.make_async_copy(done.at[index], out.at[meta[slots[index]]], sems.at[index]))
        copies[-1].start()
    for copy in copies:
        copy.wait()


def gate_kernel(*refs):
    pass


def first_open_row(total, raw):
    return (2 * raw - total) // 16 * 16


def raw_kernel(factor, arrays, wide, landing, leaving, slots, pins, meta, *refs):
    own, other = strips_in(refs[: arrays[0]]), strips_in(refs[arrays[0] : sum(arrays)])
    queries, *refs = refs[sum(arrays) :]
    landed = refs.pop(0) if landing else None
    leavers, refs = refs[: len(leaving)], refs[len(leaving) :]
    out, done, *refs = refs[1 + pins :]
    pair = refs.pop(0) if wide else None
    values, sums, sums_two, land_sems, sems = refs
    rows_n, cols_n, _ = own[0].shape
    count, width = done.shape[1] - rows_n * cols_n, done.shape[2]
    raw = rows_n * cols_n
    ones = (rows_n // 2) * (cols_n // 2)

    copies = []
    for index, slot in enumerate(landing):
        copies.append(pltpu.make_async_copy(landed.at[index], out.at[meta[slot]], land_sems.at[index]))
        copies[-1].start()
    total, cut = done.shape[1], first_open_row(done.shape[1], rows_n * cols_n)
    slots = list(slots)

    def leave(strip, whole):
        rows = pl.ds(0, total if whole else cut)
        number = len(copies) - len(landing)
        copies.append(pltpu.make_async_copy(strip.at[rows], out.at[meta[slots.pop(0)], rows], sems.at[number]))
        copies[-1].start()

    for strips, whole in zip(leavers, leaving):
        for index in range(strips.shape[0] if whole is not None else 0):
            leave(strips.at[index], whole)

    def times(left):
        return jnp.dot(left, queries[...], preferred_element_type=jnp.float32) * factor

    def store(index, at, part):
        done[index, at : at + part.shape[0]] = part[:, :width].astype(done.dtype)
        if wide:
            pair[index, at : at + part.shape[0]] = part[:, width:].astype(done.dtype)

    for index, halves in enumerate(zip(own, other)):

        def raw_row(row):
            return jnp.concatenate([half[row] for half in halves], axis=1)

        @pl.when(meta[0] == 0)
        def _():
            for row in range(rows_n):
                store(index, row * cols_n, times(raw_row(row)))
            store(index, raw, jnp.zeros((count, values.shape[1]), jnp.float32))

        @pl.when(meta[0] != 0)
        def _():
            for row in range(count // cols_n, rows_n):
                values[row * cols_n : (row + 1) * cols_n] = times(raw_row(row))
            levels = [pooled_levels(half, sums, sums_two).astype(done.dtype) for half in halves]
            values[raw : raw + count] = times(jnp.concatenate(levels, axis=1))
            segments = [
                (values, count, raw),
                (values, raw, raw + ones),
                (values, raw, raw + ones),
                (values, raw + ones, raw + count),
                (values, raw + ones, raw + count),
            ]
            step = cols_n // 2
            for at, run in enumerate(chunks(segments, step)):
                store(index, at * step, joined(run))

        if slots:
            leave(done.at[index], False)
    for copy in copies:
        copy.wait()


def came_kernel(factor, arrays, wide, late, pins, slots, late_whole, landing, meta, *refs):
    own, other = strips_in(refs[: arrays[0]]), strips_in(refs[arrays[0] : sum(arrays)])
    queries, *refs = refs[sum(arrays) :]
    late_rows = refs.pop(0) if late else None
    refs = refs[2 + late :]
    landed = refs[0] if landing else None
    refs = refs[pins:]
    out, done, *refs = refs
    late_done = refs.pop(0) if late else None
    pair = refs.pop(0) if wide else None
    values, sems, land_sems = refs
    count, width = own[0].shape[0], done.shape[2]
    raw = done.shape[1] - count
    ones = count * 4 // 5
    copies, landings = [], []
    for index, slot in enumerate(landing):
        landings.append(pltpu.make_async_copy(landed.at[index], out.at[meta[slot]], land_sems.at[index]))
        landings[-1].start()

    def leave(strip, whole=False):
        if slots:
            cut = 0 if whole else first_open_row(raw + count, raw)
            rows = pl.ds(cut, raw + count - cut)
            slot = meta[slots[len(copies)]]
            copies.append(pltpu.make_async_copy(strip.at[rows], out.at[slot, rows], sems.at[len(copies)]))
            copies[-1].start()

    def merge(strip, part):
        @pl.when(meta[0] == 0)
        def _():
            strip[raw : raw + count] = part.astype(done.dtype)

        @pl.when(meta[0] != 0)
        def _():
            values[...] = part
            at = raw - count
            for first, last, into in ((0, ones, at), (ones, count, at + 2 * ones)):
                start = into // 16 * 16
                end = -(-(into + last - first) // 16) * 16
                parts = [values[first:last]]
                if start < into:
                    parts.insert(0, strip[start : start + 16].astype(jnp.float32)[: into - start])
                over = end - (into + last - first)
                if over:
                    parts.append(strip[end - 16 : end].astype(jnp.float32)[16 - over :])
                strip[start:end] = jnp.concatenate(parts, axis=0).astype(done.dtype)

    if late:
        for index in range(late_done.shape[0]):
            merge(late_done.at[index], late_rows[index].astype(jnp.float32))
            leave(late_done.at[index], late_whole)
    for index, halves in enumerate(zip(own, other)):
        left = jnp.concatenate([half[...] for half in halves], axis=1)
        part = jnp.dot(left, queries[...], preferred_element_type=jnp.float32) * factor
        if wide:
            pair[index] = part[:, width:].astype(done.dtype)
        merge(done.at[index], part[:, :width])
        leave(done.at[index])
    for copy in copies + landings:
        copy.wait()


def ring_local(frame_one, frame_two):
    rows_axis = lax.axis_size("rows")
    rows_n, cols_n, chans = frame_two.shape
    queries_n = frame_one.shape[0]
    half_rows = rows_n // 2
    raw = half_rows * cols_n
    count = (half_rows // 2) * (cols_n // 2) + (half_rows // 4) * (cols_n // 4)
    factor = float(1.0 / (2 * chans) ** 0.5)
    me, side = lax.axis_index("rows"), lax.axis_index("chan")

    chips = rows_axis // 2
    columns, half_way = chips // 2, chips // 2
    order = [2 * z for z in range(columns)] + [2 * z + 1 for z in reversed(range(columns))]
    ring = [(2 * order[p], 2 * order[(p + 1) % chips]) for p in range(chips)]
    ring += [(2 * order[p] + 1, 2 * order[p - 1] + 1) for p in range(chips)]
    swap = [(r, r ^ 1) for r in range(rows_axis)]
    across = [(0, 1), (1, 0)]

    core, column, line = me % 2, me // 4, (me // 2) % 2
    place = jnp.where(line == 0, column, chips - 1 - column)
    steps = jnp.arange(half_way + 1, dtype=jnp.int32)

    def strips_of(c):
        p = (place + jnp.where(c == 0, -steps, steps)) % chips
        chip = jnp.where(p < columns, 2 * p, 2 * (chips - 1 - p) + 1)
        return [2 * chip + c, 2 * chip + 1 - c]

    meta = jnp.concatenate([side[None], *strips_of(core), *strips_of(1 - core)]).astype(jnp.int32)

    def slots_of(d, other_core):
        first = 1 + (2 * other_core) * (half_way + 1) + d
        return (first,) if d in (0, half_way) else (first, first + half_way + 1)

    in_vmem = pl.BlockSpec(memory_space=pltpu.VMEM)
    anywhere = pl.BlockSpec(memory_space=pl.ANY)
    scalars = pl.BlockSpec(memory_space=pltpu.SMEM)
    out_type = jax.ShapeDtypeStruct((rows_axis, raw + count, queries_n), frame_two.dtype)
    pooling = [
        pltpu.VMEM((half_rows // 2, cols_n, chans), jnp.float32),
        pltpu.VMEM((half_rows // 4, cols_n // 2, chans), jnp.float32),
    ]
    params = pltpu.CompilerParams(vmem_limit_bytes=VMEM_BYTES)
    def modelled(us):
        return pl.CostEstimate(flops=int(us * 10**9) + 1000, bytes_accessed=1000, transcendentals=0)


    def make_extra(out, halves, cost=0, pins=(), flip=False, carry=False, passed=None):
        strips = sum(half.shape[0] for half in halves)
        handed = () if out is None else (out,)
        carried = tuple(halves) if carry else ()
        aliases = {1 + len(halves): 1} if handed else {}
        aliases.update({1 + index: 2 + index for index in range(len(carried))})
        if passed is not None:
            pins, carried = (passed, *pins), (passed,)
            aliases[1 + len(halves) + len(handed)] = 2
        return pl.pallas_call(
            functools.partial(extra_kernel, len(halves), 2 + len(carried), flip),
            out_shape=(jax.ShapeDtypeStruct((strips, count, chans), frame_two.dtype), out_type)
            + tuple(jax.ShapeDtypeStruct(half.shape, half.dtype) for half in carried),
            in_specs=[scalars] + [in_vmem] * len(halves) + [anywhere] * len(handed + pins),
            out_specs=(in_vmem, anywhere) + (in_vmem if carry else anywhere,) * len(carried),
            scratch_shapes=pooling,
            input_output_aliases=aliases,
            compiler_params=params,
            cost_estimate=modelled(cost),
            name="extra",
        )(meta, *halves, *handed, *pins)

    def correlate(out, slots, own, other, came_own, came_other, landing=(), landed=None, cost=0, pins=()):
        parts = (own, other, came_own, came_other)
        strips = sum(piece.shape[0] for piece in own)
        operands = [*own, *other, *came_own, *came_other, queries_wide]
        pair_type = jax.ShapeDtypeStruct((strips, raw + count, queries_n), frame_two.dtype)
        return pl.pallas_call(
            functools.partial(corr_kernel, factor, tuple(len(part) for part in parts), True, slots, landing, len(pins)),
            out_shape=(out_type, pair_type),
            in_specs=[scalars] + [in_vmem] * len(operands) + [anywhere] * (1 + bool(landing) + len(pins)),
            out_specs=(anywhere, in_vmem),
            scratch_shapes=[
                pltpu.VMEM((strips, raw + count, queries_n), frame_two.dtype),
                pltpu.VMEM((raw + 2 * count, 2 * queries_n), jnp.float32),
                *pooling,
                pltpu.SemaphoreType.DMA((strips,)),
                pltpu.SemaphoreType.DMA((max(1, len(landing)),)),
            ],
            input_output_aliases={1 + len(operands) + bool(landing): 0},
            compiler_params=params,
            cost_estimate=modelled(cost),
            name="correlate",
        )(meta, *operands, *([landed] if landing else []), out, *pins)

    def product_type(strips, pixels):
        return jax.ShapeDtypeStruct((strips, pixels, queries_n), frame_two.dtype)

    def raw_rows(out, own, other, wide, landing=(), landed=None, cost=0, leavers=(), leaving=(), slots=(), pins=()):
        operands = [*own, *other, queries_wide if wide else queries]
        strips = sum(half.shape[0] for half in own)
        passive = ([landed] if landing else []) + list(leavers)
        pins = tuple(pins)
        return pl.pallas_call(
            functools.partial(raw_kernel, factor, (len(own), len(other)), wide, landing, leaving, slots, len(pins)),
            out_shape=(out_type,) + (product_type(strips, raw + count),) * (1 + wide),
            in_specs=[scalars] + [in_vmem] * len(operands) + [anywhere] * (1 + len(passive) + len(pins)),
            out_specs=(anywhere,) + (in_vmem,) * (1 + wide),
            scratch_shapes=[
                pltpu.VMEM((raw + count, queries_n * (1 + wide)), jnp.float32),
                *pooling,
                pltpu.SemaphoreType.DMA((max(1, len(landing)),)),
                pltpu.SemaphoreType.DMA((max(1, len(slots)),)),
            ],
            input_output_aliases={1 + len(operands) + len(passive): 0},
            compiler_params=params,
            cost_estimate=modelled(cost),
            name="raw_rows",
        )(meta, *operands, *passive, out, *pins)

    def came_rows(out, done, slots, own, other, wide, late=(), cost=0, pins=(), landing=()):
        operands = [*own, *other, queries_wide if wide else queries, *late[:1]]
        first = 1 + len(operands)
        inout = [out, done, *late[1:]]
        extra_types = (product_type(done.shape[0], count),) if wide else ()
        return pl.pallas_call(
            functools.partial(came_kernel, factor, (len(own), len(other)), wide, len(late) // 2, len(pins), slots, not G("NL"), landing),
            out_shape=tuple(jax.ShapeDtypeStruct(array.shape, array.dtype) for array in inout) + extra_types,
            in_specs=[scalars] + [in_vmem] * len(operands) + [anywhere] + [in_vmem] * (len(inout) - 1) + [anywhere] * len(pins),
            out_specs=(anywhere,) + (in_vmem,) * (len(inout) - 1 + wide),
            scratch_shapes=[
                pltpu.VMEM((count, queries_n), jnp.float32),
                pltpu.SemaphoreType.DMA((max(1, len(slots)),)),
                pltpu.SemaphoreType.DMA((max(1, len(landing)),)),
            ],
            input_output_aliases={first + index: index for index in range(len(inout))},
            compiler_params=params,
            cost_estimate=modelled(cost),
            name="came_rows",
        )(meta, *operands, *inout, *pins)

    def gate(out, pins, cost):
        handed = (out, *pins)
        return pl.pallas_call(
            gate_kernel,
            out_shape=tuple(jax.ShapeDtypeStruct(array.shape, array.dtype) for array in handed),
            in_specs=[anywhere] * len(handed),
            out_specs=(anywhere,) * len(handed),
            input_output_aliases={index: index for index in range(len(handed))},
            compiler_params=params,
            cost_estimate=modelled(cost),
            name="gate",
        )(*handed)

    mine = lax.dynamic_slice_in_dim(frame_two, side * half_rows, half_rows, axis=0)[None]
    theirs = lax.dynamic_slice_in_dim(frame_two, (1 - side) * half_rows, half_rows, axis=0)[None]
    if G("XQ"):
        sent = jnp.concatenate([theirs.reshape(raw, chans), frame_one], axis=0)
        got = lax.ppermute(sent, "chan", across)
        partner, queries_other = got[:raw].reshape(theirs.shape), got[raw:]
    else:
        partner = lax.ppermute(theirs, "chan", across)
        queries_other = lax.ppermute(frame_one, "chan", across)
    def all_queries(mine, theirs):
        own_core = jnp.concatenate([mine.T, theirs.T], axis=0)
        return own_core, jnp.concatenate([own_core, lax.ppermute(own_core, "rows", swap)], axis=1)

    if not G("QC"): queries, queries_wide = all_queries(frame_one, queries_other)

    def permute_rows(pairs, pieces):
        return [lax.ppermute(piece, "rows", pairs) for piece in pieces]

    def whole(pieces):
        return pieces if len(pieces) == 1 else [jnp.concatenate(pieces, axis=0)]

    came = {0: ([mine], [partner])}
    moving = [[half, *permute_rows(swap, [half])] for half in (mine, partner)]
    join = [G("JA"), G("JB")]
    for d in range(1, half_way + 1):
        if d == half_way:
            moving = [[pieces[0][:1]] for pieces in moving]
        if d == half_way - 1 and G("BSPL"):
            moving[1] = [moving[1][0][:1], moving[1][0][1:]]
        moving = [whole(pieces) if d == join[part] else pieces for part, pieces in enumerate(moving)]
        if d == 1:
            ring_first = moving[1][-1]
        moving = [permute_rows(ring, pieces) for pieces in moving]
        came[d] = tuple(moving)
    across_came = {}

    def do_extra(out, d, part, pin=None):
        pins = () if pin is None else tuple(across_came[pin]) if isinstance(pin, tuple) else (pin,)
        across_came[d, 1 - part] = []
        groups = [[piece] for piece in came[d][part]] if part and d == half_way - 1 else [came[d][part]]
        for pieces in groups:
            extra, out = make_extra(out, pieces, G(f"X{d}{part}"), pins)
            across_came[d, 1 - part].append(lax.ppermute(extra, "chan", across))
            pins = ()
        return out

    lag = G("LAG")
    waiting = []

    def landing(now):
        if waiting and waiting[0][0] <= now:
            return waiting.pop(0)[1:]
        return (), None

    def product(out, d, pins=(), now=None):
        out, pair = correlate(out, slots_of(d, 0), *came[d], across_came[d, 0], across_came[d, 1], *landing(d if now is None else now), G(f"C{d}"), pins)
        waiting.append((d + lag, slots_of(d, 1), permute_rows(swap, [pair])[0]))
        return out

    if G("QC"):
        extra, out, sent = make_extra(None, came[0][0], G("X00"), ({1: partner, 2: ring_first}[G("PINX")],) if G("PINX") else (), passed=frame_one)
        across_came[0, 1] = [lax.ppermute(extra, "chan", across)]
        queries, queries_wide = all_queries(frame_one, lax.ppermute(sent, "chan", across))
    else:
        out = do_extra(None, 0, 0, partner if G("PINX") else None)
    lacking, out = make_extra(out, [theirs], G("X01"), tuple(across_came[0, 1]) if G("PIN01") else (), flip=True)
    across_came[0, 0] = [lacking]
    near, far = half_way - 1, half_way

    def swap_one(piece):
        return permute_rows(swap, [piece])[0]

    def near_raw(out):
        return raw_rows(out, *came[near], True, *landing(near), G("F3"), pins=tuple(across_came[far, 1]) if G("PR") else ())

    swapped = []

    def far_extra(out, part, pins):
        extra, out, piece = make_extra(out, came[far][part], G(f"X4{part}"), pins, carry=True)
        came[far][part][0] = piece
        across_came[far, 1 - part] = [lax.ppermute(extra, "chan", across)]
        swapped.append(swap_one(piece))
        return out

    out = do_extra(out, 1, 0)
    out = do_extra(out, 2, 0, (1, 1))
    out = do_extra(out, 1, 1, (2, 1))
    out = product(out, 0)
    for d in range(3, far):
        out = do_extra(out, d, 0, (d - 2, 0))
        out = product(out, d - 2)
        out = do_extra(out, d - 1, 1, (d, 1))
    out = far_extra(out, 0, tuple(across_came[near - 1, 0]) if G("P4") else ())
    across_came[near, 0] = []
    groups = [came[near][1]] if G("ONEX") else [[piece] for piece in came[near][1]]
    for index, pieces in enumerate(groups):
        if index == len(groups) - G("CPOS"):
            out = product(out, near - 1, now=near)
        extra, out = make_extra(out, pieces, G("X31"), tuple(across_came[far, 1]) if G("P3") == index + 1 else ())
        across_came[near, 0].append(lax.ppermute(extra, "chan", across))
    out, near_done, near_pair = near_raw(out)
    out = far_extra(out, 1, (swapped[0],) if G("PS0") == 1 else ())
    near_late = swap_one(near_pair)
    pins = (tuple(across_came[far, 1]) if G("PE4") == 1 else ()) + ((swapped[0],) if G("PS0") == 2 else ())

    slots = slots_of(near, 1) + slots_of(far, 0) + slots_of(far, 1)

    landing_now, landed_now = landing(far) if G("LC") else ((), None)
    pins = ((landed_now,) if landing_now else ()) + pins
    out, near_done, near_rows = came_rows(
        out, near_done, (), across_came[near, 0], across_came[near, 1], True, cost=G("F2"), pins=pins, landing=landing_now
    )
    near_rows = swap_one(near_rows)
    out, far_done = raw_rows(
        out,
        [came[far][0][0], swapped[0]],
        [came[far][1][0], swapped[1]],
        False,
        *landing(far),
        G("F0"),
        (near_done, near_late),
        (True, False if G("NL") else None),
        slots_of(near, 0) + (slots if G("NL") else slots[len(slots_of(near, 1)) :]),
    )
    out, own, other = gate(out, [across_came[far, 0][0], across_came[far, 1][0]], G("GATE"))
    return came_rows(out, far_done, slots, [own, swap_one(own)], [other, swap_one(other)], False, (near_rows, near_late), G("F1"))[0]


def solution(mesh):
    rows_axis, groups = mesh.shape["rows"], mesh.shape["chan"]

    def local(frame_one, frame_two):
        rows_n, cols_n, chans = frame_two.shape
        ring = groups == 2 and rows_axis % 8 == 0 and rows_axis >= 16 and rows_n % 8 == 0 and cols_n % 32 == 0 and chans % LANES == 0
        return (ring_local if ring else gather_local)(frame_one, frame_two)

    in_specs = (P("rows", "chan"), P("rows", None, "chan"))
    out_specs = P(None, "chan", "rows")
    return jax.shard_map(local, mesh=mesh, in_specs=in_specs, out_specs=out_specs, check_vma=False)
```

```python
import functools

import jax
import jax.numpy as jnp
from jax import lax
from jax.experimental import pallas as pl
from jax.experimental.pallas import tpu as pltpu
from jax.sharding import PartitionSpec as P

LANES = 128
PARAMS = {'LAG': 2, 'F0': 10, 'F1': 0, 'PS0': 2, 'JA': 3, 'JB': 1, 'C0POS': 2, 'GATE': 30, 'F3': 0, 'F2': 22, 'NL': 1, 'PE4': 0, 'P4': 0, 'P3': 1, 'CPOS': 1, 'LC': 0, 'BSPL': 1, 'ONEX': 1, 'EL': 1, 'WH': 0, 'X00': 10, 'X01': 10, 'C0': 10, 'X10': 10, 'X11': 10, 'C1': 10, 'X20': 10, 'X21': 10, 'C2': 3, 'X30': 10, 'X31': 3, 'C3': 10, 'X40': 10, 'X41': 10, 'C4': 10}


def G(name):
    return PARAMS.get(name, 0)


VMEM_BYTES = 28 * 1024 * 1024


def pool_strip(strip):
    full = strip.astype(jnp.float32)
    rows_n, cols_n, chans = full.shape
    level_one = full.reshape(rows_n // 2, 2, cols_n // 2, 2, chans).mean(axis=(1, 3))
    level_two = level_one.reshape(rows_n // 4, 2, cols_n // 4, 2, chans).mean(axis=(1, 3))
    joined = jnp.concatenate(
        [full.reshape(-1, chans), level_one.reshape(-1, chans), level_two.reshape(-1, chans)],
        axis=0,
    )
    return joined.astype(jnp.bfloat16)


def gather_local(frame_one, frame_two):
    groups = lax.axis_size("chan")
    queries = lax.all_gather(frame_one, "chan", axis=0, tiled=False)
    channels = queries.shape[0] * queries.shape[2]
    factor = 1.0 / jnp.sqrt(jnp.float32(channels))
    pooled = pool_strip(frame_two)
    share = pooled.shape[0] // groups
    traded = lax.all_to_all(
        pooled.reshape(groups, share, pooled.shape[1]), "chan", split_axis=0, concat_axis=0, tiled=True
    )
    gathered = lax.all_gather(traded, "rows", axis=0, tiled=False)
    values = jnp.einsum("skpc,kqc->spq", gathered, queries, preferred_element_type=jnp.float32)
    return (values * factor).astype(jnp.bfloat16)


def pooled_levels(half, sums, sums_two):
    rows_n, cols_n, _ = half.shape
    means = []
    for row in range(rows_n // 2):
        sums[row] = half[2 * row].astype(jnp.float32) + half[2 * row + 1].astype(jnp.float32)
        left = sums[row, pl.ds(0, cols_n // 2, stride=2), :]
        right = sums[row, pl.ds(1, cols_n // 2, stride=2), :]
        means.append((left + right) * 0.25)
    means_two = []
    for row in range(rows_n // 4):
        sums_two[row] = means[2 * row] + means[2 * row + 1]
        left = sums_two[row, pl.ds(0, cols_n // 4, stride=2), :]
        right = sums_two[row, pl.ds(1, cols_n // 4, stride=2), :]
        means_two.append((left + right) * 0.25)
    return jnp.concatenate(means + means_two, axis=0)


def strips_in(refs):
    return [ref.at[index] for ref in refs for index in range(ref.shape[0])]


def extra_kernel(pieces, results, flip, meta, *refs):
    halves = strips_in(refs[:pieces])
    extra, sums, sums_two = refs[-2 - results], *refs[-2:]
    count, cols_n = extra.shape[1], halves[0].shape[1]
    upper = meta[0] == (1 if flip else 0)

    @pl.when(upper)
    def _():
        for index, half in enumerate(halves):
            extra[index] = pooled_levels(half, sums, sums_two).astype(extra.dtype)

    @pl.when(jnp.logical_not(upper))
    def _():
        for index, half in enumerate(halves):
            parts, left, row = [], count, 0
            while left > 0:
                parts.append(half[row].astype(jnp.float32)[: min(left, cols_n)])
                left, row = left - cols_n, row + 1
            extra[index] = jnp.concatenate(parts, axis=0).astype(extra.dtype)


def chunks(segments, step):
    todo, runs = list(segments), []
    while todo:
        run, room = [], step
        while todo and room > 0:
            ref, first, last = todo.pop(0)
            take = min(room, last - first)
            run.append((ref, first, first + take))
            room -= take
            if first + take < last:
                todo.insert(0, (ref, first + take, last))
        runs.append(run)
    return runs


def joined(run):
    parts = [ref[first:last].astype(jnp.float32) for ref, first, last in run]
    return parts[0] if len(parts) == 1 else jnp.concatenate(parts, axis=0)


def corr_kernel(factor, pieces, wide, slots, landing, pins, meta, *refs):
    own, other = strips_in(refs[: pieces[0]]), strips_in(refs[pieces[0] : sum(pieces[:2])])
    refs = refs[sum(pieces[:2]) :]
    came_own, came_other = strips_in(refs[: pieces[2]]), strips_in(refs[pieces[2] : pieces[2] + pieces[3]])
    queries, *refs = refs[pieces[2] + pieces[3] :]
    landed = refs.pop(0) if landing else None
    out, *refs = refs[1 + pins :]
    pair = refs.pop(0) if wide else None
    done, values, sums, sums_two, sems, land_sems = refs
    rows_n, cols_n, _ = own[0].shape
    count, width = came_own[0].shape[0], done.shape[2]
    raw = rows_n * cols_n
    ones = (rows_n // 2) * (cols_n // 2)

    copies = []
    for index, slot in enumerate(landing):
        copies.append(pltpu.make_async_copy(landed.at[index], out.at[meta[slot]], land_sems.at[index]))
        copies[-1].start()

    def times(left):
        return jnp.dot(left, queries[...], preferred_element_type=jnp.float32) * factor

    def store(index, at, part):
        done[index, at : at + part.shape[0]] = part[:, :width].astype(done.dtype)
        if wide:
            pair[index, at : at + part.shape[0]] = part[:, width:].astype(done.dtype)

    for index in range(len(own)):

        def raw_row(row):
            return jnp.concatenate([own[index][row], other[index][row]], axis=1)

        def came_rows():
            return jnp.concatenate([came_own[index][...], came_other[index][...]], axis=1)

        @pl.when(meta[0] == 0)
        def _():
            for row in range(rows_n):
                store(index, row * cols_n, times(raw_row(row)))
            store(index, raw, times(came_rows()))

        @pl.when(meta[0] != 0)
        def _():
            for row in range(count // cols_n, rows_n):
                values[row * cols_n : (row + 1) * cols_n] = times(raw_row(row))
            values[raw : raw + count] = times(came_rows())
            levels = [pooled_levels(half[index], sums, sums_two).astype(done.dtype) for half in (own, other)]
            lower = raw + count
            values[lower : lower + count] = times(jnp.concatenate(levels, axis=1))
            segments = [
                (values, count, raw),
                (values, raw, raw + ones),
                (values, lower, lower + ones),
                (values, raw + ones, raw + count),
                (values, lower + ones, lower + count),
            ]
            step = cols_n // 2
            for at, run in enumerate(chunks(segments, step)):
                store(index, at * step, joined(run))

        copies.append(pltpu.make_async_copy(done.at[index], out.at[meta[slots[index]]], sems.at[index]))
        copies[-1].start()
    for copy in copies:
        copy.wait()


def gate_kernel(*refs):
    pass


def first_open_row(total, raw):
    return (2 * raw - total) // 16 * 16


def raw_kernel(factor, arrays, wide, landing, leaving, slots, pins, meta, *refs):
    own, other = strips_in(refs[: arrays[0]]), strips_in(refs[arrays[0] : sum(arrays)])
    queries, *refs = refs[sum(arrays) :]
    landed = refs.pop(0) if landing else None
    leavers, refs = refs[: len(leaving)], refs[len(leaving) :]
    out, done, *refs = refs[1 + pins :]
    pair = refs.pop(0) if wide else None
    values, sums, sums_two, land_sems, sems = refs
    rows_n, cols_n, _ = own[0].shape
    count, width = done.shape[1] - rows_n * cols_n, done.shape[2]
    raw = rows_n * cols_n
    ones = (rows_n // 2) * (cols_n // 2)

    copies = []
    for index, slot in enumerate(landing):
        copies.append(pltpu.make_async_copy(landed.at[index], out.at[meta[slot]], land_sems.at[index]))
        copies[-1].start()
    total, cut = done.shape[1], first_open_row(done.shape[1], rows_n * cols_n)
    slots = list(slots)

    def leave(strip, part):
        rows = {"all": pl.ds(0, total), "settled": pl.ds(0, cut), "rest": pl.ds(cut, total - cut)}[part]
        number = len(copies) - len(landing)
        copies.append(pltpu.make_async_copy(strip.at[rows], out.at[meta[slots.pop(0)], rows], sems.at[number]))
        copies[-1].start()

    for strips, part in zip(leavers, leaving):
        for index in range(strips.shape[0] if part else 0):
            leave(strips.at[index], part)

    def times(left):
        return jnp.dot(left, queries[...], preferred_element_type=jnp.float32) * factor

    def store(index, at, part):
        done[index, at : at + part.shape[0]] = part[:, :width].astype(done.dtype)
        if wide:
            pair[index, at : at + part.shape[0]] = part[:, width:].astype(done.dtype)

    for index, halves in enumerate(zip(own, other)):

        def raw_row(row):
            return jnp.concatenate([half[row] for half in halves], axis=1)

        @pl.when(meta[0] == 0)
        def _():
            for row in range(rows_n):
                store(index, row * cols_n, times(raw_row(row)))
            store(index, raw, jnp.zeros((count, values.shape[1]), jnp.float32))

        @pl.when(meta[0] != 0)
        def _():
            for row in range(count // cols_n, rows_n):
                values[row * cols_n : (row + 1) * cols_n] = times(raw_row(row))
            levels = [pooled_levels(half, sums, sums_two).astype(done.dtype) for half in halves]
            values[raw : raw + count] = times(jnp.concatenate(levels, axis=1))
            segments = [
                (values, count, raw),
                (values, raw, raw + ones),
                (values, raw, raw + ones),
                (values, raw + ones, raw + count),
                (values, raw + ones, raw + count),
            ]
            step = cols_n // 2
            for at, run in enumerate(chunks(segments, step)):
                store(index, at * step, joined(run))

        if slots:
            leave(done.at[index], "settled")
    for copy in copies:
        copy.wait()


def came_kernel(factor, arrays, wide, late, pins, slots, late_whole, landing, meta, *refs):
    own, other = strips_in(refs[: arrays[0]]), strips_in(refs[arrays[0] : sum(arrays)])
    queries, *refs = refs[sum(arrays) :]
    late_rows = refs.pop(0) if late else None
    refs = refs[2 + late :]
    landed = refs[0] if landing else None
    refs = refs[pins:]
    out, done, *refs = refs
    late_done = refs.pop(0) if late else None
    pair = refs.pop(0) if wide else None
    values, sems, land_sems = refs
    count, width = own[0].shape[0], done.shape[2]
    raw = done.shape[1] - count
    ones = count * 4 // 5
    copies, landings = [], []
    for index, slot in enumerate(landing):
        landings.append(pltpu.make_async_copy(landed.at[index], out.at[meta[slot]], land_sems.at[index]))
        landings[-1].start()

    def leave(strip, whole=False):
        if slots:
            cut = 0 if whole else first_open_row(raw + count, raw)
            rows = pl.ds(cut, raw + count - cut)
            slot = meta[slots[len(copies)]]
            copies.append(pltpu.make_async_copy(strip.at[rows], out.at[slot, rows], sems.at[len(copies)]))
            copies[-1].start()

    def merge(strip, part):
        @pl.when(meta[0] == 0)
        def _():
            strip[raw : raw + count] = part.astype(done.dtype)

        @pl.when(meta[0] != 0)
        def _():
            values[...] = part
            at = raw - count
            for first, last, into in ((0, ones, at), (ones, count, at + 2 * ones)):
                start = into // 16 * 16
                end = -(-(into + last - first) // 16) * 16
                parts = [values[first:last]]
                if start < into:
                    parts.insert(0, strip[start : start + 16].astype(jnp.float32)[: into - start])
                over = end - (into + last - first)
                if over:
                    parts.append(strip[end - 16 : end].astype(jnp.float32)[16 - over :])
                strip[start:end] = jnp.concatenate(parts, axis=0).astype(done.dtype)

    if late:
        for index in range(late_done.shape[0]):
            merge(late_done.at[index], late_rows[index].astype(jnp.float32))
            leave(late_done.at[index], late_whole)
    for index, halves in enumerate(zip(own, other)):
        left = jnp.concatenate([half[...] for half in halves], axis=1)
        part = jnp.dot(left, queries[...], preferred_element_type=jnp.float32) * factor
        if wide:
            pair[index] = part[:, width:].astype(done.dtype)
        merge(done.at[index], part[:, :width])
        leave(done.at[index])
    for copy in copies + landings:
        copy.wait()


def ring_local(frame_one, frame_two):
    rows_axis = lax.axis_size("rows")
    rows_n, cols_n, chans = frame_two.shape
    queries_n = frame_one.shape[0]
    half_rows = rows_n // 2
    raw = half_rows * cols_n
    count = (half_rows // 2) * (cols_n // 2) + (half_rows // 4) * (cols_n // 4)
    factor = float(1.0 / (2 * chans) ** 0.5)
    me, side = lax.axis_index("rows"), lax.axis_index("chan")

    chips = rows_axis // 2
    columns, half_way = chips // 2, chips // 2
    order = [2 * z for z in range(columns)] + [2 * z + 1 for z in reversed(range(columns))]
    ring = [(2 * order[p], 2 * order[(p + 1) % chips]) for p in range(chips)]
    ring += [(2 * order[p] + 1, 2 * order[p - 1] + 1) for p in range(chips)]
    swap = [(r, r ^ 1) for r in range(rows_axis)]
    across = [(0, 1), (1, 0)]

    core, column, line = me % 2, me // 4, (me // 2) % 2
    place = jnp.where(line == 0, column, chips - 1 - column)
    steps = jnp.arange(half_way + 1, dtype=jnp.int32)

    def strips_of(c):
        p = (place + jnp.where(c == 0, -steps, steps)) % chips
        chip = jnp.where(p < columns, 2 * p, 2 * (chips - 1 - p) + 1)
        return [2 * chip + c, 2 * chip + 1 - c]

    meta = jnp.concatenate([side[None], *strips_of(core), *strips_of(1 - core)]).astype(jnp.int32)

    def slots_of(d, other_core):
        first = 1 + (2 * other_core) * (half_way + 1) + d
        return (first,) if d in (0, half_way) else (first, first + half_way + 1)

    in_vmem = pl.BlockSpec(memory_space=pltpu.VMEM)
    anywhere = pl.BlockSpec(memory_space=pl.ANY)
    scalars = pl.BlockSpec(memory_space=pltpu.SMEM)
    out_type = jax.ShapeDtypeStruct((rows_axis, raw + count, queries_n), frame_two.dtype)
    pooling = [
        pltpu.VMEM((half_rows // 2, cols_n, chans), jnp.float32),
        pltpu.VMEM((half_rows // 4, cols_n // 2, chans), jnp.float32),
    ]
    params = pltpu.CompilerParams(vmem_limit_bytes=VMEM_BYTES)
    def modelled(us):
        return pl.CostEstimate(flops=int(us * 10**9) + 1000, bytes_accessed=1000, transcendentals=0)


    def make_extra(out, halves, cost=0, pins=(), flip=False, carry=False, passed=None):
        strips = sum(half.shape[0] for half in halves)
        handed = () if out is None else (out,)
        carried = tuple(halves) if carry else ()
        aliases = {1 + len(halves): 1} if handed else {}
        aliases.update({1 + index: 2 + index for index in range(len(carried))})
        if passed is not None:
            pins, carried = (passed, *pins), (passed,)
            aliases[1 + len(halves) + len(handed)] = 2
        return pl.pallas_call(
            functools.partial(extra_kernel, len(halves), 2 + len(carried), flip),
            out_shape=(jax.ShapeDtypeStruct((strips, count, chans), frame_two.dtype), out_type)
            + tuple(jax.ShapeDtypeStruct(half.shape, half.dtype) for half in carried),
            in_specs=[scalars] + [in_vmem] * len(halves) + [anywhere] * len(handed + pins),
            out_specs=(in_vmem, anywhere) + (in_vmem if carry else anywhere,) * len(carried),
            scratch_shapes=pooling,
            input_output_aliases=aliases,
            compiler_params=params,
            cost_estimate=modelled(cost),
            name="extra",
        )(meta, *halves, *handed, *pins)

    def correlate(out, slots, own, other, came_own, came_other, landing=(), landed=None, cost=0, pins=()):
        parts = (own, other, came_own, came_other)
        strips = sum(piece.shape[0] for piece in own)
        operands = [*own, *other, *came_own, *came_other, queries_wide]
        pair_type = jax.ShapeDtypeStruct((strips, raw + count, queries_n), frame_two.dtype)
        return pl.pallas_call(
            functools.partial(corr_kernel, factor, tuple(len(part) for part in parts), True, slots, landing, len(pins)),
            out_shape=(out_type, pair_type),
            in_specs=[scalars] + [in_vmem] * len(operands) + [anywhere] * (1 + bool(landing) + len(pins)),
            out_specs=(anywhere, in_vmem),
            scratch_shapes=[
                pltpu.VMEM((strips, raw + count, queries_n), frame_two.dtype),
                pltpu.VMEM((raw + 2 * count, 2 * queries_n), jnp.float32),
                *pooling,
                pltpu.SemaphoreType.DMA((strips,)),
                pltpu.SemaphoreType.DMA((max(1, len(landing)),)),
            ],
            input_output_aliases={1 + len(operands) + bool(landing): 0},
            compiler_params=params,
            cost_estimate=modelled(cost),
            name="correlate",
        )(meta, *operands, *([landed] if landing else []), out, *pins)

    def product_type(strips, pixels):
        return jax.ShapeDtypeStruct((strips, pixels, queries_n), frame_two.dtype)

    def raw_rows(out, own, other, wide, landing=(), landed=None, cost=0, leavers=(), leaving=(), slots=(), pins=()):
        operands = [*own, *other, queries_wide if wide else queries]
        strips = sum(half.shape[0] for half in own)
        passive = ([landed] if landing else []) + list(leavers)
        pins = tuple(pins)
        return pl.pallas_call(
            functools.partial(raw_kernel, factor, (len(own), len(other)), wide, landing, leaving, slots, len(pins)),
            out_shape=(out_type,) + (product_type(strips, raw + count),) * (1 + wide),
            in_specs=[scalars] + [in_vmem] * len(operands) + [anywhere] * (1 + len(passive) + len(pins)),
            out_specs=(anywhere,) + (in_vmem,) * (1 + wide),
            scratch_shapes=[
                pltpu.VMEM((raw + count, queries_n * (1 + wide)), jnp.float32),
                *pooling,
                pltpu.SemaphoreType.DMA((max(1, len(landing)),)),
                pltpu.SemaphoreType.DMA((max(1, len(slots)),)),
            ],
            input_output_aliases={1 + len(operands) + len(passive): 0},
            compiler_params=params,
            cost_estimate=modelled(cost),
            name="raw_rows",
        )(meta, *operands, *passive, out, *pins)

    def came_rows(out, done, slots, own, other, wide, late=(), cost=0, pins=(), landing=()):
        operands = [*own, *other, queries_wide if wide else queries, *late[:1]]
        first = 1 + len(operands)
        inout = [out, done, *late[1:]]
        extra_types = (product_type(done.shape[0], count),) if wide else ()
        return pl.pallas_call(
            functools.partial(came_kernel, factor, (len(own), len(other)), wide, len(late) // 2, len(pins), slots, not G("NL"), landing),
            out_shape=tuple(jax.ShapeDtypeStruct(array.shape, array.dtype) for array in inout) + extra_types,
            in_specs=[scalars] + [in_vmem] * len(operands) + [anywhere] + [in_vmem] * (len(inout) - 1) + [anywhere] * len(pins),
            out_specs=(anywhere,) + (in_vmem,) * (len(inout) - 1 + wide),
            scratch_shapes=[
                pltpu.VMEM((count, queries_n), jnp.float32),
                pltpu.SemaphoreType.DMA((max(1, len(slots)),)),
                pltpu.SemaphoreType.DMA((max(1, len(landing)),)),
            ],
            input_output_aliases={first + index: index for index in range(len(inout))},
            compiler_params=params,
            cost_estimate=modelled(cost),
            name="came_rows",
        )(meta, *operands, *inout, *pins)

    def gate(out, pins, cost):
        handed = (out, *pins)
        return pl.pallas_call(
            gate_kernel,
            out_shape=tuple(jax.ShapeDtypeStruct(array.shape, array.dtype) for array in handed),
            in_specs=[anywhere] * len(handed),
            out_specs=(anywhere,) * len(handed),
            input_output_aliases={index: index for index in range(len(handed))},
            compiler_params=params,
            cost_estimate=modelled(cost),
            name="gate",
        )(*handed)

    mine = lax.dynamic_slice_in_dim(frame_two, side * half_rows, half_rows, axis=0)[None]
    theirs = lax.dynamic_slice_in_dim(frame_two, (1 - side) * half_rows, half_rows, axis=0)[None]
    if G("WH"):
        theirs = jnp.where(side == 0, frame_two[half_rows:], frame_two[:half_rows])[None]
    if G("XQ"):
        sent = jnp.concatenate([theirs.reshape(raw, chans), frame_one], axis=0)
        got = lax.ppermute(sent, "chan", across)
        partner, queries_other = got[:raw].reshape(theirs.shape), got[raw:]
    else:
        partner = lax.ppermute(theirs, "chan", across)
        queries_other = lax.ppermute(frame_one, "chan", across)
    def all_queries(mine, theirs):
        own_core = jnp.concatenate([mine.T, theirs.T], axis=0)
        return own_core, jnp.concatenate([own_core, lax.ppermute(own_core, "rows", swap)], axis=1)

    if not G("QC"): queries, queries_wide = all_queries(frame_one, queries_other)

    def permute_rows(pairs, pieces):
        return [lax.ppermute(piece, "rows", pairs) for piece in pieces]

    def whole(pieces):
        return pieces if len(pieces) == 1 else [jnp.concatenate(pieces, axis=0)]

    came = {0: ([mine], [partner])}
    moving = [[half, *permute_rows(swap, [half])] for half in (mine, partner)]
    join = [G("JA"), G("JB")]
    for d in range(1, half_way + 1):
        if d == half_way:
            moving = [[pieces[0][:1]] for pieces in moving]
        if d == half_way - 1 and G("BSPL"):
            moving[1] = [moving[1][0][:1], moving[1][0][1:]]
        moving = [whole(pieces) if d == join[part] else pieces for part, pieces in enumerate(moving)]
        if d == 1:
            ring_first = moving[1][-1]
        moving = [permute_rows(ring, pieces) for pieces in moving]
        came[d] = tuple(moving)
    across_came = {}

    def do_extra(out, d, part, pin=None):
        pins = () if pin is None else tuple(across_came[pin]) if isinstance(pin, tuple) else (pin,)
        across_came[d, 1 - part] = []
        groups = [[piece] for piece in came[d][part]] if part and d == half_way - 1 else [came[d][part]]
        for pieces in groups:
            extra, out = make_extra(out, pieces, G(f"X{d}{part}"), pins)
            across_came[d, 1 - part].append(lax.ppermute(extra, "chan", across))
            pins = ()
        return out

    lag = G("LAG")
    waiting = []

    def landing(now):
        if waiting and waiting[0][0] <= now:
            return waiting.pop(0)[1:]
        return (), None

    def product(out, d, pins=(), now=None):
        out, pair = correlate(out, slots_of(d, 0), *came[d], across_came[d, 0], across_came[d, 1], *landing(d if now is None else now), G(f"C{d}"), pins)
        waiting.append((d + lag, slots_of(d, 1), permute_rows(swap, [pair])[0]))
        return out

    if G("QC"):
        extra, out, sent = make_extra(None, came[0][0], G("X00"), ({1: partner, 2: ring_first}[G("PINX")],) if G("PINX") else (), passed=frame_one)
        across_came[0, 1] = [lax.ppermute(extra, "chan", across)]
        queries, queries_wide = all_queries(frame_one, lax.ppermute(sent, "chan", across))
    else:
        out = do_extra(None, 0, 0, partner if G("PINX") else None)
    lacking, out = make_extra(out, [theirs], G("X01"), tuple(across_came[0, 1]) if G("PIN01") else (), flip=True)
    across_came[0, 0] = [lacking]
    near, far = half_way - 1, half_way

    def swap_one(piece):
        return permute_rows(swap, [piece])[0]

    def near_raw(out):
        return raw_rows(out, *came[near], True, *landing(near), G("F3"), slots=slots_of(near, 0) if G("EL") else (), pins=tuple(across_came[far, 1]) if G("PR") else ())

    swapped = []

    def far_extra(out, part, pins):
        extra, out, piece = make_extra(out, came[far][part], G(f"X4{part}"), pins, carry=True)
        came[far][part][0] = piece
        across_came[far, 1 - part] = [lax.ppermute(extra, "chan", across)]
        swapped.append(swap_one(piece))
        return out

    out = do_extra(out, 1, 0)
    out = do_extra(out, 2, 0, (1, 1))
    out = do_extra(out, 1, 1, (2, 1))
    out = product(out, 0)
    for d in range(3, far):
        out = do_extra(out, d, 0, (d - 2, 0))
        out = product(out, d - 2)
        out = do_extra(out, d - 1, 1, (d, 1))
    out = far_extra(out, 0, tuple(across_came[near - 1, 0]) if G("P4") else ())
    across_came[near, 0] = []
    groups = [came[near][1]] if G("ONEX") else [[piece] for piece in came[near][1]]
    for index, pieces in enumerate(groups):
        if index == len(groups) - G("CPOS"):
            out = product(out, near - 1, now=near)
        extra, out = make_extra(out, pieces, G("X31"), tuple(across_came[far, 1]) if G("P3") == index + 1 else ())
        across_came[near, 0].append(lax.ppermute(extra, "chan", across))
    out, near_done, near_pair = near_raw(out)
    out = far_extra(out, 1, (swapped[0],) if G("PS0") == 1 else ())
    near_late = swap_one(near_pair)
    pins = (tuple(across_came[far, 1]) if G("PE4") == 1 else ()) + ((swapped[0],) if G("PS0") == 2 else ())

    slots = slots_of(near, 1) + slots_of(far, 0) + slots_of(far, 1)

    landing_now, landed_now = landing(far) if G("LC") else ((), None)
    pins = ((landed_now,) if landing_now else ()) + pins
    out, near_done, near_rows = came_rows(
        out, near_done, (), across_came[near, 0], across_came[near, 1], True, cost=G("F2"), pins=pins, landing=landing_now
    )
    near_rows = swap_one(near_rows)
    out, far_done = raw_rows(
        out,
        [came[far][0][0], swapped[0]],
        [came[far][1][0], swapped[1]],
        False,
        *landing(far),
        G("F0"),
        (near_done, near_late),
        ("rest" if G("EL") else "all", "settled" if G("NL") else None),
        slots_of(near, 0) + (slots if G("NL") else slots[len(slots_of(near, 1)) :]),
    )
    out, own, other = gate(out, [across_came[far, 0][0], across_came[far, 1][0]], G("GATE"))
    return came_rows(out, far_done, slots, [own, swap_one(own)], [other, swap_one(other)], False, (near_rows, near_late), G("F1"))[0]


def solution(mesh):
    rows_axis, groups = mesh.shape["rows"], mesh.shape["chan"]

    def local(frame_one, frame_two):
        rows_n, cols_n, chans = frame_two.shape
        ring = groups == 2 and rows_axis % 8 == 0 and rows_axis >= 16 and rows_n % 8 == 0 and cols_n % 32 == 0 and chans % LANES == 0
        return (ring_local if ring else gather_local)(frame_one, frame_two)

    in_specs = (P("rows", "chan"), P("rows", None, "chan"))
    out_specs = P(None, "chan", "rows")
    return jax.shard_map(local, mesh=mesh, in_specs=in_specs, out_specs=out_specs, check_vma=False)
```

```python
import functools

import jax
import jax.numpy as jnp
from jax import lax
from jax.experimental import pallas as pl
from jax.experimental.pallas import tpu as pltpu
from jax.sharding import PartitionSpec as P

LANES = 128
PARAMS = {'LAG': 2, 'F0': 10, 'F1': 0, 'PS0': 2, 'JA': 3, 'JB': 1, 'C0POS': 2, 'GATE': 30, 'F3': 0, 'F2': 22, 'NL': 1, 'PE4': 0, 'P4': 0, 'P3': 1, 'CPOS': 1, 'LC': 1, 'BSPL': 1, 'ONEX': 1, 'EL': 1, 'WH': 0, 'X00': 10, 'X01': 10, 'C0': 10, 'X10': 10, 'X11': 10, 'C1': 10, 'X20': 10, 'X21': 10, 'C2': 3, 'X30': 10, 'X31': 3, 'C3': 10, 'X40': 10, 'X41': 24, 'C4': 10}


def G(name):
    return PARAMS.get(name, 0)


VMEM_BYTES = 28 * 1024 * 1024


def pool_strip(strip):
    full = strip.astype(jnp.float32)
    rows_n, cols_n, chans = full.shape
    level_one = full.reshape(rows_n // 2, 2, cols_n // 2, 2, chans).mean(axis=(1, 3))
    level_two = level_one.reshape(rows_n // 4, 2, cols_n // 4, 2, chans).mean(axis=(1, 3))
    joined = jnp.concatenate(
        [full.reshape(-1, chans), level_one.reshape(-1, chans), level_two.reshape(-1, chans)],
        axis=0,
    )
    return joined.astype(jnp.bfloat16)


def gather_local(frame_one, frame_two):
    groups = lax.axis_size("chan")
    queries = lax.all_gather(frame_one, "chan", axis=0, tiled=False)
    channels = queries.shape[0] * queries.shape[2]
    factor = 1.0 / jnp.sqrt(jnp.float32(channels))
    pooled = pool_strip(frame_two)
    share = pooled.shape[0] // groups
    traded = lax.all_to_all(
        pooled.reshape(groups, share, pooled.shape[1]), "chan", split_axis=0, concat_axis=0, tiled=True
    )
    gathered = lax.all_gather(traded, "rows", axis=0, tiled=False)
    values = jnp.einsum("skpc,kqc->spq", gathered, queries, preferred_element_type=jnp.float32)
    return (values * factor).astype(jnp.bfloat16)


def pooled_levels(half, sums, sums_two):
    rows_n, cols_n, _ = half.shape
    means = []
    for row in range(rows_n // 2):
        sums[row] = half[2 * row].astype(jnp.float32) + half[2 * row + 1].astype(jnp.float32)
        left = sums[row, pl.ds(0, cols_n // 2, stride=2), :]
        right = sums[row, pl.ds(1, cols_n // 2, stride=2), :]
        means.append((left + right) * 0.25)
    means_two = []
    for row in range(rows_n // 4):
        sums_two[row] = means[2 * row] + means[2 * row + 1]
        left = sums_two[row, pl.ds(0, cols_n // 4, stride=2), :]
        right = sums_two[row, pl.ds(1, cols_n // 4, stride=2), :]
        means_two.append((left + right) * 0.25)
    return jnp.concatenate(means + means_two, axis=0)


def strips_in(refs):
    return [ref.at[index] for ref in refs for index in range(ref.shape[0])]


def extra_kernel(pieces, results, flip, meta, *refs):
    halves = strips_in(refs[:pieces])
    extra, sums, sums_two = refs[-2 - results], *refs[-2:]
    count, cols_n = extra.shape[1], halves[0].shape[1]
    upper = meta[0] == (1 if flip else 0)

    @pl.when(upper)
    def _():
        for index, half in enumerate(halves):
            extra[index] = pooled_levels(half, sums, sums_two).astype(extra.dtype)

    @pl.when(jnp.logical_not(upper))
    def _():
        for index, half in enumerate(halves):
            parts, left, row = [], count, 0
            while left > 0:
                parts.append(half[row].astype(jnp.float32)[: min(left, cols_n)])
                left, row = left - cols_n, row + 1
            extra[index] = jnp.concatenate(parts, axis=0).astype(extra.dtype)


def chunks(segments, step):
    todo, runs = list(segments), []
    while todo:
        run, room = [], step
        while todo and room > 0:
            ref, first, last = todo.pop(0)
            take = min(room, last - first)
            run.append((ref, first, first + take))
            room -= take
            if first + take < last:
                todo.insert(0, (ref, first + take, last))
        runs.append(run)
    return runs


def joined(run):
    parts = [ref[first:last].astype(jnp.float32) for ref, first, last in run]
    return parts[0] if len(parts) == 1 else jnp.concatenate(parts, axis=0)


def corr_kernel(factor, pieces, wide, slots, landing, pins, meta, *refs):
    own, other = strips_in(refs[: pieces[0]]), strips_in(refs[pieces[0] : sum(pieces[:2])])
    refs = refs[sum(pieces[:2]) :]
    came_own, came_other = strips_in(refs[: pieces[2]]), strips_in(refs[pieces[2] : pieces[2] + pieces[3]])
    queries, *refs = refs[pieces[2] + pieces[3] :]
    landed = refs.pop(0) if landing else None
    out, *refs = refs[1 + pins :]
    pair = refs.pop(0) if wide else None
    done, values, sums, sums_two, sems, land_sems = refs
    rows_n, cols_n, _ = own[0].shape
    count, width = came_own[0].shape[0], done.shape[2]
    raw = rows_n * cols_n
    ones = (rows_n // 2) * (cols_n // 2)

    copies = []
    for index, slot in enumerate(landing):
        copies.append(pltpu.make_async_copy(landed.at[index], out.at[meta[slot]], land_sems.at[index]))
        copies[-1].start()

    def times(left):
        return jnp.dot(left, queries[...], preferred_element_type=jnp.float32) * factor

    def store(index, at, part):
        done[index, at : at + part.shape[0]] = part[:, :width].astype(done.dtype)
        if wide:
            pair[index, at : at + part.shape[0]] = part[:, width:].astype(done.dtype)

    for index in range(len(own)):

        def raw_row(row):
            return jnp.concatenate([own[index][row], other[index][row]], axis=1)

        def came_rows():
            return jnp.concatenate([came_own[index][...], came_other[index][...]], axis=1)

        @pl.when(meta[0] == 0)
        def _():
            for row in range(rows_n):
                store(index, row * cols_n, times(raw_row(row)))
            store(index, raw, times(came_rows()))

        @pl.when(meta[0] != 0)
        def _():
            for row in range(count // cols_n, rows_n):
                values[row * cols_n : (row + 1) * cols_n] = times(raw_row(row))
            values[raw : raw + count] = times(came_rows())
            levels = [pooled_levels(half[index], sums, sums_two).astype(done.dtype) for half in (own, other)]
            lower = raw + count
            values[lower : lower + count] = times(jnp.concatenate(levels, axis=1))
            segments = [
                (values, count, raw),
                (values, raw, raw + ones),
                (values, lower, lower + ones),
                (values, raw + ones, raw + count),
                (values, lower + ones, lower + count),
            ]
            step = cols_n // 2
            for at, run in enumerate(chunks(segments, step)):
                store(index, at * step, joined(run))

        copies.append(pltpu.make_async_copy(done.at[index], out.at[meta[slots[index]]], sems.at[index]))
        copies[-1].start()
    for copy in copies:
        copy.wait()


def gate_kernel(*refs):
    pass


def first_open_row(total, raw):
    return (2 * raw - total) // 16 * 16


def raw_kernel(factor, arrays, wide, landing, leaving, slots, pins, meta, *refs):
    own, other = strips_in(refs[: arrays[0]]), strips_in(refs[arrays[0] : sum(arrays)])
    queries, *refs = refs[sum(arrays) :]
    landed = refs.pop(0) if landing else None
    leavers, refs = refs[: len(leaving)], refs[len(leaving) :]
    out, done, *refs = refs[1 + pins :]
    pair = refs.pop(0) if wide else None
    values, sums, sums_two, land_sems, sems = refs
    rows_n, cols_n, _ = own[0].shape
    count, width = done.shape[1] - rows_n * cols_n, done.shape[2]
    raw = rows_n * cols_n
    ones = (rows_n // 2) * (cols_n // 2)

    copies = []
    for index, slot in enumerate(landing):
        copies.append(pltpu.make_async_copy(landed.at[index], out.at[meta[slot]], land_sems.at[index]))
        copies[-1].start()
    total, cut = done.shape[1], first_open_row(done.shape[1], rows_n * cols_n)
    slots = list(slots)

    def leave(strip, part):
        rows = {"all": pl.ds(0, total), "settled": pl.ds(0, cut), "rest": pl.ds(cut, total - cut)}[part]
        number = len(copies) - len(landing)
        copies.append(pltpu.make_async_copy(strip.at[rows], out.at[meta[slots.pop(0)], rows], sems.at[number]))
        copies[-1].start()

    for strips, part in zip(leavers, leaving):
        for index in range(strips.shape[0] if part else 0):
            leave(strips.at[index], part)

    def times(left):
        return jnp.dot(left, queries[...], preferred_element_type=jnp.float32) * factor

    def store(index, at, part):
        done[index, at : at + part.shape[0]] = part[:, :width].astype(done.dtype)
        if wide:
            pair[index, at : at + part.shape[0]] = part[:, width:].astype(done.dtype)

    for index, halves in enumerate(zip(own, other)):

        def raw_row(row):
            return jnp.concatenate([half[row] for half in halves], axis=1)

        @pl.when(meta[0] == 0)
        def _():
            for row in range(rows_n):
                store(index, row * cols_n, times(raw_row(row)))
            store(index, raw, jnp.zeros((count, values.shape[1]), jnp.float32))

        @pl.when(meta[0] != 0)
        def _():
            for row in range(count // cols_n, rows_n):
                values[row * cols_n : (row + 1) * cols_n] = times(raw_row(row))
            levels = [pooled_levels(half, sums, sums_two).astype(done.dtype) for half in halves]
            values[raw : raw + count] = times(jnp.concatenate(levels, axis=1))
            segments = [
                (values, count, raw),
                (values, raw, raw + ones),
                (values, raw, raw + ones),
                (values, raw + ones, raw + count),
                (values, raw + ones, raw + count),
            ]
            step = cols_n // 2
            for at, run in enumerate(chunks(segments, step)):
                store(index, at * step, joined(run))

        if slots:
            leave(done.at[index], "settled")
    for copy in copies:
        copy.wait()


def came_kernel(factor, arrays, wide, late, pins, slots, late_whole, landing, meta, *refs):
    own, other = strips_in(refs[: arrays[0]]), strips_in(refs[arrays[0] : sum(arrays)])
    queries, *refs = refs[sum(arrays) :]
    late_rows = refs.pop(0) if late else None
    refs = refs[2 + late :]
    landed = refs[0] if landing else None
    refs = refs[pins:]
    out, done, *refs = refs
    late_done = refs.pop(0) if late else None
    pair = refs.pop(0) if wide else None
    values, sems, land_sems = refs
    count, width = own[0].shape[0], done.shape[2]
    raw = done.shape[1] - count
    ones = count * 4 // 5
    copies, landings = [], []
    for index, slot in enumerate(landing):
        landings.append(pltpu.make_async_copy(landed.at[index], out.at[meta[slot]], land_sems.at[index]))
        landings[-1].start()

    def leave(strip, whole=False):
        if slots:
            cut = 0 if whole else first_open_row(raw + count, raw)
            rows = pl.ds(cut, raw + count - cut)
            slot = meta[slots[len(copies)]]
            copies.append(pltpu.make_async_copy(strip.at[rows], out.at[slot, rows], sems.at[len(copies)]))
            copies[-1].start()

    def merge(strip, part):
        @pl.when(meta[0] == 0)
        def _():
            strip[raw : raw + count] = part.astype(done.dtype)

        @pl.when(meta[0] != 0)
        def _():
            values[...] = part
            at = raw - count
            for first, last, into in ((0, ones, at), (ones, count, at + 2 * ones)):
                start = into // 16 * 16
                end = -(-(into + last - first) // 16) * 16
                parts = [values[first:last]]
                if start < into:
                    parts.insert(0, strip[start : start + 16].astype(jnp.float32)[: into - start])
                over = end - (into + last - first)
                if over:
                    parts.append(strip[end - 16 : end].astype(jnp.float32)[16 - over :])
                strip[start:end] = jnp.concatenate(parts, axis=0).astype(done.dtype)

    if late:
        for index in range(late_done.shape[0]):
            merge(late_done.at[index], late_rows[index].astype(jnp.float32))
            leave(late_done.at[index], late_whole)
    for index, halves in enumerate(zip(own, other)):
        left = jnp.concatenate([half[...] for half in halves], axis=1)
        part = jnp.dot(left, queries[...], preferred_element_type=jnp.float32) * factor
        if wide:
            pair[index] = part[:, width:].astype(done.dtype)
        merge(done.at[index], part[:, :width])
        leave(done.at[index])
    for copy in copies + landings:
        copy.wait()


def ring_local(frame_one, frame_two):
    rows_axis = lax.axis_size("rows")
    rows_n, cols_n, chans = frame_two.shape
    queries_n = frame_one.shape[0]
    half_rows = rows_n // 2
    raw = half_rows * cols_n
    count = (half_rows // 2) * (cols_n // 2) + (half_rows // 4) * (cols_n // 4)
    factor = float(1.0 / (2 * chans) ** 0.5)
    me, side = lax.axis_index("rows"), lax.axis_index("chan")

    chips = rows_axis // 2
    columns, half_way = chips // 2, chips // 2
    order = [2 * z for z in range(columns)] + [2 * z + 1 for z in reversed(range(columns))]
    ring = [(2 * order[p], 2 * order[(p + 1) % chips]) for p in range(chips)]
    ring += [(2 * order[p] + 1, 2 * order[p - 1] + 1) for p in range(chips)]
    swap = [(r, r ^ 1) for r in range(rows_axis)]
    across = [(0, 1), (1, 0)]

    core, column, line = me % 2, me // 4, (me // 2) % 2
    place = jnp.where(line == 0, column, chips - 1 - column)
    steps = jnp.arange(half_way + 1, dtype=jnp.int32)

    def strips_of(c):
        p = (place + jnp.where(c == 0, -steps, steps)) % chips
        chip = jnp.where(p < columns, 2 * p, 2 * (chips - 1 - p) + 1)
        return [2 * chip + c, 2 * chip + 1 - c]

    meta = jnp.concatenate([side[None], *strips_of(core), *strips_of(1 - core)]).astype(jnp.int32)

    def slots_of(d, other_core):
        first = 1 + (2 * other_core) * (half_way + 1) + d
        return (first,) if d in (0, half_way) else (first, first + half_way + 1)

    in_vmem = pl.BlockSpec(memory_space=pltpu.VMEM)
    anywhere = pl.BlockSpec(memory_space=pl.ANY)
    scalars = pl.BlockSpec(memory_space=pltpu.SMEM)
    out_type = jax.ShapeDtypeStruct((rows_axis, raw + count, queries_n), frame_two.dtype)
    pooling = [
        pltpu.VMEM((half_rows // 2, cols_n, chans), jnp.float32),
        pltpu.VMEM((half_rows // 4, cols_n // 2, chans), jnp.float32),
    ]
    params = pltpu.CompilerParams(vmem_limit_bytes=VMEM_BYTES)
    def modelled(us):
        return pl.CostEstimate(flops=int(us * 10**9) + 1000, bytes_accessed=1000, transcendentals=0)


    def make_extra(out, halves, cost=0, pins=(), flip=False, carry=False, passed=None):
        strips = sum(half.shape[0] for half in halves)
        handed = () if out is None else (out,)
        carried = tuple(halves) if carry else ()
        aliases = {1 + len(halves): 1} if handed else {}
        aliases.update({1 + index: 2 + index for index in range(len(carried))})
        if passed is not None:
            pins, carried = (passed, *pins), (passed,)
            aliases[1 + len(halves) + len(handed)] = 2
        return pl.pallas_call(
            functools.partial(extra_kernel, len(halves), 2 + len(carried), flip),
            out_shape=(jax.ShapeDtypeStruct((strips, count, chans), frame_two.dtype), out_type)
            + tuple(jax.ShapeDtypeStruct(half.shape, half.dtype) for half in carried),
            in_specs=[scalars] + [in_vmem] * len(halves) + [anywhere] * len(handed + pins),
            out_specs=(in_vmem, anywhere) + (in_vmem if carry else anywhere,) * len(carried),
            scratch_shapes=pooling,
            input_output_aliases=aliases,
            compiler_params=params,
            cost_estimate=modelled(cost),
            name="extra",
        )(meta, *halves, *handed, *pins)

    def correlate(out, slots, own, other, came_own, came_other, landing=(), landed=None, cost=0, pins=()):
        parts = (own, other, came_own, came_other)
        strips = sum(piece.shape[0] for piece in own)
        operands = [*own, *other, *came_own, *came_other, queries_wide]
        pair_type = jax.ShapeDtypeStruct((strips, raw + count, queries_n), frame_two.dtype)
        return pl.pallas_call(
            functools.partial(corr_kernel, factor, tuple(len(part) for part in parts), True, slots, landing, len(pins)),
            out_shape=(out_type, pair_type),
            in_specs=[scalars] + [in_vmem] * len(operands) + [anywhere] * (1 + bool(landing) + len(pins)),
            out_specs=(anywhere, in_vmem),
            scratch_shapes=[
                pltpu.VMEM((strips, raw + count, queries_n), frame_two.dtype),
                pltpu.VMEM((raw + 2 * count, 2 * queries_n), jnp.float32),
                *pooling,
                pltpu.SemaphoreType.DMA((strips,)),
                pltpu.SemaphoreType.DMA((max(1, len(landing)),)),
            ],
            input_output_aliases={1 + len(operands) + bool(landing): 0},
            compiler_params=params,
            cost_estimate=modelled(cost),
            name="correlate",
        )(meta, *operands, *([landed] if landing else []), out, *pins)

    def product_type(strips, pixels):
        return jax.ShapeDtypeStruct((strips, pixels, queries_n), frame_two.dtype)

    def raw_rows(out, own, other, wide, landing=(), landed=None, cost=0, leavers=(), leaving=(), slots=(), pins=()):
        operands = [*own, *other, queries_wide if wide else queries]
        strips = sum(half.shape[0] for half in own)
        passive = ([landed] if landing else []) + list(leavers)
        pins = tuple(pins)
        return pl.pallas_call(
            functools.partial(raw_kernel, factor, (len(own), len(other)), wide, landing, leaving, slots, len(pins)),
            out_shape=(out_type,) + (product_type(strips, raw + count),) * (1 + wide),
            in_specs=[scalars] + [in_vmem] * len(operands) + [anywhere] * (1 + len(passive) + len(pins)),
            out_specs=(anywhere,) + (in_vmem,) * (1 + wide),
            scratch_shapes=[
                pltpu.VMEM((raw + count, queries_n * (1 + wide)), jnp.float32),
                *pooling,
                pltpu.SemaphoreType.DMA((max(1, len(landing)),)),
                pltpu.SemaphoreType.DMA((max(1, len(slots)),)),
            ],
            input_output_aliases={1 + len(operands) + len(passive): 0},
            compiler_params=params,
            cost_estimate=modelled(cost),
            name="raw_rows",
        )(meta, *operands, *passive, out, *pins)

    def came_rows(out, done, slots, own, other, wide, late=(), cost=0, pins=(), landing=()):
        operands = [*own, *other, queries_wide if wide else queries, *late[:1]]
        first = 1 + len(operands)
        inout = [out, done, *late[1:]]
        extra_types = (product_type(done.shape[0], count),) if wide else ()
        return pl.pallas_call(
            functools.partial(came_kernel, factor, (len(own), len(other)), wide, len(late) // 2, len(pins), slots, not G("NL"), landing),
            out_shape=tuple(jax.ShapeDtypeStruct(array.shape, array.dtype) for array in inout) + extra_types,
            in_specs=[scalars] + [in_vmem] * len(operands) + [anywhere] + [in_vmem] * (len(inout) - 1) + [anywhere] * len(pins),
            out_specs=(anywhere,) + (in_vmem,) * (len(inout) - 1 + wide),
            scratch_shapes=[
                pltpu.VMEM((count, queries_n), jnp.float32),
                pltpu.SemaphoreType.DMA((max(1, len(slots)),)),
                pltpu.SemaphoreType.DMA((max(1, len(landing)),)),
            ],
            input_output_aliases={first + index: index for index in range(len(inout))},
            compiler_params=params,
            cost_estimate=modelled(cost),
            name="came_rows",
        )(meta, *operands, *inout, *pins)

    def gate(out, pins, cost):
        handed = (out, *pins)
        return pl.pallas_call(
            gate_kernel,
            out_shape=tuple(jax.ShapeDtypeStruct(array.shape, array.dtype) for array in handed),
            in_specs=[anywhere] * len(handed),
            out_specs=(anywhere,) * len(handed),
            input_output_aliases={index: index for index in range(len(handed))},
            compiler_params=params,
            cost_estimate=modelled(cost),
            name="gate",
        )(*handed)

    mine = lax.dynamic_slice_in_dim(frame_two, side * half_rows, half_rows, axis=0)[None]
    theirs = lax.dynamic_slice_in_dim(frame_two, (1 - side) * half_rows, half_rows, axis=0)[None]
    if G("WH"):
        theirs = jnp.where(side == 0, frame_two[half_rows:], frame_two[:half_rows])[None]
    if G("XQ"):
        sent = jnp.concatenate([theirs.reshape(raw, chans), frame_one], axis=0)
        got = lax.ppermute(sent, "chan", across)
        partner, queries_other = got[:raw].reshape(theirs.shape), got[raw:]
    else:
        partner = lax.ppermute(theirs, "chan", across)
        queries_other = lax.ppermute(frame_one, "chan", across)
    def all_queries(mine, theirs):
        own_core = jnp.concatenate([mine.T, theirs.T], axis=0)
        return own_core, jnp.concatenate([own_core, lax.ppermute(own_core, "rows", swap)], axis=1)

    if not G("QC"): queries, queries_wide = all_queries(frame_one, queries_other)

    def permute_rows(pairs, pieces):
        return [lax.ppermute(piece, "rows", pairs) for piece in pieces]

    def whole(pieces):
        return pieces if len(pieces) == 1 else [jnp.concatenate(pieces, axis=0)]

    came = {0: ([mine], [partner])}
    moving = [[half, *permute_rows(swap, [half])] for half in (mine, partner)]
    join = [G("JA"), G("JB")]
    for d in range(1, half_way + 1):
        if d == half_way:
            moving = [[pieces[0][:1]] for pieces in moving]
        if d == half_way - 1 and G("BSPL"):
            moving[1] = [moving[1][0][:1], moving[1][0][1:]]
        moving = [whole(pieces) if d == join[part] else pieces for part, pieces in enumerate(moving)]
        if d == 1:
            ring_first = moving[1][-1]
        moving = [permute_rows(ring, pieces) for pieces in moving]
        came[d] = tuple(moving)
    across_came = {}

    def do_extra(out, d, part, pin=None):
        pins = () if pin is None else tuple(across_came[pin]) if isinstance(pin, tuple) else (pin,)
        across_came[d, 1 - part] = []
        groups = [[piece] for piece in came[d][part]] if part and d == half_way - 1 else [came[d][part]]
        for pieces in groups:
            extra, out = make_extra(out, pieces, G(f"X{d}{part}"), pins)
            across_came[d, 1 - part].append(lax.ppermute(extra, "chan", across))
            pins = ()
        return out

    lag = G("LAG")
    waiting = []

    def landing(now):
        if waiting and waiting[0][0] <= now:
            return waiting.pop(0)[1:]
        return (), None

    def product(out, d, pins=(), now=None):
        out, pair = correlate(out, slots_of(d, 0), *came[d], across_came[d, 0], across_came[d, 1], *landing(d if now is None else now), G(f"C{d}"), pins)
        waiting.append((d + lag, slots_of(d, 1), permute_rows(swap, [pair])[0]))
        return out

    if G("QC"):
        extra, out, sent = make_extra(None, came[0][0], G("X00"), ({1: partner, 2: ring_first}[G("PINX")],) if G("PINX") else (), passed=frame_one)
        across_came[0, 1] = [lax.ppermute(extra, "chan", across)]
        queries, queries_wide = all_queries(frame_one, lax.ppermute(sent, "chan", across))
    else:
        out = do_extra(None, 0, 0, partner if G("PINX") else None)
    lacking, out = make_extra(out, [theirs], G("X01"), tuple(across_came[0, 1]) if G("PIN01") else (), flip=True)
    across_came[0, 0] = [lacking]
    near, far = half_way - 1, half_way

    def swap_one(piece):
        return permute_rows(swap, [piece])[0]

    def near_raw(out):
        return raw_rows(out, *came[near], True, *landing(near), G("F3"), slots=slots_of(near, 0) if G("EL") else (), pins=tuple(across_came[far, 1]) if G("PR") else ())

    swapped = []

    def far_extra(out, part, pins):
        extra, out, piece = make_extra(out, came[far][part], G(f"X4{part}"), pins, carry=True)
        came[far][part][0] = piece
        across_came[far, 1 - part] = [lax.ppermute(extra, "chan", across)]
        swapped.append(swap_one(piece))
        return out

    out = do_extra(out, 1, 0)
    out = do_extra(out, 2, 0, (1, 1))
    out = do_extra(out, 1, 1, (2, 1))
    out = product(out, 0)
    for d in range(3, far):
        out = do_extra(out, d, 0, (d - 2, 0))
        out = product(out, d - 2)
        out = do_extra(out, d - 1, 1, (d, 1))
    out = far_extra(out, 0, tuple(across_came[near - 1, 0]) if G("P4") else ())
    across_came[near, 0] = []
    groups = [came[near][1]] if G("ONEX") else [[piece] for piece in came[near][1]]
    for index, pieces in enumerate(groups):
        if index == len(groups) - G("CPOS"):
            out = product(out, near - 1, now=near)
        extra, out = make_extra(out, pieces, G("X31"), tuple(across_came[far, 1]) if G("P3") == index + 1 else ())
        across_came[near, 0].append(lax.ppermute(extra, "chan", across))
    out, near_done, near_pair = near_raw(out)
    out = far_extra(out, 1, (swapped[0],) if G("PS0") == 1 else ())
    near_late = swap_one(near_pair)
    pins = (tuple(across_came[far, 1]) if G("PE4") == 1 else ()) + ((swapped[0],) if G("PS0") == 2 else ())

    slots = slots_of(near, 1) + slots_of(far, 0) + slots_of(far, 1)

    landing_now, landed_now = landing(far) if G("LC") else ((), None)
    pins = ((landed_now,) if landing_now else ()) + pins
    out, near_done, near_rows = came_rows(
        out, near_done, (), across_came[near, 0], across_came[near, 1], True, cost=G("F2"), pins=pins, landing=landing_now
    )
    near_rows = swap_one(near_rows)
    out, far_done = raw_rows(
        out,
        [came[far][0][0], swapped[0]],
        [came[far][1][0], swapped[1]],
        False,
        *landing(far),
        G("F0"),
        (near_done, near_late),
        ("rest" if G("EL") else "all", "settled" if G("NL") else None),
        slots_of(near, 0) + (slots if G("NL") else slots[len(slots_of(near, 1)) :]),
    )
    out, own, other = gate(out, [across_came[far, 0][0], across_came[far, 1][0]], G("GATE"))
    return came_rows(out, far_done, slots, [own, swap_one(own)], [other, swap_one(other)], False, (near_rows, near_late), G("F1"))[0]


def solution(mesh):
    rows_axis, groups = mesh.shape["rows"], mesh.shape["chan"]

    def local(frame_one, frame_two):
        rows_n, cols_n, chans = frame_two.shape
        ring = groups == 2 and rows_axis % 8 == 0 and rows_axis >= 16 and rows_n % 8 == 0 and cols_n % 32 == 0 and chans % LANES == 0
        return (ring_local if ring else gather_local)(frame_one, frame_two)

    in_specs = (P("rows", "chan"), P("rows", None, "chan"))
    out_specs = P(None, "chan", "rows")
    return jax.shard_map(local, mesh=mesh, in_specs=in_specs, out_specs=out_specs, check_vma=False)
```

```python
import functools

import jax
import jax.numpy as jnp
from jax import lax
from jax.experimental import pallas as pl
from jax.experimental.pallas import tpu as pltpu
from jax.sharding import PartitionSpec as P

LANES = 128
PARAMS = {'LAG': 2, 'F0': 10, 'F1': 0, 'PS0': 2, 'JA': 3, 'JB': 1, 'C0POS': 2, 'GATE': 30, 'F3': 10, 'F2': 22, 'NL': 1, 'PE4': 0, 'P4': 0, 'P3': 1, 'CPOS': 1, 'LC': 1, 'BSPL': 0, 'EL': 1, 'WH': 0, 'X00': 10, 'X01': 10, 'C0': 10, 'X10': 10, 'X11': 10, 'C1': 10, 'X20': 10, 'X21': 10, 'C2': 10, 'X30': 10, 'X31': 10, 'C3': 10, 'X40': 10, 'X41': 10, 'C4': 10}


def G(name):
    return PARAMS.get(name, 0)


VMEM_BYTES = 28 * 1024 * 1024


def pool_strip(strip):
    full = strip.astype(jnp.float32)
    rows_n, cols_n, chans = full.shape
    level_one = full.reshape(rows_n // 2, 2, cols_n // 2, 2, chans).mean(axis=(1, 3))
    level_two = level_one.reshape(rows_n // 4, 2, cols_n // 4, 2, chans).mean(axis=(1, 3))
    joined = jnp.concatenate(
        [full.reshape(-1, chans), level_one.reshape(-1, chans), level_two.reshape(-1, chans)],
        axis=0,
    )
    return joined.astype(jnp.bfloat16)


def gather_local(frame_one, frame_two):
    groups = lax.axis_size("chan")
    queries = lax.all_gather(frame_one, "chan", axis=0, tiled=False)
    channels = queries.shape[0] * queries.shape[2]
    factor = 1.0 / jnp.sqrt(jnp.float32(channels))
    pooled = pool_strip(frame_two)
    share = pooled.shape[0] // groups
    traded = lax.all_to_all(
        pooled.reshape(groups, share, pooled.shape[1]), "chan", split_axis=0, concat_axis=0, tiled=True
    )
    gathered = lax.all_gather(traded, "rows", axis=0, tiled=False)
    values = jnp.einsum("skpc,kqc->spq", gathered, queries, preferred_element_type=jnp.float32)
    return (values * factor).astype(jnp.bfloat16)


def pooled_levels(half, sums, sums_two):
    rows_n, cols_n, _ = half.shape
    means = []
    for row in range(rows_n // 2):
        sums[row] = half[2 * row].astype(jnp.float32) + half[2 * row + 1].astype(jnp.float32)
        left = sums[row, pl.ds(0, cols_n // 2, stride=2), :]
        right = sums[row, pl.ds(1, cols_n // 2, stride=2), :]
        means.append((left + right) * 0.25)
    means_two = []
    for row in range(rows_n // 4):
        sums_two[row] = means[2 * row] + means[2 * row + 1]
        left = sums_two[row, pl.ds(0, cols_n // 4, stride=2), :]
        right = sums_two[row, pl.ds(1, cols_n // 4, stride=2), :]
        means_two.append((left + right) * 0.25)
    return jnp.concatenate(means + means_two, axis=0)


def strips_in(refs):
    return [ref.at[index] for ref in refs for index in range(ref.shape[0])]


def extra_kernel(pieces, results, flip, meta, *refs):
    halves = strips_in(refs[:pieces])
    extra, sums, sums_two = refs[-2 - results], *refs[-2:]
    count, cols_n = extra.shape[1], halves[0].shape[1]
    upper = meta[0] == (1 if flip else 0)

    @pl.when(upper)
    def _():
        for index, half in enumerate(halves):
            extra[index] = pooled_levels(half, sums, sums_two).astype(extra.dtype)

    @pl.when(jnp.logical_not(upper))
    def _():
        for index, half in enumerate(halves):
            parts, left, row = [], count, 0
            while left > 0:
                parts.append(half[row].astype(jnp.float32)[: min(left, cols_n)])
                left, row = left - cols_n, row + 1
            extra[index] = jnp.concatenate(parts, axis=0).astype(extra.dtype)


def chunks(segments, step):
    todo, runs = list(segments), []
    while todo:
        run, room = [], step
        while todo and room > 0:
            ref, first, last = todo.pop(0)
            take = min(room, last - first)
            run.append((ref, first, first + take))
            room -= take
            if first + take < last:
                todo.insert(0, (ref, first + take, last))
        runs.append(run)
    return runs


def joined(run):
    parts = [ref[first:last].astype(jnp.float32) for ref, first, last in run]
    return parts[0] if len(parts) == 1 else jnp.concatenate(parts, axis=0)


def corr_kernel(factor, pieces, wide, slots, landing, pins, meta, *refs):
    own, other = strips_in(refs[: pieces[0]]), strips_in(refs[pieces[0] : sum(pieces[:2])])
    refs = refs[sum(pieces[:2]) :]
    came_own, came_other = strips_in(refs[: pieces[2]]), strips_in(refs[pieces[2] : pieces[2] + pieces[3]])
    queries, *refs = refs[pieces[2] + pieces[3] :]
    landed = refs.pop(0) if landing else None
    out, *refs = refs[1 + pins :]
    pair = refs.pop(0) if wide else None
    done, values, sums, sums_two, sems, land_sems = refs
    rows_n, cols_n, _ = own[0].shape
    count, width = came_own[0].shape[0], done.shape[2]
    raw = rows_n * cols_n
    ones = (rows_n // 2) * (cols_n // 2)

    copies = []
    for index, slot in enumerate(landing):
        copies.append(pltpu.make_async_copy(landed.at[index], out.at[meta[slot]], land_sems.at[index]))
        copies[-1].start()

    def times(left):
        return jnp.dot(left, queries[...], preferred_element_type=jnp.float32) * factor

    def store(index, at, part):
        done[index, at : at + part.shape[0]] = part[:, :width].astype(done.dtype)
        if wide:
            pair[index, at : at + part.shape[0]] = part[:, width:].astype(done.dtype)

    for index in range(len(own)):

        def raw_row(row):
            return jnp.concatenate([own[index][row], other[index][row]], axis=1)

        def came_rows():
            return jnp.concatenate([came_own[index][...], came_other[index][...]], axis=1)

        @pl.when(meta[0] == 0)
        def _():
            for row in range(rows_n):
                store(index, row * cols_n, times(raw_row(row)))
            store(index, raw, times(came_rows()))

        @pl.when(meta[0] != 0)
        def _():
            for row in range(count // cols_n, rows_n):
                values[row * cols_n : (row + 1) * cols_n] = times(raw_row(row))
            values[raw : raw + count] = times(came_rows())
            levels = [pooled_levels(half[index], sums, sums_two).astype(done.dtype) for half in (own, other)]
            lower = raw + count
            values[lower : lower + count] = times(jnp.concatenate(levels, axis=1))
            segments = [
                (values, count, raw),
                (values, raw, raw + ones),
                (values, lower, lower + ones),
                (values, raw + ones, raw + count),
                (values, lower + ones, lower + count),
            ]
            step = cols_n // 2
            for at, run in enumerate(chunks(segments, step)):
                store(index, at * step, joined(run))

        copies.append(pltpu.make_async_copy(done.at[index], out.at[meta[slots[index]]], sems.at[index]))
        copies[-1].start()
    for copy in copies:
        copy.wait()


def late_kernel(slots, raw, meta, rows, _, __, out, strips, values, sems):
    total = strips.shape[1]
    count, cut = total - raw, first_open_row(total, raw)
    ones, copies = count * 4 // 5, []
    for index, slot in enumerate(slots):
        strip = strips.at[index]
        part = rows[index].astype(jnp.float32)

        @pl.when(meta[0] == 0)
        def _():
            strip[raw:total] = part.astype(strips.dtype)

        @pl.when(meta[0] != 0)
        def _():
            values[...] = part
            at = raw - count
            for first, last, into in ((0, ones, at), (ones, count, at + 2 * ones)):
                start = into // 16 * 16
                end = -(-(into + last - first) // 16) * 16
                parts = [values[first:last]]
                if start < into:
                    parts.insert(0, strip[start : start + 16].astype(jnp.float32)[: into - start])
                over = end - (into + last - first)
                if over:
                    parts.append(strip[end - 16 : end].astype(jnp.float32)[16 - over :])
                strip[start:end] = jnp.concatenate(parts, axis=0).astype(strips.dtype)

        open_rows = pl.ds(cut, total - cut)
        copies.append(pltpu.make_async_copy(strip.at[open_rows], out.at[meta[slot], open_rows], sems.at[index]))
        copies[-1].start()
    for copy in copies:
        copy.wait()


def gate_kernel(*refs):
    pass


def first_open_row(total, raw):
    return (2 * raw - total) // 16 * 16


def raw_kernel(factor, arrays, wide, landing, leaving, slots, pins, meta, *refs):
    own, other = strips_in(refs[: arrays[0]]), strips_in(refs[arrays[0] : sum(arrays)])
    queries, *refs = refs[sum(arrays) :]
    landed = refs.pop(0) if landing else None
    leavers, refs = refs[: len(leaving)], refs[len(leaving) :]
    out, done, *refs = refs[1 + pins :]
    pair = refs.pop(0) if wide else None
    values, sums, sums_two, land_sems, sems = refs
    rows_n, cols_n, _ = own[0].shape
    count, width = done.shape[1] - rows_n * cols_n, done.shape[2]
    raw = rows_n * cols_n
    ones = (rows_n // 2) * (cols_n // 2)

    copies = []
    for index, slot in enumerate(landing):
        copies.append(pltpu.make_async_copy(landed.at[index], out.at[meta[slot]], land_sems.at[index]))
        copies[-1].start()
    total, cut = done.shape[1], first_open_row(done.shape[1], rows_n * cols_n)
    slots = list(slots)

    def leave(strip, part):
        rows = {"all": pl.ds(0, total), "settled": pl.ds(0, cut), "rest": pl.ds(cut, total - cut)}[part]
        number = len(copies) - len(landing)
        copies.append(pltpu.make_async_copy(strip.at[rows], out.at[meta[slots.pop(0)], rows], sems.at[number]))
        copies[-1].start()

    for strips, part in zip(leavers, leaving):
        for index in range(strips.shape[0] if part else 0):
            leave(strips.at[index], part)

    def times(left):
        return jnp.dot(left, queries[...], preferred_element_type=jnp.float32) * factor

    def store(index, at, part):
        done[index, at : at + part.shape[0]] = part[:, :width].astype(done.dtype)
        if wide:
            pair[index, at : at + part.shape[0]] = part[:, width:].astype(done.dtype)

    for index, halves in enumerate(zip(own, other)):

        def raw_row(row):
            return jnp.concatenate([half[row] for half in halves], axis=1)

        @pl.when(meta[0] == 0)
        def _():
            for row in range(rows_n):
                store(index, row * cols_n, times(raw_row(row)))
            store(index, raw, jnp.zeros((count, values.shape[1]), jnp.float32))

        @pl.when(meta[0] != 0)
        def _():
            for row in range(count // cols_n, rows_n):
                values[row * cols_n : (row + 1) * cols_n] = times(raw_row(row))
            levels = [pooled_levels(half, sums, sums_two).astype(done.dtype) for half in halves]
            values[raw : raw + count] = times(jnp.concatenate(levels, axis=1))
            segments = [
                (values, count, raw),
                (values, raw, raw + ones),
                (values, raw, raw + ones),
                (values, raw + ones, raw + count),
                (values, raw + ones, raw + count),
            ]
            step = cols_n // 2
            for at, run in enumerate(chunks(segments, step)):
                store(index, at * step, joined(run))

        if slots:
            leave(done.at[index], "settled")
    for copy in copies:
        copy.wait()


def came_kernel(factor, arrays, wide, late, pins, slots, late_whole, landing, meta, *refs):
    own, other = strips_in(refs[: arrays[0]]), strips_in(refs[arrays[0] : sum(arrays)])
    queries, *refs = refs[sum(arrays) :]
    late_rows = refs.pop(0) if late else None
    refs = refs[2 + late :]
    landed = refs[0] if landing else None
    refs = refs[pins:]
    out, done, *refs = refs
    late_done = refs.pop(0) if late else None
    pair = refs.pop(0) if wide else None
    values, sems, land_sems = refs
    count, width = own[0].shape[0], done.shape[2]
    raw = done.shape[1] - count
    ones = count * 4 // 5
    copies, landings = [], []
    for index, slot in enumerate(landing):
        landings.append(pltpu.make_async_copy(landed.at[index], out.at[meta[slot]], land_sems.at[index]))
        landings[-1].start()

    def leave(strip, whole=False):
        if slots:
            cut = 0 if whole else first_open_row(raw + count, raw)
            rows = pl.ds(cut, raw + count - cut)
            slot = meta[slots[len(copies)]]
            copies.append(pltpu.make_async_copy(strip.at[rows], out.at[slot, rows], sems.at[len(copies)]))
            copies[-1].start()

    def merge(strip, part):
        @pl.when(meta[0] == 0)
        def _():
            strip[raw : raw + count] = part.astype(done.dtype)

        @pl.when(meta[0] != 0)
        def _():
            values[...] = part
            at = raw - count
            for first, last, into in ((0, ones, at), (ones, count, at + 2 * ones)):
                start = into // 16 * 16
                end = -(-(into + last - first) // 16) * 16
                parts = [values[first:last]]
                if start < into:
                    parts.insert(0, strip[start : start + 16].astype(jnp.float32)[: into - start])
                over = end - (into + last - first)
                if over:
                    parts.append(strip[end - 16 : end].astype(jnp.float32)[16 - over :])
                strip[start:end] = jnp.concatenate(parts, axis=0).astype(done.dtype)

    if late:
        for index in range(late_done.shape[0]):
            merge(late_done.at[index], late_rows[index].astype(jnp.float32))
            leave(late_done.at[index], late_whole)
    for index, halves in enumerate(zip(own, other)):
        left = jnp.concatenate([half[...] for half in halves], axis=1)
        part = jnp.dot(left, queries[...], preferred_element_type=jnp.float32) * factor
        if wide:
            pair[index] = part[:, width:].astype(done.dtype)
        merge(done.at[index], part[:, :width])
        leave(done.at[index])
    for copy in copies + landings:
        copy.wait()


def ring_local(frame_one, frame_two):
    rows_axis = lax.axis_size("rows")
    rows_n, cols_n, chans = frame_two.shape
    queries_n = frame_one.shape[0]
    half_rows = rows_n // 2
    raw = half_rows * cols_n
    count = (half_rows // 2) * (cols_n // 2) + (half_rows // 4) * (cols_n // 4)
    factor = float(1.0 / (2 * chans) ** 0.5)
    me, side = lax.axis_index("rows"), lax.axis_index("chan")

    chips = rows_axis // 2
    columns, half_way = chips // 2, chips // 2
    order = [2 * z for z in range(columns)] + [2 * z + 1 for z in reversed(range(columns))]
    ring = [(2 * order[p], 2 * order[(p + 1) % chips]) for p in range(chips)]
    ring += [(2 * order[p] + 1, 2 * order[p - 1] + 1) for p in range(chips)]
    swap = [(r, r ^ 1) for r in range(rows_axis)]
    across = [(0, 1), (1, 0)]

    core, column, line = me % 2, me // 4, (me // 2) % 2
    place = jnp.where(line == 0, column, chips - 1 - column)
    steps = jnp.arange(half_way + 1, dtype=jnp.int32)

    def strips_of(c):
        p = (place + jnp.where(c == 0, -steps, steps)) % chips
        chip = jnp.where(p < columns, 2 * p, 2 * (chips - 1 - p) + 1)
        return [2 * chip + c, 2 * chip + 1 - c]

    meta = jnp.concatenate([side[None], *strips_of(core), *strips_of(1 - core)]).astype(jnp.int32)

    def slots_of(d, other_core):
        first = 1 + (2 * other_core) * (half_way + 1) + d
        return (first,) if d in (0, half_way) else (first, first + half_way + 1)

    in_vmem = pl.BlockSpec(memory_space=pltpu.VMEM)
    anywhere = pl.BlockSpec(memory_space=pl.ANY)
    scalars = pl.BlockSpec(memory_space=pltpu.SMEM)
    out_type = jax.ShapeDtypeStruct((rows_axis, raw + count, queries_n), frame_two.dtype)
    pooling = [
        pltpu.VMEM((half_rows // 2, cols_n, chans), jnp.float32),
        pltpu.VMEM((half_rows // 4, cols_n // 2, chans), jnp.float32),
    ]
    params = pltpu.CompilerParams(vmem_limit_bytes=VMEM_BYTES)
    def modelled(us):
        return pl.CostEstimate(flops=int(us * 10**9) + 1000, bytes_accessed=1000, transcendentals=0)


    def make_extra(out, halves, cost=0, pins=(), flip=False, carry=False, passed=None):
        strips = sum(half.shape[0] for half in halves)
        handed = () if out is None else (out,)
        carried = tuple(halves) if carry else ()
        aliases = {1 + len(halves): 1} if handed else {}
        aliases.update({1 + index: 2 + index for index in range(len(carried))})
        if passed is not None:
            pins, carried = (passed, *pins), (passed,)
            aliases[1 + len(halves) + len(handed)] = 2
        return pl.pallas_call(
            functools.partial(extra_kernel, len(halves), 2 + len(carried), flip),
            out_shape=(jax.ShapeDtypeStruct((strips, count, chans), frame_two.dtype), out_type)
            + tuple(jax.ShapeDtypeStruct(half.shape, half.dtype) for half in carried),
            in_specs=[scalars] + [in_vmem] * len(halves) + [anywhere] * len(handed + pins),
            out_specs=(in_vmem, anywhere) + (in_vmem if carry else anywhere,) * len(carried),
            scratch_shapes=pooling,
            input_output_aliases=aliases,
            compiler_params=params,
            cost_estimate=modelled(cost),
            name="extra",
        )(meta, *halves, *handed, *pins)

    def correlate(out, slots, own, other, came_own, came_other, landing=(), landed=None, cost=0, pins=()):
        parts = (own, other, came_own, came_other)
        strips = sum(piece.shape[0] for piece in own)
        operands = [*own, *other, *came_own, *came_other, queries_wide]
        pair_type = jax.ShapeDtypeStruct((strips, raw + count, queries_n), frame_two.dtype)
        return pl.pallas_call(
            functools.partial(corr_kernel, factor, tuple(len(part) for part in parts), True, slots, landing, len(pins)),
            out_shape=(out_type, pair_type),
            in_specs=[scalars] + [in_vmem] * len(operands) + [anywhere] * (1 + bool(landing) + len(pins)),
            out_specs=(anywhere, in_vmem),
            scratch_shapes=[
                pltpu.VMEM((strips, raw + count, queries_n), frame_two.dtype),
                pltpu.VMEM((raw + 2 * count, 2 * queries_n), jnp.float32),
                *pooling,
                pltpu.SemaphoreType.DMA((strips,)),
                pltpu.SemaphoreType.DMA((max(1, len(landing)),)),
            ],
            input_output_aliases={1 + len(operands) + bool(landing): 0},
            compiler_params=params,
            cost_estimate=modelled(cost),
            name="correlate",
        )(meta, *operands, *([landed] if landing else []), out, *pins)

    def product_type(strips, pixels):
        return jax.ShapeDtypeStruct((strips, pixels, queries_n), frame_two.dtype)

    def raw_rows(out, own, other, wide, landing=(), landed=None, cost=0, leavers=(), leaving=(), slots=(), pins=()):
        operands = [*own, *other, queries_wide if wide else queries]
        strips = sum(half.shape[0] for half in own)
        passive = ([landed] if landing else []) + list(leavers)
        pins = tuple(pins)
        return pl.pallas_call(
            functools.partial(raw_kernel, factor, (len(own), len(other)), wide, landing, leaving, slots, len(pins)),
            out_shape=(out_type,) + (product_type(strips, raw + count),) * (1 + wide),
            in_specs=[scalars] + [in_vmem] * len(operands) + [anywhere] * (1 + len(passive) + len(pins)),
            out_specs=(anywhere,) + (in_vmem,) * (1 + wide),
            scratch_shapes=[
                pltpu.VMEM((raw + count, queries_n * (1 + wide)), jnp.float32),
                *pooling,
                pltpu.SemaphoreType.DMA((max(1, len(landing)),)),
                pltpu.SemaphoreType.DMA((max(1, len(slots)),)),
            ],
            input_output_aliases={1 + len(operands) + len(passive): 0},
            compiler_params=params,
            cost_estimate=modelled(cost),
            name="raw_rows",
        )(meta, *operands, *passive, out, *pins)

    def came_rows(out, done, slots, own, other, wide, late=(), cost=0, pins=(), landing=()):
        operands = [*own, *other, queries_wide if wide else queries, *late[:1]]
        first = 1 + len(operands)
        inout = [out, done, *late[1:]]
        extra_types = (product_type(done.shape[0], count),) if wide else ()
        return pl.pallas_call(
            functools.partial(came_kernel, factor, (len(own), len(other)), wide, len(late) // 2, len(pins), slots, not G("NL"), landing),
            out_shape=tuple(jax.ShapeDtypeStruct(array.shape, array.dtype) for array in inout) + extra_types,
            in_specs=[scalars] + [in_vmem] * len(operands) + [anywhere] + [in_vmem] * (len(inout) - 1) + [anywhere] * len(pins),
            out_specs=(anywhere,) + (in_vmem,) * (len(inout) - 1 + wide),
            scratch_shapes=[
                pltpu.VMEM((count, queries_n), jnp.float32),
                pltpu.SemaphoreType.DMA((max(1, len(slots)),)),
                pltpu.SemaphoreType.DMA((max(1, len(landing)),)),
            ],
            input_output_aliases={first + index: index for index in range(len(inout))},
            compiler_params=params,
            cost_estimate=modelled(cost),
            name="came_rows",
        )(meta, *operands, *inout, *pins)

    def gate(out, pins, cost):
        handed = (out, *pins)
        return pl.pallas_call(
            gate_kernel,
            out_shape=tuple(jax.ShapeDtypeStruct(array.shape, array.dtype) for array in handed),
            in_specs=[anywhere] * len(handed),
            out_specs=(anywhere,) * len(handed),
            input_output_aliases={index: index for index in range(len(handed))},
            compiler_params=params,
            cost_estimate=modelled(cost),
            name="gate",
        )(*handed)

    mine = lax.dynamic_slice_in_dim(frame_two, side * half_rows, half_rows, axis=0)[None]
    theirs = lax.dynamic_slice_in_dim(frame_two, (1 - side) * half_rows, half_rows, axis=0)[None]
    if G("WH"):
        theirs = jnp.where(side == 0, frame_two[half_rows:], frame_two[:half_rows])[None]
    if G("XQ"):
        sent = jnp.concatenate([theirs.reshape(raw, chans), frame_one], axis=0)
        got = lax.ppermute(sent, "chan", across)
        partner, queries_other = got[:raw].reshape(theirs.shape), got[raw:]
    else:
        partner = lax.ppermute(theirs, "chan", across)
        queries_other = lax.ppermute(frame_one, "chan", across)
    def all_queries(mine, theirs):
        own_core = jnp.concatenate([mine.T, theirs.T], axis=0)
        return own_core, jnp.concatenate([own_core, lax.ppermute(own_core, "rows", swap)], axis=1)

    if not G("QC"): queries, queries_wide = all_queries(frame_one, queries_other)

    def permute_rows(pairs, pieces):
        return [lax.ppermute(piece, "rows", pairs) for piece in pieces]

    def whole(pieces):
        return pieces if len(pieces) == 1 else [jnp.concatenate(pieces, axis=0)]

    came = {0: ([mine], [partner])}
    moving = [[half, *permute_rows(swap, [half])] for half in (mine, partner)]
    join = [G("JA"), G("JB")]
    for d in range(1, half_way + 1):
        if d == half_way:
            moving = [[pieces[0][:1]] for pieces in moving]
        if d == half_way - 1 and G("BSPL"):
            moving[1] = [moving[1][0][:1], moving[1][0][1:]]
        moving = [whole(pieces) if d == join[part] else pieces for part, pieces in enumerate(moving)]
        if d == 1:
            ring_first = moving[1][-1]
        moving = [permute_rows(ring, pieces) for pieces in moving]
        came[d] = tuple(moving)
    across_came = {}

    def do_extra(out, d, part, pin=None):
        pins = () if pin is None else tuple(across_came[pin]) if isinstance(pin, tuple) else (pin,)
        across_came[d, 1 - part] = []
        groups = [[piece] for piece in came[d][part]] if part and d == half_way - 1 else [came[d][part]]
        for pieces in groups:
            extra, out = make_extra(out, pieces, G(f"X{d}{part}"), pins)
            across_came[d, 1 - part].append(lax.ppermute(extra, "chan", across))
            pins = ()
        return out

    lag = G("LAG")
    waiting = []

    def landing(now):
        if waiting and waiting[0][0] <= now:
            return waiting.pop(0)[1:]
        return (), None

    def product(out, d, pins=(), now=None):
        out, pair = correlate(out, slots_of(d, 0), *came[d], across_came[d, 0], across_came[d, 1], *landing(d if now is None else now), G(f"C{d}"), pins)
        waiting.append((d + lag, slots_of(d, 1), permute_rows(swap, [pair])[0]))
        return out

    if G("QC"):
        extra, out, sent = make_extra(None, came[0][0], G("X00"), ({1: partner, 2: ring_first}[G("PINX")],) if G("PINX") else (), passed=frame_one)
        across_came[0, 1] = [lax.ppermute(extra, "chan", across)]
        queries, queries_wide = all_queries(frame_one, lax.ppermute(sent, "chan", across))
    else:
        out = do_extra(None, 0, 0, partner if G("PINX") else None)
    lacking, out = make_extra(out, [theirs], G("X01"), tuple(across_came[0, 1]) if G("PIN01") else (), flip=True)
    across_came[0, 0] = [lacking]
    near, far = half_way - 1, half_way

    def swap_one(piece):
        return permute_rows(swap, [piece])[0]

    def near_raw(out):
        return raw_rows(out, *came[near], True, *landing(near), G("F3"), slots=slots_of(near, 0) if G("EL") else (), pins=tuple(across_came[far, 1]) if G("PR") else ())

    swapped = []

    def far_extra(out, part, pins):
        extra, out, piece = make_extra(out, came[far][part], G(f"X4{part}"), pins, carry=True)
        came[far][part][0] = piece
        across_came[far, 1 - part] = [lax.ppermute(extra, "chan", across)]
        swapped.append(swap_one(piece))
        return out

    out = do_extra(out, 1, 0)
    out = do_extra(out, 2, 0, (1, 1))
    out = do_extra(out, 1, 1, (2, 1))
    out = product(out, 0)
    for d in range(3, far):
        out = do_extra(out, d, 0, (d - 2, 0))
        out = product(out, d - 2)
        out = do_extra(out, d - 1, 1, (d, 1))
    out = far_extra(out, 0, tuple(across_came[near - 1, 0]) if G("P4") else ())
    across_came[near, 0] = []
    groups = [came[near][1]] if G("ONEX") else [[piece] for piece in came[near][1]]
    for index, pieces in enumerate(groups):
        if index == len(groups) - G("CPOS"):
            out = product(out, near - 1, now=near)
        extra, out = make_extra(out, pieces, G("X31"), tuple(across_came[far, 1]) if G("P3") == index + 1 else ())
        across_came[near, 0].append(lax.ppermute(extra, "chan", across))
    out, near_done, near_pair = near_raw(out)
    out = far_extra(out, 1, (swapped[0],) if G("PS0") == 1 else ())
    near_late = swap_one(near_pair)
    pins = (tuple(across_came[far, 1]) if G("PE4") == 1 else ()) + ((swapped[0],) if G("PS0") == 2 else ())

    slots = slots_of(near, 1) + slots_of(far, 0) + slots_of(far, 1)

    landing_now, landed_now = landing(far) if G("LC") else ((), None)
    pins = ((landed_now,) if landing_now else ()) + pins
    out, near_done, near_rows = came_rows(
        out, near_done, (), across_came[near, 0], across_came[near, 1], True, cost=G("F2"), pins=pins, landing=landing_now
    )
    near_rows = swap_one(near_rows)
    out, far_done = raw_rows(
        out,
        [came[far][0][0], swapped[0]],
        [came[far][1][0], swapped[1]],
        False,
        *landing(far),
        G("F0"),
        (near_done, near_late),
        ("rest" if G("EL") else "all", "settled" if G("NL") else None),
        slots_of(near, 0) + (slots if G("NL") else slots[len(slots_of(near, 1)) :]),
    )
    late_slots = slots_of(near, 1)
    out, _ = pl.pallas_call(
        functools.partial(late_kernel, late_slots, raw),
        out_shape=(out_type, jax.ShapeDtypeStruct(near_late.shape, near_late.dtype)),
        in_specs=[scalars, in_vmem, anywhere, in_vmem],
        out_specs=(anywhere, in_vmem),
        scratch_shapes=[
            pltpu.VMEM((count, queries_n), jnp.float32),
            pltpu.SemaphoreType.DMA((len(late_slots),)),
        ],
        input_output_aliases={2: 0, 3: 1},
        compiler_params=params,
        cost_estimate=modelled(0),
        name="late_rows",
    )(meta, near_rows, out, near_late)
    out, own, other = gate(out, [across_came[far, 0][0], across_came[far, 1][0]], G("GATE"))
    slots = slots_of(far, 0) + slots_of(far, 1)
    return came_rows(out, far_done, slots, [own, swap_one(own)], [other, swap_one(other)], False, (), G("F1"))[0]


def solution(mesh):
    rows_axis, groups = mesh.shape["rows"], mesh.shape["chan"]

    def local(frame_one, frame_two):
        rows_n, cols_n, chans = frame_two.shape
        ring = groups == 2 and rows_axis % 8 == 0 and rows_axis >= 16 and rows_n % 8 == 0 and cols_n % 32 == 0 and chans % LANES == 0
        return (ring_local if ring else gather_local)(frame_one, frame_two)

    in_specs = (P("rows", "chan"), P("rows", None, "chan"))
    out_specs = P(None, "chan", "rows")
    return jax.shard_map(local, mesh=mesh, in_specs=in_specs, out_specs=out_specs, check_vma=False)
```

```python
import functools

import jax
import jax.numpy as jnp
from jax import lax
from jax.experimental import pallas as pl
from jax.experimental.pallas import tpu as pltpu
from jax.sharding import PartitionSpec as P

LANES = 128
PARAMS = {'LAG': 2, 'F0': 10, 'F1': 0, 'PS0': 2, 'JA': 3, 'JB': 1, 'C0POS': 2, 'GATE': 30, 'F3': 0, 'F2': 22, 'NL': 1, 'PE4': 0, 'P4': 0, 'P3': 1, 'CPOS': 1, 'LC': 1, 'BSPL': 1, 'ONEX': 1, 'EL': 1, 'WH': 0, 'X00': 10, 'X01': 10, 'C0': 10, 'X10': 10, 'X11': 10, 'C1': 10, 'X20': 10, 'X21': 10, 'C2': 3, 'X30': 10, 'X31': 3, 'C3': 10, 'X40': 10, 'X41': 24, 'C4': 10}


def G(name):
    return PARAMS.get(name, 0)


VMEM_BYTES = 28 * 1024 * 1024


def pool_strip(strip):
    full = strip.astype(jnp.float32)
    rows_n, cols_n, chans = full.shape
    level_one = full.reshape(rows_n // 2, 2, cols_n // 2, 2, chans).mean(axis=(1, 3))
    level_two = level_one.reshape(rows_n // 4, 2, cols_n // 4, 2, chans).mean(axis=(1, 3))
    joined = jnp.concatenate(
        [full.reshape(-1, chans), level_one.reshape(-1, chans), level_two.reshape(-1, chans)],
        axis=0,
    )
    return joined.astype(jnp.bfloat16)


def gather_local(frame_one, frame_two):
    groups = lax.axis_size("chan")
    queries = lax.all_gather(frame_one, "chan", axis=0, tiled=False)
    channels = queries.shape[0] * queries.shape[2]
    factor = 1.0 / jnp.sqrt(jnp.float32(channels))
    pooled = pool_strip(frame_two)
    share = pooled.shape[0] // groups
    traded = lax.all_to_all(
        pooled.reshape(groups, share, pooled.shape[1]), "chan", split_axis=0, concat_axis=0, tiled=True
    )
    gathered = lax.all_gather(traded, "rows", axis=0, tiled=False)
    values = jnp.einsum("skpc,kqc->spq", gathered, queries, preferred_element_type=jnp.float32)
    return (values * factor).astype(jnp.bfloat16)


def pooled_levels(half, sums, sums_two):
    rows_n, cols_n, _ = half.shape
    means = []
    for row in range(rows_n // 2):
        sums[row] = half[2 * row].astype(jnp.float32) + half[2 * row + 1].astype(jnp.float32)
        left = sums[row, pl.ds(0, cols_n // 2, stride=2), :]
        right = sums[row, pl.ds(1, cols_n // 2, stride=2), :]
        means.append((left + right) * 0.25)
    means_two = []
    for row in range(rows_n // 4):
        sums_two[row] = means[2 * row] + means[2 * row + 1]
        left = sums_two[row, pl.ds(0, cols_n // 4, stride=2), :]
        right = sums_two[row, pl.ds(1, cols_n // 4, stride=2), :]
        means_two.append((left + right) * 0.25)
    return jnp.concatenate(means + means_two, axis=0)


def strips_in(refs):
    return [ref.at[index] for ref in refs for index in range(ref.shape[0])]


def extra_kernel(pieces, results, flip, meta, *refs):
    halves = strips_in(refs[:pieces])
    extra, sums, sums_two = refs[-2 - results], *refs[-2:]
    count, cols_n = extra.shape[1], halves[0].shape[1]
    upper = meta[0] == (1 if flip else 0)

    @pl.when(upper)
    def _():
        for index, half in enumerate(halves):
            extra[index] = pooled_levels(half, sums, sums_two).astype(extra.dtype)

    @pl.when(jnp.logical_not(upper))
    def _():
        for index, half in enumerate(halves):
            parts, left, row = [], count, 0
            while left > 0:
                parts.append(half[row].astype(jnp.float32)[: min(left, cols_n)])
                left, row = left - cols_n, row + 1
            extra[index] = jnp.concatenate(parts, axis=0).astype(extra.dtype)


def chunks(segments, step):
    todo, runs = list(segments), []
    while todo:
        run, room = [], step
        while todo and room > 0:
            ref, first, last = todo.pop(0)
            take = min(room, last - first)
            run.append((ref, first, first + take))
            room -= take
            if first + take < last:
                todo.insert(0, (ref, first + take, last))
        runs.append(run)
    return runs


def joined(run):
    parts = [ref[first:last].astype(jnp.float32) for ref, first, last in run]
    return parts[0] if len(parts) == 1 else jnp.concatenate(parts, axis=0)


def corr_kernel(factor, pieces, wide, slots, landing, pins, meta, *refs):
    own, other = strips_in(refs[: pieces[0]]), strips_in(refs[pieces[0] : sum(pieces[:2])])
    refs = refs[sum(pieces[:2]) :]
    came_own, came_other = strips_in(refs[: pieces[2]]), strips_in(refs[pieces[2] : pieces[2] + pieces[3]])
    queries, *refs = refs[pieces[2] + pieces[3] :]
    landed = refs.pop(0) if landing else None
    out, *refs = refs[1 + pins :]
    pair = refs.pop(0) if wide else None
    done, values, sums, sums_two, sems, land_sems = refs
    rows_n, cols_n, _ = own[0].shape
    count, width = came_own[0].shape[0], done.shape[2]
    raw = rows_n * cols_n
    ones = (rows_n // 2) * (cols_n // 2)

    copies = []
    for index, slot in enumerate(landing):
        copies.append(pltpu.make_async_copy(landed.at[index], out.at[meta[slot]], land_sems.at[index]))
        copies[-1].start()

    def times(left):
        return jnp.dot(left, queries[...], preferred_element_type=jnp.float32) * factor

    def store(index, at, part):
        done[index, at : at + part.shape[0]] = part[:, :width].astype(done.dtype)
        if wide:
            pair[index, at : at + part.shape[0]] = part[:, width:].astype(done.dtype)

    for index in range(len(own)):

        def raw_row(row):
            return jnp.concatenate([own[index][row], other[index][row]], axis=1)

        def came_rows():
            return jnp.concatenate([came_own[index][...], came_other[index][...]], axis=1)

        @pl.when(meta[0] == 0)
        def _():
            for row in range(rows_n):
                store(index, row * cols_n, times(raw_row(row)))
            store(index, raw, times(came_rows()))

        @pl.when(meta[0] != 0)
        def _():
            for row in range(count // cols_n, rows_n):
                values[row * cols_n : (row + 1) * cols_n] = times(raw_row(row))
            values[raw : raw + count] = times(came_rows())
            levels = [pooled_levels(half[index], sums, sums_two).astype(done.dtype) for half in (own, other)]
            lower = raw + count
            values[lower : lower + count] = times(jnp.concatenate(levels, axis=1))
            segments = [
                (values, count, raw),
                (values, raw, raw + ones),
                (values, lower, lower + ones),
                (values, raw + ones, raw + count),
                (values, lower + ones, lower + count),
            ]
            step = cols_n // 2
            for at, run in enumerate(chunks(segments, step)):
                store(index, at * step, joined(run))

        copies.append(pltpu.make_async_copy(done.at[index], out.at[meta[slots[index]]], sems.at[index]))
        copies[-1].start()
    for copy in copies:
        copy.wait()


def land_kernel(slots, meta, strips, _, out, sems):
    copies = []
    for index, slot in enumerate(slots):
        copies.append(pltpu.make_async_copy(strips.at[index], out.at[meta[slot]], sems.at[index]))
        copies[-1].start()
    for copy in copies:
        copy.wait()


def gate_kernel(*refs):
    pass


def first_open_row(total, raw):
    return (2 * raw - total) // 16 * 16


def raw_kernel(factor, arrays, wide, landing, leaving, slots, pins, meta, *refs):
    own, other = strips_in(refs[: arrays[0]]), strips_in(refs[arrays[0] : sum(arrays)])
    queries, *refs = refs[sum(arrays) :]
    landed = refs.pop(0) if landing else None
    leavers, refs = refs[: len(leaving)], refs[len(leaving) :]
    out, done, *refs = refs[1 + pins :]
    pair = refs.pop(0) if wide else None
    values, sums, sums_two, land_sems, sems = refs
    rows_n, cols_n, _ = own[0].shape
    count, width = done.shape[1] - rows_n * cols_n, done.shape[2]
    raw = rows_n * cols_n
    ones = (rows_n // 2) * (cols_n // 2)

    copies = []
    for index, slot in enumerate(landing):
        copies.append(pltpu.make_async_copy(landed.at[index], out.at[meta[slot]], land_sems.at[index]))
        copies[-1].start()
    total, cut = done.shape[1], first_open_row(done.shape[1], rows_n * cols_n)
    slots = list(slots)

    def leave(strip, part):
        rows = {"all": pl.ds(0, total), "settled": pl.ds(0, cut), "rest": pl.ds(cut, total - cut)}[part]
        number = len(copies) - len(landing)
        copies.append(pltpu.make_async_copy(strip.at[rows], out.at[meta[slots.pop(0)], rows], sems.at[number]))
        copies[-1].start()

    for strips, part in zip(leavers, leaving):
        for index in range(strips.shape[0] if part else 0):
            leave(strips.at[index], part)

    def times(left):
        return jnp.dot(left, queries[...], preferred_element_type=jnp.float32) * factor

    def store(index, at, part):
        done[index, at : at + part.shape[0]] = part[:, :width].astype(done.dtype)
        if wide:
            pair[index, at : at + part.shape[0]] = part[:, width:].astype(done.dtype)

    for index, halves in enumerate(zip(own, other)):

        def raw_row(row):
            return jnp.concatenate([half[row] for half in halves], axis=1)

        @pl.when(meta[0] == 0)
        def _():
            for row in range(rows_n):
                store(index, row * cols_n, times(raw_row(row)))
            store(index, raw, jnp.zeros((count, values.shape[1]), jnp.float32))

        @pl.when(meta[0] != 0)
        def _():
            for row in range(count // cols_n, rows_n):
                values[row * cols_n : (row + 1) * cols_n] = times(raw_row(row))
            levels = [pooled_levels(half, sums, sums_two).astype(done.dtype) for half in halves]
            values[raw : raw + count] = times(jnp.concatenate(levels, axis=1))
            segments = [
                (values, count, raw),
                (values, raw, raw + ones),
                (values, raw, raw + ones),
                (values, raw + ones, raw + count),
                (values, raw + ones, raw + count),
            ]
            step = cols_n // 2
            for at, run in enumerate(chunks(segments, step)):
                store(index, at * step, joined(run))

        if slots:
            leave(done.at[index], "settled")
    for copy in copies:
        copy.wait()


def came_kernel(factor, arrays, wide, late, pins, slots, late_whole, landing, meta, *refs):
    own, other = strips_in(refs[: arrays[0]]), strips_in(refs[arrays[0] : sum(arrays)])
    queries, *refs = refs[sum(arrays) :]
    late_rows = refs.pop(0) if late else None
    refs = refs[2 + late :]
    landed = refs[0] if landing else None
    refs = refs[pins:]
    out, done, *refs = refs
    late_done = refs.pop(0) if late else None
    pair = refs.pop(0) if wide else None
    values, sems, land_sems = refs
    count, width = own[0].shape[0], done.shape[2]
    raw = done.shape[1] - count
    ones = count * 4 // 5
    copies, landings = [], []
    for index, slot in enumerate(landing):
        landings.append(pltpu.make_async_copy(landed.at[index], out.at[meta[slot]], land_sems.at[index]))
        landings[-1].start()

    def leave(strip, whole=False):
        if slots:
            cut = 0 if whole else first_open_row(raw + count, raw)
            rows = pl.ds(cut, raw + count - cut)
            slot = meta[slots[len(copies)]]
            copies.append(pltpu.make_async_copy(strip.at[rows], out.at[slot, rows], sems.at[len(copies)]))
            copies[-1].start()

    def merge(strip, part):
        @pl.when(meta[0] == 0)
        def _():
            strip[raw : raw + count] = part.astype(done.dtype)

        @pl.when(meta[0] != 0)
        def _():
            values[...] = part
            at = raw - count
            for first, last, into in ((0, ones, at), (ones, count, at + 2 * ones)):
                start = into // 16 * 16
                end = -(-(into + last - first) // 16) * 16
                parts = [values[first:last]]
                if start < into:
                    parts.insert(0, strip[start : start + 16].astype(jnp.float32)[: into - start])
                over = end - (into + last - first)
                if over:
                    parts.append(strip[end - 16 : end].astype(jnp.float32)[16 - over :])
                strip[start:end] = jnp.concatenate(parts, axis=0).astype(done.dtype)

    if late:
        for index in range(late_done.shape[0]):
            merge(late_done.at[index], late_rows[index].astype(jnp.float32))
            leave(late_done.at[index], late_whole)
    for index, halves in enumerate(zip(own, other)):
        left = jnp.concatenate([half[...] for half in halves], axis=1)
        part = jnp.dot(left, queries[...], preferred_element_type=jnp.float32) * factor
        if wide:
            pair[index] = part[:, width:].astype(done.dtype)
        merge(done.at[index], part[:, :width])
        leave(done.at[index])
    for copy in copies + landings:
        copy.wait()


def ring_local(frame_one, frame_two):
    rows_axis = lax.axis_size("rows")
    rows_n, cols_n, chans = frame_two.shape
    queries_n = frame_one.shape[0]
    half_rows = rows_n // 2
    raw = half_rows * cols_n
    count = (half_rows // 2) * (cols_n // 2) + (half_rows // 4) * (cols_n // 4)
    factor = float(1.0 / (2 * chans) ** 0.5)
    me, side = lax.axis_index("rows"), lax.axis_index("chan")

    chips = rows_axis // 2
    columns, half_way = chips // 2, chips // 2
    order = [2 * z for z in range(columns)] + [2 * z + 1 for z in reversed(range(columns))]
    ring = [(2 * order[p], 2 * order[(p + 1) % chips]) for p in range(chips)]
    ring += [(2 * order[p] + 1, 2 * order[p - 1] + 1) for p in range(chips)]
    swap = [(r, r ^ 1) for r in range(rows_axis)]
    across = [(0, 1), (1, 0)]

    core, column, line = me % 2, me // 4, (me // 2) % 2
    place = jnp.where(line == 0, column, chips - 1 - column)
    steps = jnp.arange(half_way + 1, dtype=jnp.int32)

    def strips_of(c):
        p = (place + jnp.where(c == 0, -steps, steps)) % chips
        chip = jnp.where(p < columns, 2 * p, 2 * (chips - 1 - p) + 1)
        return [2 * chip + c, 2 * chip + 1 - c]

    meta = jnp.concatenate([side[None], *strips_of(core), *strips_of(1 - core)]).astype(jnp.int32)

    def slots_of(d, other_core):
        first = 1 + (2 * other_core) * (half_way + 1) + d
        return (first,) if d in (0, half_way) else (first, first + half_way + 1)

    in_vmem = pl.BlockSpec(memory_space=pltpu.VMEM)
    anywhere = pl.BlockSpec(memory_space=pl.ANY)
    scalars = pl.BlockSpec(memory_space=pltpu.SMEM)
    out_type = jax.ShapeDtypeStruct((rows_axis, raw + count, queries_n), frame_two.dtype)
    pooling = [
        pltpu.VMEM((half_rows // 2, cols_n, chans), jnp.float32),
        pltpu.VMEM((half_rows // 4, cols_n // 2, chans), jnp.float32),
    ]
    params = pltpu.CompilerParams(vmem_limit_bytes=VMEM_BYTES)
    def modelled(us):
        return pl.CostEstimate(flops=int(us * 10**9) + 1000, bytes_accessed=1000, transcendentals=0)


    def make_extra(out, halves, cost=0, pins=(), flip=False, carry=False, passed=None):
        strips = sum(half.shape[0] for half in halves)
        handed = () if out is None else (out,)
        carried = tuple(halves) if carry else ()
        aliases = {1 + len(halves): 1} if handed else {}
        aliases.update({1 + index: 2 + index for index in range(len(carried))})
        if passed is not None:
            pins, carried = (passed, *pins), (passed,)
            aliases[1 + len(halves) + len(handed)] = 2
        return pl.pallas_call(
            functools.partial(extra_kernel, len(halves), 2 + len(carried), flip),
            out_shape=(jax.ShapeDtypeStruct((strips, count, chans), frame_two.dtype), out_type)
            + tuple(jax.ShapeDtypeStruct(half.shape, half.dtype) for half in carried),
            in_specs=[scalars] + [in_vmem] * len(halves) + [anywhere] * len(handed + pins),
            out_specs=(in_vmem, anywhere) + (in_vmem if carry else anywhere,) * len(carried),
            scratch_shapes=pooling,
            input_output_aliases=aliases,
            compiler_params=params,
            cost_estimate=modelled(cost),
            name="extra",
        )(meta, *halves, *handed, *pins)

    def correlate(out, slots, own, other, came_own, came_other, landing=(), landed=None, cost=0, pins=()):
        parts = (own, other, came_own, came_other)
        strips = sum(piece.shape[0] for piece in own)
        operands = [*own, *other, *came_own, *came_other, queries_wide]
        pair_type = jax.ShapeDtypeStruct((strips, raw + count, queries_n), frame_two.dtype)
        return pl.pallas_call(
            functools.partial(corr_kernel, factor, tuple(len(part) for part in parts), True, slots, landing, len(pins)),
            out_shape=(out_type, pair_type),
            in_specs=[scalars] + [in_vmem] * len(operands) + [anywhere] * (1 + bool(landing) + len(pins)),
            out_specs=(anywhere, in_vmem),
            scratch_shapes=[
                pltpu.VMEM((strips, raw + count, queries_n), frame_two.dtype),
                pltpu.VMEM((raw + 2 * count, 2 * queries_n), jnp.float32),
                *pooling,
                pltpu.SemaphoreType.DMA((strips,)),
                pltpu.SemaphoreType.DMA((max(1, len(landing)),)),
            ],
            input_output_aliases={1 + len(operands) + bool(landing): 0},
            compiler_params=params,
            cost_estimate=modelled(cost),
            name="correlate",
        )(meta, *operands, *([landed] if landing else []), out, *pins)

    def product_type(strips, pixels):
        return jax.ShapeDtypeStruct((strips, pixels, queries_n), frame_two.dtype)

    def raw_rows(out, own, other, wide, landing=(), landed=None, cost=0, leavers=(), leaving=(), slots=(), pins=()):
        operands = [*own, *other, queries_wide if wide else queries]
        strips = sum(half.shape[0] for half in own)
        passive = ([landed] if landing else []) + list(leavers)
        pins = tuple(pins)
        return pl.pallas_call(
            functools.partial(raw_kernel, factor, (len(own), len(other)), wide, landing, leaving, slots, len(pins)),
            out_shape=(out_type,) + (product_type(strips, raw + count),) * (1 + wide),
            in_specs=[scalars] + [in_vmem] * len(operands) + [anywhere] * (1 + len(passive) + len(pins)),
            out_specs=(anywhere,) + (in_vmem,) * (1 + wide),
            scratch_shapes=[
                pltpu.VMEM((raw + count, queries_n * (1 + wide)), jnp.float32),
                *pooling,
                pltpu.SemaphoreType.DMA((max(1, len(landing)),)),
                pltpu.SemaphoreType.DMA((max(1, len(slots)),)),
            ],
            input_output_aliases={1 + len(operands) + len(passive): 0},
            compiler_params=params,
            cost_estimate=modelled(cost),
            name="raw_rows",
        )(meta, *operands, *passive, out, *pins)

    def came_rows(out, done, slots, own, other, wide, late=(), cost=0, pins=(), landing=()):
        operands = [*own, *other, queries_wide if wide else queries, *late[:1]]
        first = 1 + len(operands)
        inout = [out, done, *late[1:]]
        extra_types = (product_type(done.shape[0], count),) if wide else ()
        return pl.pallas_call(
            functools.partial(came_kernel, factor, (len(own), len(other)), wide, len(late) // 2, len(pins), slots, not G("NL"), landing),
            out_shape=tuple(jax.ShapeDtypeStruct(array.shape, array.dtype) for array in inout) + extra_types,
            in_specs=[scalars] + [in_vmem] * len(operands) + [anywhere] + [in_vmem] * (len(inout) - 1) + [anywhere] * len(pins),
            out_specs=(anywhere,) + (in_vmem,) * (len(inout) - 1 + wide),
            scratch_shapes=[
                pltpu.VMEM((count, queries_n), jnp.float32),
                pltpu.SemaphoreType.DMA((max(1, len(slots)),)),
                pltpu.SemaphoreType.DMA((max(1, len(landing)),)),
            ],
            input_output_aliases={first + index: index for index in range(len(inout))},
            compiler_params=params,
            cost_estimate=modelled(cost),
            name="came_rows",
        )(meta, *operands, *inout, *pins)

    def gate(out, pins, cost):
        handed = (out, *pins)
        return pl.pallas_call(
            gate_kernel,
            out_shape=tuple(jax.ShapeDtypeStruct(array.shape, array.dtype) for array in handed),
            in_specs=[anywhere] * len(handed),
            out_specs=(anywhere,) * len(handed),
            input_output_aliases={index: index for index in range(len(handed))},
            compiler_params=params,
            cost_estimate=modelled(cost),
            name="gate",
        )(*handed)

    mine = lax.dynamic_slice_in_dim(frame_two, side * half_rows, half_rows, axis=0)[None]
    theirs = lax.dynamic_slice_in_dim(frame_two, (1 - side) * half_rows, half_rows, axis=0)[None]
    if G("WH"):
        theirs = jnp.where(side == 0, frame_two[half_rows:], frame_two[:half_rows])[None]
    if G("XQ"):
        sent = jnp.concatenate([theirs.reshape(raw, chans), frame_one], axis=0)
        got = lax.ppermute(sent, "chan", across)
        partner, queries_other = got[:raw].reshape(theirs.shape), got[raw:]
    else:
        partner = lax.ppermute(theirs, "chan", across)
        queries_other = lax.ppermute(frame_one, "chan", across)
    def all_queries(mine, theirs):
        own_core = jnp.concatenate([mine.T, theirs.T], axis=0)
        return own_core, jnp.concatenate([own_core, lax.ppermute(own_core, "rows", swap)], axis=1)

    if not G("QC"): queries, queries_wide = all_queries(frame_one, queries_other)

    def permute_rows(pairs, pieces):
        return [lax.ppermute(piece, "rows", pairs) for piece in pieces]

    def whole(pieces):
        return pieces if len(pieces) == 1 else [jnp.concatenate(pieces, axis=0)]

    came = {0: ([mine], [partner])}
    moving = [[half, *permute_rows(swap, [half])] for half in (mine, partner)]
    join = [G("JA"), G("JB")]
    for d in range(1, half_way + 1):
        if d == half_way:
            moving = [[pieces[0][:1]] for pieces in moving]
        if d == half_way - 1 and G("BSPL"):
            moving[1] = [moving[1][0][:1], moving[1][0][1:]]
        moving = [whole(pieces) if d == join[part] else pieces for part, pieces in enumerate(moving)]
        if d == 1:
            ring_first = moving[1][-1]
        moving = [permute_rows(ring, pieces) for pieces in moving]
        came[d] = tuple(moving)
    across_came = {}

    def do_extra(out, d, part, pin=None):
        pins = () if pin is None else tuple(across_came[pin]) if isinstance(pin, tuple) else (pin,)
        across_came[d, 1 - part] = []
        groups = [[piece] for piece in came[d][part]] if part and d == half_way - 1 else [came[d][part]]
        for pieces in groups:
            extra, out = make_extra(out, pieces, G(f"X{d}{part}"), pins)
            across_came[d, 1 - part].append(lax.ppermute(extra, "chan", across))
            pins = ()
        return out

    lag = G("LAG")
    waiting = []

    def landing(now):
        if waiting and waiting[0][0] <= now:
            return waiting.pop(0)[1:]
        return (), None

    def product(out, d, pins=(), now=None):
        out, pair = correlate(out, slots_of(d, 0), *came[d], across_came[d, 0], across_came[d, 1], *landing(d if now is None else now), G(f"C{d}"), pins)
        waiting.append((d + lag, slots_of(d, 1), permute_rows(swap, [pair])[0]))
        return out

    if G("QC"):
        extra, out, sent = make_extra(None, came[0][0], G("X00"), ({1: partner, 2: ring_first}[G("PINX")],) if G("PINX") else (), passed=frame_one)
        across_came[0, 1] = [lax.ppermute(extra, "chan", across)]
        queries, queries_wide = all_queries(frame_one, lax.ppermute(sent, "chan", across))
    else:
        out = do_extra(None, 0, 0, partner if G("PINX") else None)
    lacking, out = make_extra(out, [theirs], G("X01"), tuple(across_came[0, 1]) if G("PIN01") else (), flip=True)
    across_came[0, 0] = [lacking]
    near, far = half_way - 1, half_way

    def swap_one(piece):
        return permute_rows(swap, [piece])[0]

    def near_raw(out):
        return raw_rows(out, *came[near], True, *landing(near), G("F3"), slots=slots_of(near, 0) if G("EL") else (), pins=tuple(across_came[far, 1]) if G("PR") else ())

    swapped = []

    def far_extra(out, part, pins):
        extra, out, piece = make_extra(out, came[far][part], G(f"X4{part}"), pins, carry=True)
        came[far][part][0] = piece
        across_came[far, 1 - part] = [lax.ppermute(extra, "chan", across)]
        swapped.append(swap_one(piece))
        return out

    out = do_extra(out, 1, 0)
    out = do_extra(out, 2, 0, (1, 1))
    out = do_extra(out, 1, 1, (2, 1))
    out = product(out, 0)
    for d in range(3, far):
        out = do_extra(out, d, 0, (d - 2, 0))
        out = product(out, d - 2)
        out = do_extra(out, d - 1, 1, (d, 1))
    out = far_extra(out, 0, tuple(across_came[near - 1, 0]) if G("P4") else ())
    across_came[near, 0] = []
    groups = [came[near][1]] if G("ONEX") else [[piece] for piece in came[near][1]]
    for index, pieces in enumerate(groups):
        if index == len(groups) - G("CPOS"):
            out = product(out, near - 1, now=near)
        extra, out = make_extra(out, pieces, G("X31"), tuple(across_came[far, 1]) if G("P3") == index + 1 else ())
        across_came[near, 0].append(lax.ppermute(extra, "chan", across))
    out, near_done, near_pair = near_raw(out)
    out = far_extra(out, 1, (swapped[0],) if G("PS0") == 1 else ())
    near_late = swap_one(near_pair)
    pins = (tuple(across_came[far, 1]) if G("PE4") == 1 else ()) + ((swapped[0],) if G("PS0") == 2 else ())

    slots = slots_of(near, 1) + slots_of(far, 0) + slots_of(far, 1)

    landing_now, landed_now = landing(far)
    out = pl.pallas_call(
        functools.partial(land_kernel, landing_now),
        out_shape=out_type,
        in_specs=[scalars, anywhere, anywhere],
        out_specs=anywhere,
        scratch_shapes=[pltpu.SemaphoreType.DMA((len(landing_now),))],
        input_output_aliases={2: 0},
        compiler_params=params,
        cost_estimate=modelled(0),
        name="land",
    )(meta, landed_now, out)
    landing_now = ()
    out, near_done, near_rows = came_rows(
        out, near_done, (), across_came[near, 0], across_came[near, 1], True, cost=G("F2"), pins=pins, landing=landing_now
    )
    near_rows = swap_one(near_rows)
    out, far_done = raw_rows(
        out,
        [came[far][0][0], swapped[0]],
        [came[far][1][0], swapped[1]],
        False,
        *landing(far),
        G("F0"),
        (near_done, near_late),
        ("rest" if G("EL") else "all", "settled" if G("NL") else None),
        slots_of(near, 0) + (slots if G("NL") else slots[len(slots_of(near, 1)) :]),
    )
    out, own, other = gate(out, [across_came[far, 0][0], across_came[far, 1][0]], G("GATE"))
    return came_rows(out, far_done, slots, [own, swap_one(own)], [other, swap_one(other)], False, (near_rows, near_late), G("F1"))[0]


def solution(mesh):
    rows_axis, groups = mesh.shape["rows"], mesh.shape["chan"]

    def local(frame_one, frame_two):
        rows_n, cols_n, chans = frame_two.shape
        ring = groups == 2 and rows_axis % 8 == 0 and rows_axis >= 16 and rows_n % 8 == 0 and cols_n % 32 == 0 and chans % LANES == 0
        return (ring_local if ring else gather_local)(frame_one, frame_two)

    in_specs = (P("rows", "chan"), P("rows", None, "chan"))
    out_specs = P(None, "chan", "rows")
    return jax.shard_map(local, mesh=mesh, in_specs=in_specs, out_specs=out_specs, check_vma=False)
```

```python
import functools

import jax
import jax.numpy as jnp
from jax import lax
from jax.experimental import pallas as pl
from jax.experimental.pallas import tpu as pltpu
from jax.sharding import PartitionSpec as P

LANES = 128
PARAMS = {'LAG': 2, 'F0': 10, 'F1': 0, 'PS0': 2, 'JA': 3, 'JB': 1, 'C0POS': 2, 'GATE': 30, 'F3': 0, 'F2': 22, 'NL': 0, 'PE4': 0, 'P4': 0, 'P3': 1, 'CPOS': 1, 'LC': 1, 'BSPL': 1, 'ONEX': 1, 'EL': 1, 'WH': 0, 'X00': 10, 'X01': 10, 'C0': 10, 'X10': 10, 'X11': 10, 'C1': 10, 'X20': 10, 'X21': 10, 'C2': 3, 'X30': 10, 'X31': 3, 'C3': 10, 'X40': 10, 'X41': 24, 'C4': 10}


def G(name):
    return PARAMS.get(name, 0)


VMEM_BYTES = 28 * 1024 * 1024


def pool_strip(strip):
    full = strip.astype(jnp.float32)
    rows_n, cols_n, chans = full.shape
    level_one = full.reshape(rows_n // 2, 2, cols_n // 2, 2, chans).mean(axis=(1, 3))
    level_two = level_one.reshape(rows_n // 4, 2, cols_n // 4, 2, chans).mean(axis=(1, 3))
    joined = jnp.concatenate(
        [full.reshape(-1, chans), level_one.reshape(-1, chans), level_two.reshape(-1, chans)],
        axis=0,
    )
    return joined.astype(jnp.bfloat16)


def gather_local(frame_one, frame_two):
    groups = lax.axis_size("chan")
    queries = lax.all_gather(frame_one, "chan", axis=0, tiled=False)
    channels = queries.shape[0] * queries.shape[2]
    factor = 1.0 / jnp.sqrt(jnp.float32(channels))
    pooled = pool_strip(frame_two)
    share = pooled.shape[0] // groups
    traded = lax.all_to_all(
        pooled.reshape(groups, share, pooled.shape[1]), "chan", split_axis=0, concat_axis=0, tiled=True
    )
    gathered = lax.all_gather(traded, "rows", axis=0, tiled=False)
    values = jnp.einsum("skpc,kqc->spq", gathered, queries, preferred_element_type=jnp.float32)
    return (values * factor).astype(jnp.bfloat16)


def pooled_levels(half, sums, sums_two):
    rows_n, cols_n, _ = half.shape
    means = []
    for row in range(rows_n // 2):
        sums[row] = half[2 * row].astype(jnp.float32) + half[2 * row + 1].astype(jnp.float32)
        left = sums[row, pl.ds(0, cols_n // 2, stride=2), :]
        right = sums[row, pl.ds(1, cols_n // 2, stride=2), :]
        means.append((left + right) * 0.25)
    means_two = []
    for row in range(rows_n // 4):
        sums_two[row] = means[2 * row] + means[2 * row + 1]
        left = sums_two[row, pl.ds(0, cols_n // 4, stride=2), :]
        right = sums_two[row, pl.ds(1, cols_n // 4, stride=2), :]
        means_two.append((left + right) * 0.25)
    return jnp.concatenate(means + means_two, axis=0)


def strips_in(refs):
    return [ref.at[index] for ref in refs for index in range(ref.shape[0])]


def extra_kernel(pieces, results, flip, meta, *refs):
    halves = strips_in(refs[:pieces])
    extra, sums, sums_two = refs[-2 - results], *refs[-2:]
    count, cols_n = extra.shape[1], halves[0].shape[1]
    upper = meta[0] == (1 if flip else 0)

    @pl.when(upper)
    def _():
        for index, half in enumerate(halves):
            extra[index] = pooled_levels(half, sums, sums_two).astype(extra.dtype)

    @pl.when(jnp.logical_not(upper))
    def _():
        for index, half in enumerate(halves):
            parts, left, row = [], count, 0
            while left > 0:
                parts.append(half[row].astype(jnp.float32)[: min(left, cols_n)])
                left, row = left - cols_n, row + 1
            extra[index] = jnp.concatenate(parts, axis=0).astype(extra.dtype)


def chunks(segments, step):
    todo, runs = list(segments), []
    while todo:
        run, room = [], step
        while todo and room > 0:
            ref, first, last = todo.pop(0)
            take = min(room, last - first)
            run.append((ref, first, first + take))
            room -= take
            if first + take < last:
                todo.insert(0, (ref, first + take, last))
        runs.append(run)
    return runs


def joined(run):
    parts = [ref[first:last].astype(jnp.float32) for ref, first, last in run]
    return parts[0] if len(parts) == 1 else jnp.concatenate(parts, axis=0)


def corr_kernel(factor, pieces, wide, slots, landing, pins, meta, *refs):
    own, other = strips_in(refs[: pieces[0]]), strips_in(refs[pieces[0] : sum(pieces[:2])])
    refs = refs[sum(pieces[:2]) :]
    came_own, came_other = strips_in(refs[: pieces[2]]), strips_in(refs[pieces[2] : pieces[2] + pieces[3]])
    queries, *refs = refs[pieces[2] + pieces[3] :]
    landed = refs.pop(0) if landing else None
    out, *refs = refs[1 + pins :]
    pair = refs.pop(0) if wide else None
    done, values, sums, sums_two, sems, land_sems = refs
    rows_n, cols_n, _ = own[0].shape
    count, width = came_own[0].shape[0], done.shape[2]
    raw = rows_n * cols_n
    ones = (rows_n // 2) * (cols_n // 2)

    copies = []
    for index, slot in enumerate(landing):
        copies.append(pltpu.make_async_copy(landed.at[index], out.at[meta[slot]], land_sems.at[index]))
        copies[-1].start()

    def times(left):
        return jnp.dot(left, queries[...], preferred_element_type=jnp.float32) * factor

    def store(index, at, part):
        done[index, at : at + part.shape[0]] = part[:, :width].astype(done.dtype)
        if wide:
            pair[index, at : at + part.shape[0]] = part[:, width:].astype(done.dtype)

    for index in range(len(own)):

        def raw_row(row):
            return jnp.concatenate([own[index][row], other[index][row]], axis=1)

        def came_rows():
            return jnp.concatenate([came_own[index][...], came_other[index][...]], axis=1)

        @pl.when(meta[0] == 0)
        def _():
            for row in range(rows_n):
                store(index, row * cols_n, times(raw_row(row)))
            store(index, raw, times(came_rows()))

        @pl.when(meta[0] != 0)
        def _():
            for row in range(count // cols_n, rows_n):
                values[row * cols_n : (row + 1) * cols_n] = times(raw_row(row))
            values[raw : raw + count] = times(came_rows())
            levels = [pooled_levels(half[index], sums, sums_two).astype(done.dtype) for half in (own, other)]
            lower = raw + count
            values[lower : lower + count] = times(jnp.concatenate(levels, axis=1))
            segments = [
                (values, count, raw),
                (values, raw, raw + ones),
                (values, lower, lower + ones),
                (values, raw + ones, raw + count),
                (values, lower + ones, lower + count),
            ]
            step = cols_n // 2
            for at, run in enumerate(chunks(segments, step)):
                store(index, at * step, joined(run))

        copies.append(pltpu.make_async_copy(done.at[index], out.at[meta[slots[index]]], sems.at[index]))
        copies[-1].start()
    for copy in copies:
        copy.wait()


def land_kernel(slots, meta, strips, _, out, sems):
    copies = []
    for index, slot in enumerate(slots):
        copies.append(pltpu.make_async_copy(strips.at[index], out.at[meta[slot]], sems.at[index]))
        copies[-1].start()
    for copy in copies:
        copy.wait()


def gate_kernel(*refs):
    pass


def first_open_row(total, raw):
    return (2 * raw - total) // 16 * 16


def raw_kernel(factor, arrays, wide, landing, leaving, slots, pins, meta, *refs):
    own, other = strips_in(refs[: arrays[0]]), strips_in(refs[arrays[0] : sum(arrays)])
    queries, *refs = refs[sum(arrays) :]
    landed = refs.pop(0) if landing else None
    leavers, refs = refs[: len(leaving)], refs[len(leaving) :]
    out, done, *refs = refs[1 + pins :]
    pair = refs.pop(0) if wide else None
    values, sums, sums_two, land_sems, sems = refs
    rows_n, cols_n, _ = own[0].shape
    count, width = done.shape[1] - rows_n * cols_n, done.shape[2]
    raw = rows_n * cols_n
    ones = (rows_n // 2) * (cols_n // 2)

    copies = []
    for index, slot in enumerate(landing):
        copies.append(pltpu.make_async_copy(landed.at[index], out.at[meta[slot]], land_sems.at[index]))
        copies[-1].start()
    total, cut = done.shape[1], first_open_row(done.shape[1], rows_n * cols_n)
    slots = list(slots)

    def leave(strip, part):
        rows = {"all": pl.ds(0, total), "settled": pl.ds(0, cut), "rest": pl.ds(cut, total - cut)}[part]
        number = len(copies) - len(landing)
        copies.append(pltpu.make_async_copy(strip.at[rows], out.at[meta[slots.pop(0)], rows], sems.at[number]))
        copies[-1].start()

    for strips, part in zip(leavers, leaving):
        for index in range(strips.shape[0] if part else 0):
            leave(strips.at[index], part)

    def times(left):
        return jnp.dot(left, queries[...], preferred_element_type=jnp.float32) * factor

    def store(index, at, part):
        done[index, at : at + part.shape[0]] = part[:, :width].astype(done.dtype)
        if wide:
            pair[index, at : at + part.shape[0]] = part[:, width:].astype(done.dtype)

    for index, halves in enumerate(zip(own, other)):

        def raw_row(row):
            return jnp.concatenate([half[row] for half in halves], axis=1)

        @pl.when(meta[0] == 0)
        def _():
            for row in range(rows_n):
                store(index, row * cols_n, times(raw_row(row)))
            store(index, raw, jnp.zeros((count, values.shape[1]), jnp.float32))

        @pl.when(meta[0] != 0)
        def _():
            for row in range(count // cols_n, rows_n):
                values[row * cols_n : (row + 1) * cols_n] = times(raw_row(row))
            levels = [pooled_levels(half, sums, sums_two).astype(done.dtype) for half in halves]
            values[raw : raw + count] = times(jnp.concatenate(levels, axis=1))
            segments = [
                (values, count, raw),
                (values, raw, raw + ones),
                (values, raw, raw + ones),
                (values, raw + ones, raw + count),
                (values, raw + ones, raw + count),
            ]
            step = cols_n // 2
            for at, run in enumerate(chunks(segments, step)):
                store(index, at * step, joined(run))

        if slots:
            leave(done.at[index], "settled")
    for copy in copies:
        copy.wait()


def came_kernel(factor, arrays, wide, late, pins, slots, late_whole, landing, meta, *refs):
    own, other = strips_in(refs[: arrays[0]]), strips_in(refs[arrays[0] : sum(arrays)])
    queries, *refs = refs[sum(arrays) :]
    late_rows = refs.pop(0) if late else None
    refs = refs[2 + late :]
    landed = refs[0] if landing else None
    refs = refs[pins:]
    out, done, *refs = refs
    late_done = refs.pop(0) if late else None
    pair = refs.pop(0) if wide else None
    values, sems, land_sems = refs
    count, width = own[0].shape[0], done.shape[2]
    raw = done.shape[1] - count
    ones = count * 4 // 5
    copies, landings = [], []
    for index, slot in enumerate(landing):
        landings.append(pltpu.make_async_copy(landed.at[index], out.at[meta[slot]], land_sems.at[index]))
        landings[-1].start()

    def leave(strip, whole=False):
        if slots:
            cut = 0 if whole else first_open_row(raw + count, raw)
            rows = pl.ds(cut, raw + count - cut)
            slot = meta[slots[len(copies)]]
            copies.append(pltpu.make_async_copy(strip.at[rows], out.at[slot, rows], sems.at[len(copies)]))
            copies[-1].start()

    def merge(strip, part):
        @pl.when(meta[0] == 0)
        def _():
            strip[raw : raw + count] = part.astype(done.dtype)

        @pl.when(meta[0] != 0)
        def _():
            values[...] = part
            at = raw - count
            for first, last, into in ((0, ones, at), (ones, count, at + 2 * ones)):
                start = into // 16 * 16
                end = -(-(into + last - first) // 16) * 16
                parts = [values[first:last]]
                if start < into:
                    parts.insert(0, strip[start : start + 16].astype(jnp.float32)[: into - start])
                over = end - (into + last - first)
                if over:
                    parts.append(strip[end - 16 : end].astype(jnp.float32)[16 - over :])
                strip[start:end] = jnp.concatenate(parts, axis=0).astype(done.dtype)

    if late:
        for index in range(late_done.shape[0]):
            merge(late_done.at[index], late_rows[index].astype(jnp.float32))
            leave(late_done.at[index], late_whole)
    for index, halves in enumerate(zip(own, other)):
        left = jnp.concatenate([half[...] for half in halves], axis=1)
        part = jnp.dot(left, queries[...], preferred_element_type=jnp.float32) * factor
        if wide:
            pair[index] = part[:, width:].astype(done.dtype)
        merge(done.at[index], part[:, :width])
        leave(done.at[index])
    for copy in copies + landings:
        copy.wait()


def ring_local(frame_one, frame_two):
    rows_axis = lax.axis_size("rows")
    rows_n, cols_n, chans = frame_two.shape
    queries_n = frame_one.shape[0]
    half_rows = rows_n // 2
    raw = half_rows * cols_n
    count = (half_rows // 2) * (cols_n // 2) + (half_rows // 4) * (cols_n // 4)
    factor = float(1.0 / (2 * chans) ** 0.5)
    me, side = lax.axis_index("rows"), lax.axis_index("chan")

    chips = rows_axis // 2
    columns, half_way = chips // 2, chips // 2
    order = [2 * z for z in range(columns)] + [2 * z + 1 for z in reversed(range(columns))]
    ring = [(2 * order[p], 2 * order[(p + 1) % chips]) for p in range(chips)]
    ring += [(2 * order[p] + 1, 2 * order[p - 1] + 1) for p in range(chips)]
    swap = [(r, r ^ 1) for r in range(rows_axis)]
    across = [(0, 1), (1, 0)]

    core, column, line = me % 2, me // 4, (me // 2) % 2
    place = jnp.where(line == 0, column, chips - 1 - column)
    steps = jnp.arange(half_way + 1, dtype=jnp.int32)

    def strips_of(c):
        p = (place + jnp.where(c == 0, -steps, steps)) % chips
        chip = jnp.where(p < columns, 2 * p, 2 * (chips - 1 - p) + 1)
        return [2 * chip + c, 2 * chip + 1 - c]

    meta = jnp.concatenate([side[None], *strips_of(core), *strips_of(1 - core)]).astype(jnp.int32)

    def slots_of(d, other_core):
        first = 1 + (2 * other_core) * (half_way + 1) + d
        return (first,) if d in (0, half_way) else (first, first + half_way + 1)

    in_vmem = pl.BlockSpec(memory_space=pltpu.VMEM)
    anywhere = pl.BlockSpec(memory_space=pl.ANY)
    scalars = pl.BlockSpec(memory_space=pltpu.SMEM)
    out_type = jax.ShapeDtypeStruct((rows_axis, raw + count, queries_n), frame_two.dtype)
    pooling = [
        pltpu.VMEM((half_rows // 2, cols_n, chans), jnp.float32),
        pltpu.VMEM((half_rows // 4, cols_n // 2, chans), jnp.float32),
    ]
    params = pltpu.CompilerParams(vmem_limit_bytes=VMEM_BYTES)
    def modelled(us):
        return pl.CostEstimate(flops=int(us * 10**9) + 1000, bytes_accessed=1000, transcendentals=0)


    def make_extra(out, halves, cost=0, pins=(), flip=False, carry=False, passed=None):
        strips = sum(half.shape[0] for half in halves)
        handed = () if out is None else (out,)
        carried = tuple(halves) if carry else ()
        aliases = {1 + len(halves): 1} if handed else {}
        aliases.update({1 + index: 2 + index for index in range(len(carried))})
        if passed is not None:
            pins, carried = (passed, *pins), (passed,)
            aliases[1 + len(halves) + len(handed)] = 2
        return pl.pallas_call(
            functools.partial(extra_kernel, len(halves), 2 + len(carried), flip),
            out_shape=(jax.ShapeDtypeStruct((strips, count, chans), frame_two.dtype), out_type)
            + tuple(jax.ShapeDtypeStruct(half.shape, half.dtype) for half in carried),
            in_specs=[scalars] + [in_vmem] * len(halves) + [anywhere] * len(handed + pins),
            out_specs=(in_vmem, anywhere) + (in_vmem if carry else anywhere,) * len(carried),
            scratch_shapes=pooling,
            input_output_aliases=aliases,
            compiler_params=params,
            cost_estimate=modelled(cost),
            name="extra",
        )(meta, *halves, *handed, *pins)

    def correlate(out, slots, own, other, came_own, came_other, landing=(), landed=None, cost=0, pins=()):
        parts = (own, other, came_own, came_other)
        strips = sum(piece.shape[0] for piece in own)
        operands = [*own, *other, *came_own, *came_other, queries_wide]
        pair_type = jax.ShapeDtypeStruct((strips, raw + count, queries_n), frame_two.dtype)
        return pl.pallas_call(
            functools.partial(corr_kernel, factor, tuple(len(part) for part in parts), True, slots, landing, len(pins)),
            out_shape=(out_type, pair_type),
            in_specs=[scalars] + [in_vmem] * len(operands) + [anywhere] * (1 + bool(landing) + len(pins)),
            out_specs=(anywhere, in_vmem),
            scratch_shapes=[
                pltpu.VMEM((strips, raw + count, queries_n), frame_two.dtype),
                pltpu.VMEM((raw + 2 * count, 2 * queries_n), jnp.float32),
                *pooling,
                pltpu.SemaphoreType.DMA((strips,)),
                pltpu.SemaphoreType.DMA((max(1, len(landing)),)),
            ],
            input_output_aliases={1 + len(operands) + bool(landing): 0},
            compiler_params=params,
            cost_estimate=modelled(cost),
            name="correlate",
        )(meta, *operands, *([landed] if landing else []), out, *pins)

    def product_type(strips, pixels):
        return jax.ShapeDtypeStruct((strips, pixels, queries_n), frame_two.dtype)

    def raw_rows(out, own, other, wide, landing=(), landed=None, cost=0, leavers=(), leaving=(), slots=(), pins=()):
        operands = [*own, *other, queries_wide if wide else queries]
        strips = sum(half.shape[0] for half in own)
        passive = ([landed] if landing else []) + list(leavers)
        pins = tuple(pins)
        return pl.pallas_call(
            functools.partial(raw_kernel, factor, (len(own), len(other)), wide, landing, leaving, slots, len(pins)),
            out_shape=(out_type,) + (product_type(strips, raw + count),) * (1 + wide),
            in_specs=[scalars] + [in_vmem] * len(operands) + [anywhere] * (1 + len(passive) + len(pins)),
            out_specs=(anywhere,) + (in_vmem,) * (1 + wide),
            scratch_shapes=[
                pltpu.VMEM((raw + count, queries_n * (1 + wide)), jnp.float32),
                *pooling,
                pltpu.SemaphoreType.DMA((max(1, len(landing)),)),
                pltpu.SemaphoreType.DMA((max(1, len(slots)),)),
            ],
            input_output_aliases={1 + len(operands) + len(passive): 0},
            compiler_params=params,
            cost_estimate=modelled(cost),
            name="raw_rows",
        )(meta, *operands, *passive, out, *pins)

    def came_rows(out, done, slots, own, other, wide, late=(), cost=0, pins=(), landing=()):
        operands = [*own, *other, queries_wide if wide else queries, *late[:1]]
        first = 1 + len(operands)
        inout = [out, done, *late[1:]]
        extra_types = (product_type(done.shape[0], count),) if wide else ()
        return pl.pallas_call(
            functools.partial(came_kernel, factor, (len(own), len(other)), wide, len(late) // 2, len(pins), slots, not G("NL"), landing),
            out_shape=tuple(jax.ShapeDtypeStruct(array.shape, array.dtype) for array in inout) + extra_types,
            in_specs=[scalars] + [in_vmem] * len(operands) + [anywhere] + [in_vmem] * (len(inout) - 1) + [anywhere] * len(pins),
            out_specs=(anywhere,) + (in_vmem,) * (len(inout) - 1 + wide),
            scratch_shapes=[
                pltpu.VMEM((count, queries_n), jnp.float32),
                pltpu.SemaphoreType.DMA((max(1, len(slots)),)),
                pltpu.SemaphoreType.DMA((max(1, len(landing)),)),
            ],
            input_output_aliases={first + index: index for index in range(len(inout))},
            compiler_params=params,
            cost_estimate=modelled(cost),
            name="came_rows",
        )(meta, *operands, *inout, *pins)

    def gate(out, pins, cost):
        handed = (out, *pins)
        return pl.pallas_call(
            gate_kernel,
            out_shape=tuple(jax.ShapeDtypeStruct(array.shape, array.dtype) for array in handed),
            in_specs=[anywhere] * len(handed),
            out_specs=(anywhere,) * len(handed),
            input_output_aliases={index: index for index in range(len(handed))},
            compiler_params=params,
            cost_estimate=modelled(cost),
            name="gate",
        )(*handed)

    mine = lax.dynamic_slice_in_dim(frame_two, side * half_rows, half_rows, axis=0)[None]
    theirs = lax.dynamic_slice_in_dim(frame_two, (1 - side) * half_rows, half_rows, axis=0)[None]
    if G("WH"):
        theirs = jnp.where(side == 0, frame_two[half_rows:], frame_two[:half_rows])[None]
    if G("XQ"):
        sent = jnp.concatenate([theirs.reshape(raw, chans), frame_one], axis=0)
        got = lax.ppermute(sent, "chan", across)
        partner, queries_other = got[:raw].reshape(theirs.shape), got[raw:]
    else:
        partner = lax.ppermute(theirs, "chan", across)
        queries_other = lax.ppermute(frame_one, "chan", across)
    def all_queries(mine, theirs):
        own_core = jnp.concatenate([mine.T, theirs.T], axis=0)
        return own_core, jnp.concatenate([own_core, lax.ppermute(own_core, "rows", swap)], axis=1)

    if not G("QC"): queries, queries_wide = all_queries(frame_one, queries_other)

    def permute_rows(pairs, pieces):
        return [lax.ppermute(piece, "rows", pairs) for piece in pieces]

    def whole(pieces):
        return pieces if len(pieces) == 1 else [jnp.concatenate(pieces, axis=0)]

    came = {0: ([mine], [partner])}
    moving = [[half, *permute_rows(swap, [half])] for half in (mine, partner)]
    join = [G("JA"), G("JB")]
    for d in range(1, half_way + 1):
        if d == half_way:
            moving = [[pieces[0][:1]] for pieces in moving]
        if d == half_way - 1 and G("BSPL"):
            moving[1] = [moving[1][0][:1], moving[1][0][1:]]
        moving = [whole(pieces) if d == join[part] else pieces for part, pieces in enumerate(moving)]
        if d == 1:
            ring_first = moving[1][-1]
        moving = [permute_rows(ring, pieces) for pieces in moving]
        came[d] = tuple(moving)
    across_came = {}

    def do_extra(out, d, part, pin=None):
        pins = () if pin is None else tuple(across_came[pin]) if isinstance(pin, tuple) else (pin,)
        across_came[d, 1 - part] = []
        groups = [[piece] for piece in came[d][part]] if part and d == half_way - 1 else [came[d][part]]
        for pieces in groups:
            extra, out = make_extra(out, pieces, G(f"X{d}{part}"), pins)
            across_came[d, 1 - part].append(lax.ppermute(extra, "chan", across))
            pins = ()
        return out

    lag = G("LAG")
    waiting = []

    def landing(now):
        if waiting and waiting[0][0] <= now:
            return waiting.pop(0)[1:]
        return (), None

    def product(out, d, pins=(), now=None):
        out, pair = correlate(out, slots_of(d, 0), *came[d], across_came[d, 0], across_came[d, 1], *landing(d if now is None else now), G(f"C{d}"), pins)
        waiting.append((d + lag, slots_of(d, 1), permute_rows(swap, [pair])[0]))
        return out

    if G("QC"):
        extra, out, sent = make_extra(None, came[0][0], G("X00"), ({1: partner, 2: ring_first}[G("PINX")],) if G("PINX") else (), passed=frame_one)
        across_came[0, 1] = [lax.ppermute(extra, "chan", across)]
        queries, queries_wide = all_queries(frame_one, lax.ppermute(sent, "chan", across))
    else:
        out = do_extra(None, 0, 0, partner if G("PINX") else None)
    lacking, out = make_extra(out, [theirs], G("X01"), tuple(across_came[0, 1]) if G("PIN01") else (), flip=True)
    across_came[0, 0] = [lacking]
    near, far = half_way - 1, half_way

    def swap_one(piece):
        return permute_rows(swap, [piece])[0]

    def near_raw(out):
        return raw_rows(out, *came[near], True, *landing(near), G("F3"), slots=slots_of(near, 0) if G("EL") else (), pins=tuple(across_came[far, 1]) if G("PR") else ())

    swapped = []

    def far_extra(out, part, pins):
        extra, out, piece = make_extra(out, came[far][part], G(f"X4{part}"), pins, carry=True)
        came[far][part][0] = piece
        across_came[far, 1 - part] = [lax.ppermute(extra, "chan", across)]
        swapped.append(swap_one(piece))
        return out

    out = do_extra(out, 1, 0)
    out = do_extra(out, 2, 0, (1, 1))
    out = do_extra(out, 1, 1, (2, 1))
    out = product(out, 0)
    for d in range(3, far):
        out = do_extra(out, d, 0, (d - 2, 0))
        out = product(out, d - 2)
        out = do_extra(out, d - 1, 1, (d, 1))
    out = far_extra(out, 0, tuple(across_came[near - 1, 0]) if G("P4") else ())
    across_came[near, 0] = []
    groups = [came[near][1]] if G("ONEX") else [[piece] for piece in came[near][1]]
    for index, pieces in enumerate(groups):
        if index == len(groups) - G("CPOS"):
            out = product(out, near - 1, now=near)
        extra, out = make_extra(out, pieces, G("X31"), tuple(across_came[far, 1]) if G("P3") == index + 1 else ())
        across_came[near, 0].append(lax.ppermute(extra, "chan", across))
    out, near_done, near_pair = near_raw(out)
    out = far_extra(out, 1, (swapped[0],) if G("PS0") == 1 else ())
    near_late = swap_one(near_pair)
    pins = (tuple(across_came[far, 1]) if G("PE4") == 1 else ()) + ((swapped[0],) if G("PS0") == 2 else ())

    slots = slots_of(near, 1) + slots_of(far, 0) + slots_of(far, 1)

    landing_now, landed_now = landing(far)
    out = pl.pallas_call(
        functools.partial(land_kernel, landing_now),
        out_shape=out_type,
        in_specs=[scalars, anywhere, anywhere],
        out_specs=anywhere,
        scratch_shapes=[pltpu.SemaphoreType.DMA((len(landing_now),))],
        input_output_aliases={2: 0},
        compiler_params=params,
        cost_estimate=modelled(0),
        name="land",
    )(meta, landed_now, out)
    landing_now = ()
    out, near_done, near_rows = came_rows(
        out, near_done, (), across_came[near, 0], across_came[near, 1], True, cost=G("F2"), pins=pins, landing=landing_now
    )
    near_rows = swap_one(near_rows)
    out, far_done = raw_rows(
        out,
        [came[far][0][0], swapped[0]],
        [came[far][1][0], swapped[1]],
        False,
        *landing(far),
        G("F0"),
        (near_done, near_late),
        ("rest" if G("EL") else "all", "settled" if G("NL") else None),
        slots_of(near, 0) + (slots if G("NL") else slots[len(slots_of(near, 1)) :]),
    )
    out, own, other = gate(out, [across_came[far, 0][0], across_came[far, 1][0]], G("GATE"))
    return came_rows(out, far_done, slots, [own, swap_one(own)], [other, swap_one(other)], False, (near_rows, near_late), G("F1"))[0]


def solution(mesh):
    rows_axis, groups = mesh.shape["rows"], mesh.shape["chan"]

    def local(frame_one, frame_two):
        rows_n, cols_n, chans = frame_two.shape
        ring = groups == 2 and rows_axis % 8 == 0 and rows_axis >= 16 and rows_n % 8 == 0 and cols_n % 32 == 0 and chans % LANES == 0
        return (ring_local if ring else gather_local)(frame_one, frame_two)

    in_specs = (P("rows", "chan"), P("rows", None, "chan"))
    out_specs = P(None, "chan", "rows")
    return jax.shard_map(local, mesh=mesh, in_specs=in_specs, out_specs=out_specs, check_vma=False)
```
